32 devices in a mesh: groups: 2 (over x), dom: 16 (over z, y, core).
Axes of the slice: x: 2, y: 2, z: 4, core: 2. Of those that a mesh axis runs over, the one named last changes fastest.
Arguments:
- positions: float32 [3, 8192], P(None, ('groups', 'dom')), parts along dimension 1, may hold values from -6 to 6
- features: bfloat16 [8192, 256], P(('groups', 'dom')), parts along dimension 0, may hold values from -6 to 6
- species: int32 [8192], P(('groups', 'dom')), parts along dimension 0, may hold values from 0 to 3
- neighbours: int32 [8192, 32], P(('groups', 'dom')), parts along dimension 0, may hold values from 0 to 639, as said below
- near_count: int32 [8192], P(('groups', 'dom')), parts along dimension 0, may hold values from 1 to 32
- send_left: int32 [6144], P(('groups', 'dom')), parts along dimension 0, may hold values from 0 to 255, as said below
- send_right: int32 [6144], P(('groups', 'dom')), parts along dimension 0, may hold values from 0 to 255, as said below
- radial_in: float32 [8, 64], replicated, may hold values from -4 to 4
- radial_out: bfloat16 [64, 768], replicated, may hold values from -1.5 to 1.5
- mix_weight: bfloat16 [256, 256], replicated, may hold values from -0.375 to 0.375
- product_weight: bfloat16 [768, 256], replicated, may hold values from -0.21875 to 0.21875
- species_gain: float32 [4, 256], replicated, may hold values from 0.1 to 1.9
- readout: float32 [256], replicated, may hold values from -0.375 to 0.375
Outputs:
- energies: float32 [8192], P(('groups', 'dom')), parts along dimension 0
- forces: float32 [3, 8192], P(None, ('groups', 'dom')), parts along dimension 1
- feature_grad: float32 [8192, 256], P(('groups', 'dom')), parts along dimension 0
The draws below stay inside these ranges and needn't reach their ends.
There are 2 independent parts, one for each index of `groups`. The reference program is written for one: setup_inputs(seed, part) draws one part's arguments, and reference() takes and returns one part's arrays. A program takes and returns all parts, laid end to end along the dimension named above; an argument that names none is the same for every part. Nothing has to cross between parts.
Inputs may be any that keep to these rules, and one draw needn't show every extreme that they name: `neighbours`: entries of one domain index its own table; the first domain names no left-list entries and the last no right-list entries. `send_left`: each domain's 192 entries index its own atoms. `send_right`: each domain's 192 entries index its own atoms.
All inputs are finite; a program needn't handle non-finite values.
Results may differ from the reference program's by a relative error of at most 0.013.
Values may be sent and summed in bfloat16 or wider, within the bound.
No kernel may reach another device: no remote copies, remote signals or barrier semaphores. Data moves between devices by JAX's collectives and lax.ppermute only.
A program may use at most 128 MiB of HBM per device.

```python
import jax
import jax.numpy as jnp
from jax import lax

C = 256
NB = 8
RH = 64
S = 4
K = 32
ATOMS_DEV = 256
GHOSTS = 192
ATOMS = 4096


def draw_neighbours(key, part):
    key = jax.random.fold_in(key, 11)
    rows = jnp.arange(ATOMS).astype(jnp.int32)
    dom_idx = rows // ATOMS_DEV
    local = rows % ATOMS_DEV
    ndom = ATOMS // ATOMS_DEV
    idx = jax.random.randint(key, (ATOMS, K), 0, ATOMS_DEV + 2 * GHOSTS).astype(jnp.int32)
    first = (dom_idx == 0)[:, None]
    last = (dom_idx == ndom - 1)[:, None]
    in_left = (idx >= ATOMS_DEV) & (idx < ATOMS_DEV + GHOSTS)
    in_right = idx >= ATOMS_DEV + GHOSTS
    idx = jnp.where(first & in_left, idx - GHOSTS, idx)
    idx = jnp.where(last & in_right, idx - 2 * GHOSTS, idx)
    idx = jnp.where(idx == local[:, None], (idx + 1) % ATOMS_DEV, idx)
    idx = idx.at[ATOMS_DEV, 0].set(ATOMS_DEV + 2 * GHOSTS - 1)
    idx = idx.at[ATOMS_DEV, 1].set(0)
    return idx.astype(jnp.int32)


def draw_near_count(key, part):
    key = jax.random.fold_in(key, 12)
    count = jax.random.randint(key, (ATOMS,), 1, K + 1).astype(jnp.int32)
    count = count.at[0::ATOMS_DEV].set(K)
    count = count.at[1::ATOMS_DEV].set(1)
    return count


def ghost_lists(key):
    ndom = ATOMS // ATOMS_DEV
    keys = jax.random.split(key, ndom)
    lists = jax.vmap(lambda one: jax.random.permutation(one, ATOMS_DEV)[:GHOSTS])(keys).astype(jnp.int32)
    lists = lists.at[0, 0].set(ATOMS_DEV - 1)
    lists = lists.at[0, 1].set(0)
    return lists.reshape(ndom * GHOSTS)


def draw_send_left(key, part):
    key = jax.random.fold_in(key, 13)
    return ghost_lists(key)


def draw_send_right(key, part):
    key = jax.random.fold_in(key, 14)
    return ghost_lists(key)


def with_ends(result, rng, least, high):
    longest = result.shape.index(max(result.shape))
    spots = []
    for shift in (0, 1):
        where = [jax.random.randint(jax.random.fold_in(rng, axis), (), 0, length) for axis, length in enumerate(result.shape)]
        where[longest] = (where[longest] + shift) % result.shape[longest]
        spots.append(tuple(where))
    return result.at[spots[0]].set(least).at[spots[1]].set(high)


def steps_of(rng, extent, shards, least, high):
    factor_of, own = 1.0, jax.random.fold_in(rng, 6)
    for axis_at, blocks in shards:
        steps = jnp.exp(jax.random.uniform(jax.random.fold_in(own, axis_at), (blocks,), jnp.float32, least / len(shards), high / len(shards)))
        factor_of = factor_of * jnp.repeat(steps, extent[axis_at] // blocks).reshape([-1 if axis == axis_at else 1 for axis in range(len(extent))])
    return factor_of


def noise(rng, extent, deviation, limit, shards=(), kind=jnp.bfloat16):
    entries = deviation * jax.random.normal(rng, extent, jnp.float32)
    if shards:
        entries = entries * steps_of(rng, extent, shards, -0.22, 0.18)
    return jnp.clip(entries, -limit, limit).astype(kind)


def setup_inputs(seed: int = 0, part: int = 0) -> dict:
    seeds = jax.random.split(jax.random.key(seed), 14)
    part_keys = jax.random.split(jax.random.fold_in(seeds[13], part), 14)
    return {
        "positions": noise(part_keys[0], (3, ATOMS), 1.5, 6.0, ((1, 16),), jnp.float32),
        "features": noise(part_keys[1], (ATOMS, C), 1.0, 6.0, ((0, 16),)),
        "species": with_ends(jax.random.randint(part_keys[2], (ATOMS,), 0, S), jax.random.fold_in(part_keys[2], 1), 0, S - 1).astype(jnp.int32),
        "neighbours": draw_neighbours(jax.random.fold_in(jax.random.fold_in(seeds[13], part), 71), part),
        "near_count": draw_near_count(jax.random.fold_in(jax.random.fold_in(seeds[13], part), 71), part),
        "send_left": draw_send_left(jax.random.fold_in(jax.random.fold_in(seeds[13], part), 71), part),
        "send_right": draw_send_right(jax.random.fold_in(jax.random.fold_in(seeds[13], part), 71), part),
        "radial_in": noise(seeds[7], (NB, RH), 2 ** -0.5, 4.0, (), jnp.float32),
        "radial_out": noise(seeds[8], (RH, 3 * C), (RH // 4) ** -0.5, 1.5),
        "mix_weight": noise(seeds[9], (C, C), C ** -0.5, 0.375),
        "product_weight": noise(seeds[10], (3 * C, C), (3 * C) ** -0.5, 0.21875),
        "species_gain": jnp.clip(1.0 + 0.18 * jax.random.normal(seeds[11], (S, C), jnp.float32), 0.1, 1.9),
        "readout": noise(seeds[12], (C,), C ** -0.5, 0.375, (), jnp.float32),
    }


cut_radius = 5.0
sqrt_three = 1.7320508075688772

def block_energy(pos_self, pos_near, g_near, h_self, gain_self, count, radial_in, radial_out, product_weight, readout):
    rows = pos_self.shape[1]
    slots = pos_near.shape[2]
    chans = g_near.shape[2]
    nbasis = radial_in.shape[0]
    dvec = pos_near - pos_self[:, :, None]
    r2 = lax.optimization_barrier(jnp.sum(dvec * dvec, axis=0))
    dist = jnp.sqrt(r2 + 0.25)
    live = (jnp.arange(slots)[None, :] < count[:, None]).astype(jnp.float32)
    env = jnp.maximum(1.0 - r2 / (cut_radius * cut_radius), 0.0) ** 2 * live
    orders = jnp.arange(1, nbasis + 1).astype(jnp.float32)
    basis = jnp.sin(orders * jnp.pi * dist[..., None] / cut_radius) / dist[..., None] * env[..., None]
    hidden = jax.nn.silu(jnp.dot(basis.reshape(rows * slots, nbasis), radial_in, precision=lax.Precision.HIGHEST)).astype(jnp.bfloat16)
    radial = jnp.dot(hidden, radial_out, preferred_element_type=jnp.float32).reshape(rows, slots, 3 * chans)
    ux = dvec[0] / dist
    uy = dvec[1] / dist
    uz = dvec[2] / dist
    usq = ux * ux + uy * uy + uz * uz
    harm_one = jnp.stack([ux, uy, uz])
    harm_two = jnp.stack([sqrt_three * ux * uy, sqrt_three * uy * uz, 0.5 * (3.0 * uz * uz - usq), sqrt_three * ux * uz, 0.5 * sqrt_three * (ux * ux - uy * uy)])
    term_zero = radial[:, :, :chans] * g_near
    term_one = radial[:, :, chans:2 * chans] * g_near
    term_two = radial[:, :, 2 * chans:] * g_near
    scale = 1.0 / slots
    alpha_zero = lax.optimization_barrier(jnp.sum(term_zero, axis=1)) * scale
    alpha_one = jnp.einsum('mbk,bkc->mbc', harm_one, term_one, precision=lax.Precision.HIGHEST) * scale
    alpha_two = jnp.einsum('mbk,bkc->mbc', harm_two, term_two, precision=lax.Precision.HIGHEST) * scale
    invariants = jnp.concatenate([alpha_zero, lax.optimization_barrier(jnp.sum(alpha_one * alpha_one, axis=0)), lax.optimization_barrier(jnp.sum(alpha_two * alpha_two, axis=0))], axis=-1).astype(jnp.bfloat16)
    node = jax.nn.silu(jnp.dot(invariants, product_weight, preferred_element_type=jnp.float32)) + h_self * gain_self
    return jnp.dot(node, readout, precision=lax.Precision.HIGHEST)

def reference(positions, features, species, neighbours, near_count, send_left, send_right, radial_in, radial_out, mix_weight, product_weight, species_gain, readout):
    ndom = ATOMS // ATOMS_DEV
    own = jnp.arange(ATOMS_DEV).astype(jnp.int32)
    right_lists = send_right.reshape(ndom, GHOSTS)
    left_lists = send_left.reshape(ndom, GHOSTS)
    tables = []
    for dom_idx in range(ndom):
        from_left = (dom_idx - 1) * ATOMS_DEV + right_lists[max(dom_idx - 1, 0)] if dom_idx > 0 else jnp.zeros((GHOSTS,), jnp.int32)
        from_right = (dom_idx + 1) * ATOMS_DEV + left_lists[min(dom_idx + 1, ndom - 1)] if dom_idx < ndom - 1 else jnp.zeros((GHOSTS,), jnp.int32)
        tables.append(jnp.concatenate([dom_idx * ATOMS_DEV + own, from_left.astype(jnp.int32), from_right.astype(jnp.int32)]))
    tables = jnp.stack(tables)
    dom_of = (jnp.arange(ATOMS) // ATOMS_DEV).astype(jnp.int32)
    global_nb = jnp.take_along_axis(tables[dom_of], neighbours, axis=1)
    mixed = jnp.dot(features, mix_weight, preferred_element_type=jnp.float32).astype(jnp.bfloat16).astype(jnp.float32)
    onehot = (species[:, None] == jnp.arange(S)[None, :]).astype(jnp.float32)
    gain = jnp.dot(onehot, species_gain, precision=lax.Precision.HIGHEST)
    block = 256 if ATOMS % 256 == 0 else ATOMS_DEV
    nblocks = ATOMS // block

    def total(pos, gfeat, hfeat):

        def one(idx):
            start = idx * block
            nb_blk = lax.dynamic_slice_in_dim(global_nb, start, block, 0)
            return block_energy(lax.dynamic_slice_in_dim(pos, start, block, 1), pos[:, nb_blk], gfeat[nb_blk], lax.dynamic_slice_in_dim(hfeat, start, block, 0), lax.dynamic_slice_in_dim(gain, start, block, 0), lax.dynamic_slice_in_dim(near_count, start, block, 0), radial_in, radial_out, product_weight, readout)
        energies = lax.map(jax.checkpoint(one), jnp.arange(nblocks)).reshape(ATOMS)
        return (jnp.sum(energies), energies)
    hfloat = features.astype(jnp.float32)
    energy_sum, pull, energies = jax.vjp(total, positions, mixed, hfloat, has_aux=True)
    d_pos, d_mixed, d_h = pull(jnp.ones_like(energy_sum))
    feature_grad = d_h + jnp.dot(d_mixed, mix_weight.astype(jnp.float32).T, precision=lax.Precision.HIGHEST)
    return (energies, -d_pos, feature_grad)
```

```python
import functools

import jax
import jax.numpy as jnp
from jax import lax
from jax.experimental import pallas as pl
from jax.experimental.pallas import tpu as pltpu
from jax.sharding import PartitionSpec as P

cut_radius = 5.0
sqrt_three = 1.7320508075688772
pi = 3.141592653589793

f32 = jnp.float32
bf16 = jnp.bfloat16

BLOCK = 32
DEPTH = 8
EXTRA = 16
UNROLL = 2


def shifted(value, axis, by):
    count = lax.axis_size(axis)
    pairs = [(i, i + by) for i in range(count) if 0 <= i + by < count]
    return lax.ppermute(value, axis, pairs)


def iota(shape, dim):
    return lax.broadcasted_iota(jnp.int32, shape, dim)


def dot(a, b, ca=1, cb=0):
    return lax.dot_general(a, b, (((ca,), (cb,)), ((), ())), preferred_element_type=f32)


def parts(value, count):
    out = []
    for _ in range(count):
        head = value.astype(bf16).astype(f32)
        out.append(head)
        value = value - head
    return out


def stack_rows(rows, height):
    lanes = rows[0].shape[1]
    at = iota((height, lanes), 0)
    out = jnp.zeros((height, lanes), f32)
    for idx, row in enumerate(rows):
        out = jnp.where(at == idx, jnp.broadcast_to(row, (height, lanes)), out)
    return out


def sigmoid(x):
    return 1.0 / (1.0 + jnp.exp(-x))


def pack_kernel(pos_ref, feat_ref, mix_ref, sl_ref, sr_ref, own_ref, right_ref, left_ref):
    chans, atoms = own_ref.shape[0] - EXTRA, own_ref.shape[1]
    ghosts = sl_ref.shape[1]
    own_ref[:chans, :] = dot(mix_ref[...], feat_ref[...], 0, 1).astype(bf16)
    pos = pos_ref[...]
    rows = [p[d : d + 1, :] for p in parts(pos, 3) for d in range(3)]
    own_ref[chans:, :] = stack_rows(rows, EXTRA).astype(bf16)
    for lst, out in ((sr_ref, right_ref), (sl_ref, left_ref)):
        pick = (iota((atoms, ghosts), 0) == lst[...]).astype(f32).astype(bf16)
        out[:, :ghosts] = dot(own_ref[...], pick).astype(bf16)
        out[:, ghosts:] = jnp.zeros((chans + EXTRA, atoms - ghosts), bf16)


def sort_kernel(
    ghosts, pos_ref, cnt_ref, nb_ref, feat_ref, spec_ref, gain_ref, read_ref, nbt_ref, self_ref, rank_ref, edir_ref
):
    atoms, slots = nb_ref.shape
    cnt_row = cnt_ref[...].astype(f32)
    up, across = iota((atoms, atoms), 0), iota((atoms, atoms), 1)
    cnt_col = jnp.sum(jnp.where(up == across, cnt_row, 0.0), axis=1, keepdims=True)
    ahead_row = (cnt_col > cnt_row) | ((cnt_col == cnt_row) & (up < across))
    ahead_col = (cnt_row > cnt_col) | ((cnt_row == cnt_col) & (across < up))
    rank_row = jnp.sum(ahead_row.astype(f32), axis=0, keepdims=True)
    rank_col = jnp.sum(ahead_col.astype(f32), axis=1, keepdims=True)
    rank_ref[...] = rank_row
    nb = nb_ref[...]
    nb = jnp.where(nb >= atoms + ghosts, nb + (atoms - ghosts), nb)
    nbt = jnp.transpose(nb.astype(f32))
    high = jnp.floor(nbt * (1.0 / 256.0))
    low = nbt - high * 256.0
    pos = pos_ref[...]
    rows = [p[d : d + 1, :] for p in parts(pos, 3) for d in range(3)] + [cnt_row]
    left = jnp.concatenate([high, low, stack_rows(rows, EXTRA)], axis=0).astype(bf16)
    lane_atom = (across % BLOCK).astype(f32)
    lane_slot = iota((slots, atoms), 1) // BLOCK
    mine = lane_slot == (iota((slots, atoms), 0) % DEPTH)
    depth_at = iota((slots // DEPTH, atoms), 0) * DEPTH + iota((slots // DEPTH, atoms), 1) // BLOCK
    groups = slots // DEPTH
    for b in range(atoms // BLOCK):
        pick = (rank_col - float(b * BLOCK) == lane_atom).astype(f32).astype(bf16)
        got = dot(left, pick)
        ids = got[:slots] * 256.0 + got[slots : 2 * slots]
        tail = got[2 * slots :]
        ids = jnp.sum(jnp.where(mine, ids, 0.0).reshape(groups, DEPTH, atoms), axis=1)
        ids = jnp.where(depth_at.astype(f32) < tail[9:10], ids, -1.0)
        nbt_ref[b * groups : (b + 1) * groups, :] = ids
        self_ref[b] = tail[0:8] + tail[3:11] + tail[6:14]
    weight = gain_ref[...] * read_ref[...]
    kinds = weight.shape[0]
    direct = jnp.zeros((kinds, atoms), f32)
    for p in parts(weight, 3):
        direct += dot(p.astype(bf16), feat_ref[...], 1, 1)
    edir_ref[...] = jnp.sum(
        jnp.where(iota((kinds, atoms), 0) == spec_ref[...], direct, 0.0), axis=0, keepdims=True
    )


def main_kernel(
    depth_ref,
    own_ref,
    lrec_ref,
    rrec_ref,
    nbt_ref,
    self_ref,
    rank_ref,
    edir_ref,
    rin_ref,
    rout_ref,
    pw_ref,
    read_ref,
    en_ref,
    dmix_ref,
    dpos_ref,
    gl_ref,
    gr_ref,
    list_ref,
    table,
    selbuf,
    gbuf,
    rbuf,
    ybuf,
    dgbuf,
    abuf,
    dabuf,
    acc,
    dvec,
    harm,
    radc,
    sinb,
    cosb,
    dsil,
    dharm,
    dbas,
    wout_t,
    rank_up,
):
    high, atoms = own_ref.shape
    chans = high - EXTRA
    tiles = nbt_ref.shape[0]
    blocks = atoms // BLOCK
    groups = tiles // blocks
    hid_n = rout_ref.shape[0]
    nbasis = rin_ref.shape[0]
    scale = 1.0 / (groups * DEPTH)

    def list_group(j, live):
        need = (depth_ref[j] + (BLOCK - 1)) // BLOCK

        def put(b, state):
            front, back = state
            is_live = b < need

            @pl.when(is_live)
            def _():
                list_ref[front] = b * groups + j

            @pl.when(jnp.logical_not(is_live))
            def _():
                list_ref[back] = b * groups + j

            step = is_live.astype(jnp.int32)
            return front + step, back - (1 - step)

        return lax.fori_loop(0, blocks, put, live)

    state = (jnp.int32(0), jnp.int32(tiles - 1))
    live, _ = lax.fori_loop(0, groups, list_group, state)
    steps = (live + (UNROLL - 1)) // UNROLL

    def over_tiles(body):
        def step(i, carry):
            for u in range(UNROLL):
                body(list_ref[i * UNROLL + u])
            return carry

        lax.fori_loop(0, steps, step, 0)

    table[:, :atoms] = own_ref[...]
    table[:, atoms : 2 * atoms] = lrec_ref[...]
    table[:, 2 * atoms :] = rrec_ref[...]
    rank_up[...] = iota((atoms, atoms), 0).astype(f32).astype(bf16)
    wout_t[...] = jnp.transpose(rout_ref[...].astype(f32)).astype(bf16)
    dvec[...] = jnp.zeros(dvec.shape, f32)
    dharm[...] = jnp.zeros(dharm.shape, f32)
    dbas[...] = jnp.zeros(dbas.shape, f32)
    abuf[...] = jnp.zeros(abuf.shape, f32)
    acc[...] = jnp.zeros(acc.shape, f32)
    one, zero = jnp.ones((), bf16), jnp.zeros((), bf16)

    def gather(t):
        ids = nbt_ref[pl.ds(t, 1), :]
        up = rank_up[...]
        for s in range(3):
            row = jnp.broadcast_to((ids - float(s * atoms)).astype(bf16), (atoms, atoms))
            selbuf[t, s * atoms : (s + 1) * atoms, :] = jnp.where(row == up, one, zero)
        got = dot(table[...], selbuf[t])
        gbuf[t] = got[:chans].astype(bf16)
        tail = got[chans:]
        near = tail[0:8] + tail[3:11] + tail[6:14]
        away = near - self_ref[t // groups]
        for d in range(3):
            dvec[d, pl.ds(t, 1), :] = away[d : d + 1]

    over_tiles(gather)

    dx, dy, dz = dvec[0], dvec[1], dvec[2]
    r2 = dx * dx + dy * dy + dz * dz
    dist = jnp.sqrt(r2 + 0.25)
    inv = 1.0 / dist
    env = jnp.maximum(1.0 - r2 * (1.0 / (cut_radius * cut_radius)), 0.0)
    env2 = env * env
    ux, uy, uz = dx * inv, dy * inv, dz * inv
    radc[0] = dist * (0.5 / cut_radius)
    radc[1] = env2 * inv
    harm[0] = ux
    harm[1] = uy
    harm[2] = uz
    harm[3] = sqrt_three * ux * uy
    harm[4] = sqrt_three * uy * uz
    harm[5] = 0.5 * (3.0 * uz * uz - (ux * ux + uy * uy + uz * uz))
    harm[6] = sqrt_three * ux * uz
    harm[7] = 0.5 * sqrt_three * (ux * ux - uy * uy)

    lanes = atoms
    same = iota((BLOCK, lanes), 0) == (iota((BLOCK, lanes), 1) % BLOCK)
    seg = jnp.where(same, 1.0, 0.0).astype(bf16)
    rin_hi, rin_lo = parts(rin_ref[...], 2)
    rin_t = jnp.concatenate([rin_hi, rin_lo, rin_hi, jnp.zeros_like(rin_hi)], axis=0).astype(bf16)
    rin_b = jnp.concatenate([rin_hi, rin_lo], axis=0).astype(bf16)
    order = (iota((nbasis, lanes), 0) + 1).astype(f32)

    def forward(t):
        turn = order * radc[0, pl.ds(t, 1), :]
        half = pi * (turn - jnp.floor(turn + 0.5))
        sq = half * half
        s = half * (
            1.0
            + sq
            * (
                -1.0 / 6
                + sq * (1.0 / 120 + sq * (-1.0 / 5040 + sq * (1.0 / 362880 + sq * (-1.0 / 39916800))))
            )
        )
        c = 1.0 + sq * (
            -0.5
            + sq
            * (
                1.0 / 24
                + sq * (-1.0 / 720 + sq * (1.0 / 40320 + sq * (-1.0 / 3628800 + sq * (1.0 / 479001600))))
            )
        )
        sn, cs = 2.0 * s * c, 1.0 - 2.0 * s * s
        sinb[t] = sn
        cosb[t] = cs * order
        basis = sn * radc[1, pl.ds(t, 1), :]
        b_hi, b_lo = parts(basis, 2)
        b_all = jnp.concatenate([b_hi, b_hi, b_lo, jnp.zeros_like(b_hi)], axis=0).astype(bf16)
        pre = dot(rin_t, b_all, 0, 0)
        sig = sigmoid(pre)
        dsil[t] = sig * (1.0 + pre * (1.0 - sig))
        radial = dot(wout_t[...], (pre * sig).astype(bf16)).astype(bf16)
        rbuf[t] = radial
        for m in range(8):
            row = jnp.broadcast_to(harm[m, pl.ds(t, 1), :], (BLOCK, lanes))
            ybuf[t, m * BLOCK : (m + 1) * BLOCK, :] = jnp.where(same, row, 0.0).astype(bf16)
        g = gbuf[t]
        b = t // groups
        abuf[b, :BLOCK, :] += dot(seg, radial[:chans] * g, 1, 1)
        abuf[b, BLOCK : 4 * BLOCK, :] += dot(
            ybuf[t, : 3 * BLOCK, :], radial[chans : 2 * chans] * g, 1, 1
        )
        abuf[b, 4 * BLOCK :, :] += dot(ybuf[t, 3 * BLOCK :, :], radial[2 * chans :] * g, 1, 1)

    over_tiles(forward)

    def alpha(lm):
        return abuf[:, lm * BLOCK : (lm + 1) * BLOCK, :].reshape(atoms, chans) * scale

    inv_l = [alpha(0)]
    for ms in (range(1, 4), range(4, 9)):
        total = None
        for lm in ms:
            a = alpha(lm)
            total = a * a if total is None else total + a * a
        inv_l.append(total)
    p = None
    for l in range(3):
        term = dot(inv_l[l].astype(bf16), pw_ref[l * chans : (l + 1) * chans, :])
        p = term if p is None else p + term
    sig = sigmoid(p)
    read = read_ref[...]
    e_col = jnp.sum(p * sig * read, axis=1, keepdims=True)
    place = rank_ref[...] == iota((atoms, atoms), 0).astype(f32)
    en_ref[...] = (
        jnp.sum(jnp.where(place, jnp.broadcast_to(e_col, (atoms, atoms)), 0.0), axis=0, keepdims=True)
        + edir_ref[...]
    )
    dp = (read * sig * (1.0 + p * (1.0 - sig))).astype(bf16)
    for l, ms in enumerate((range(1), range(1, 4), range(4, 9))):
        dinv = dot(dp, pw_ref[l * chans : (l + 1) * chans, :], 1, 1) * scale
        for lm in ms:
            da = dinv if l == 0 else 2.0 * alpha(lm) * dinv
            dabuf[:, lm * BLOCK : (lm + 1) * BLOCK, :] = da.reshape(blocks, BLOCK, chans).astype(bf16)

    def backward(t):
        b = t // groups
        g = gbuf[t]
        ends = (0, 1, 4, 9)
        dg = None
        dhid = None
        for l in range(3):
            lo, hi = ends[l] * BLOCK, ends[l + 1] * BLOCK
            da = dabuf[b, lo:hi, :]
            y = seg if l == 0 else ybuf[t, lo - BLOCK : hi - BLOCK, :]
            dterm = dot(da, y, 0, 0).astype(bf16)
            radial = rbuf[t, l * chans : (l + 1) * chans, :]
            part = dterm * radial
            dg = part if dg is None else dg + part
            part = dot(rout_ref[:, l * chans : (l + 1) * chans], dterm * g)
            dhid = part if dhid is None else dhid + part
            if l:
                cross = dot(da, radial * g)
                for m in range(2 * l + 1):
                    mine = jnp.where(same, cross[m * BLOCK : (m + 1) * BLOCK, :], 0.0)
                    dharm[ends[l] - 1 + m, pl.ds(t, 1), :] = jnp.sum(mine, axis=0, keepdims=True)
        dgbuf[t, :chans, :] = dg
        both = dot(rin_b, (dhid * dsil[t]).astype(bf16))
        dbasis = both[:nbasis] + both[nbasis:]
        dbas[0, pl.ds(t, 1), :] = jnp.sum(dbasis * sinb[t], axis=0, keepdims=True)
        dbas[1, pl.ds(t, 1), :] = jnp.sum(dbasis * cosb[t], axis=0, keepdims=True)

    over_tiles(backward)

    dx, dy, dz = dvec[0], dvec[1], dvec[2]
    r2 = dx * dx + dy * dy + dz * dz
    inv = 1.0 / jnp.sqrt(r2 + 0.25)
    env = jnp.maximum(1.0 - r2 * (1.0 / (cut_radius * cut_radius)), 0.0)
    env2 = env * env
    ux, uy, uz = harm[0], harm[1], harm[2]
    gx = dharm[0] + sqrt_three * (uy * dharm[3] + uz * dharm[6] + ux * dharm[7]) - ux * dharm[5]
    gy = dharm[1] + sqrt_three * (ux * dharm[3] + uz * dharm[4] - uy * dharm[7]) - uy * dharm[5]
    gz = dharm[2] + sqrt_three * (uy * dharm[4] + ux * dharm[6]) + 2.0 * uz * dharm[5]
    dinv = dbas[0] * env2 + gx * dx + gy * dy + gz * dz
    ddist = radc[1] * (pi / cut_radius) * dbas[1] - inv * inv * dinv
    dr2 = 0.5 * inv * ddist - dbas[0] * inv * env * (2.0 / (cut_radius * cut_radius))
    slope = []
    for d, (grad, delta) in enumerate(((gx, dx), (gy, dy), (gz, dz))):
        value = grad * inv + 2.0 * delta * dr2
        slope.append(value)
        dvec[d] = value

    self_rows = []
    lane_block = iota((blocks, lanes), 1) // BLOCK
    for value in slope:
        fold = jnp.sum(value.reshape(blocks, groups, lanes), axis=1)
        by = lanes // 2
        while by >= BLOCK:
            fold = fold + pltpu.roll(fold, by, 1)
            by //= 2
        self_rows.append(
            jnp.sum(jnp.where(lane_block == iota((blocks, lanes), 0), fold, 0.0), axis=0, keepdims=True)
        )
    split = [parts(row, 3) for row in self_rows]
    rows = [split[d][k] for k in range(3) for d in range(3)]
    place = jnp.where(rank_ref[...] == iota((atoms, atoms), 0).astype(f32), 1.0, 0.0).astype(bf16)
    back = dot(stack_rows(rows, EXTRA).astype(bf16), place)
    self_grad = back[0:8] + back[3:11] + back[6:14]

    def scatter(t):
        rows = []
        for d in range(3):
            rows.append(parts(dvec[d, pl.ds(t, 1), :], 2))
        rows = [rows[d][k] for k in range(2) for d in range(3)]
        dgbuf[t, chans:, :] = stack_rows(rows, EXTRA).astype(bf16)
        acc[...] += dot(dgbuf[t], selbuf[t], 1, 1)

    over_tiles(scatter)

    dmix_ref[...] = acc[:chans, :atoms]
    tail = acc[chans:, :]
    near = tail[0:8] + tail[3:11]
    dpos_ref[...] = near[:, :atoms] - self_grad
    for s, out in ((1, gl_ref), (2, gr_ref)):
        out[:chans, :] = acc[:chans, s * atoms : (s + 1) * atoms].astype(bf16)
        pieces = parts(near[:, s * atoms : (s + 1) * atoms], 2)
        rows = [q[d : d + 1] for q in pieces for d in range(3)]
        out[chans:, :] = stack_rows(rows, EXTRA).astype(bf16)


def final_kernel(
    dmix_ref, dpos_ref, bl_ref, br_ref, sl_ref, sr_ref, mix_ref, spec_ref, gain_ref, read_ref, force_ref, grad_ref
):
    chans, atoms = dmix_ref.shape
    ghosts = sl_ref.shape[1]
    total = None
    for lst, rec in ((sr_ref, br_ref), (sl_ref, bl_ref)):
        pick = (iota((atoms, ghosts), 0) == lst[...]).astype(f32).astype(bf16)
        part = dot(rec[:, :ghosts], pick, 1, 1)
        total = part if total is None else total + part
    tail = total[chans:]
    pos = dpos_ref[...] + tail[0:8] + tail[3:11]
    force_ref[...] = -pos[:3]
    d_mixed = dmix_ref[...] + total[:chans]
    weight = gain_ref[...] * read_ref[...]
    kinds = weight.shape[0]
    chosen = (iota((kinds, atoms), 0) == spec_ref[...]).astype(f32)
    grad = None
    for q in parts(weight, 3):
        part = dot(chosen.astype(bf16), q.astype(bf16), 0, 0)
        grad = part if grad is None else grad + part
    for q in parts(d_mixed, 2):
        grad += dot(q.astype(bf16), mix_ref[...], 0, 1)
    grad_ref[...] = grad


def vmem(count):
    return [pl.BlockSpec(memory_space=pltpu.VMEM)] * count


def per_device(
    positions,
    features,
    species,
    neighbours,
    near_count,
    send_left,
    send_right,
    radial_in,
    radial_out,
    mix_weight,
    product_weight,
    species_gain,
    readout,
):
    atoms, chans = features.shape
    ghosts = send_left.shape[0]
    slots = neighbours.shape[1]
    nbasis, hid_n = radial_in.shape
    blocks, groups = atoms // BLOCK, slots // DEPTH
    tiles = blocks * groups
    high = chans + EXTRA
    sl, sr = send_left.reshape(1, ghosts), send_right.reshape(1, ghosts)
    cnt, spec = near_count.reshape(1, atoms), species.reshape(1, atoms)
    read = readout.reshape(1, chans)
    shape = jax.ShapeDtypeStruct
    params = pltpu.CompilerParams(vmem_limit_bytes=52 * 1024 * 1024)
    small = pltpu.CompilerParams(vmem_limit_bytes=16 * 1024 * 1024)

    own, to_right, to_left = pl.pallas_call(
        pack_kernel,
        out_shape=[shape((high, atoms), bf16)] * 3,
        in_specs=vmem(5),
        out_specs=vmem(3),
        compiler_params=small,
        name="pack",
    )(positions, features, mix_weight, sl, sr)
    from_left = shifted(to_right, "dom", 1)
    from_right = shifted(to_left, "dom", -1)

    nbt, self_pos, rank, edir = pl.pallas_call(
        functools.partial(sort_kernel, ghosts),
        out_shape=[
            shape((tiles, atoms), f32),
            shape((blocks, 8, atoms), f32),
            shape((1, atoms), f32),
            shape((1, atoms), f32),
        ],
        in_specs=vmem(7),
        out_specs=vmem(4),
        compiler_params=small,
        cost_estimate=pl.CostEstimate(flops=200_000_000, bytes_accessed=2_000_000, transcendentals=0),
        name="sort",
    )(positions, cnt, neighbours, features, spec, species_gain, read)
    depth = jnp.sum(
        (near_count[None, :] > DEPTH * jnp.arange(groups)[:, None]).astype(jnp.int32), axis=1
    ).astype(jnp.int32)

    scratch = [
        pltpu.SMEM((tiles,), jnp.int32),
        pltpu.VMEM((high, 3 * atoms), bf16),
        pltpu.VMEM((tiles, 3 * atoms, atoms), bf16),
        pltpu.VMEM((tiles, chans, atoms), bf16),
        pltpu.VMEM((tiles, 3 * chans, atoms), bf16),
        pltpu.VMEM((tiles, 8 * BLOCK, atoms), bf16),
        pltpu.VMEM((tiles, high, atoms), bf16),
        pltpu.VMEM((blocks, 9 * BLOCK, chans), f32),
        pltpu.VMEM((blocks, 9 * BLOCK, chans), bf16),
        pltpu.VMEM((high, 3 * atoms), f32),
        pltpu.VMEM((3, tiles, atoms), f32),
        pltpu.VMEM((8, tiles, atoms), f32),
        pltpu.VMEM((2, tiles, atoms), f32),
        pltpu.VMEM((tiles, nbasis, atoms), f32),
        pltpu.VMEM((tiles, nbasis, atoms), f32),
        pltpu.VMEM((tiles, hid_n, atoms), f32),
        pltpu.VMEM((8, tiles, atoms), f32),
        pltpu.VMEM((2, tiles, atoms), f32),
        pltpu.VMEM((3 * chans, hid_n), bf16),
        pltpu.VMEM((atoms, atoms), bf16),
    ]
    energies, dmix, dpos, ghost_left, ghost_right = pl.pallas_call(
        main_kernel,
        out_shape=[
            shape((1, atoms), f32),
            shape((chans, atoms), f32),
            shape((8, atoms), f32),
            shape((high, atoms), bf16),
            shape((high, atoms), bf16),
        ],
        in_specs=[pl.BlockSpec(memory_space=pltpu.SMEM)] + vmem(11),
        out_specs=vmem(5),
        scratch_shapes=scratch,
        compiler_params=params,
        name="interact",
    )(
        depth,
        own,
        from_left,
        from_right,
        nbt,
        self_pos,
        rank,
        edir,
        radial_in,
        radial_out,
        product_weight,
        read,
    )
    back_right = shifted(ghost_left, "dom", -1)
    back_left = shifted(ghost_right, "dom", 1)
    forces, feature_grad = pl.pallas_call(
        final_kernel,
        out_shape=[shape((3, atoms), f32), shape((atoms, chans), f32)],
        in_specs=vmem(10),
        out_specs=vmem(2),
        compiler_params=small,
        name="finish",
    )(dmix, dpos, back_left, back_right, sl, sr, mix_weight, spec, species_gain, read)
    return (energies.reshape(atoms), forces, feature_grad)


def solution(mesh):
    placed = (
        P(None, ("groups", "dom")),
        P(("groups", "dom"), None),
        P(("groups", "dom")),
        P(("groups", "dom"), None),
        P(("groups", "dom")),
        P(("groups", "dom")),
        P(("groups", "dom")),
        P(),
        P(),
        P(),
        P(),
        P(),
        P(),
    )
    return jax.shard_map(
        per_device,
        mesh=mesh,
        in_specs=placed,
        out_specs=(P(("groups", "dom")), P(None, ("groups", "dom")), P(("groups", "dom"), None)),
        check_vma=False,
    )
```

```python
import functools

import jax
import jax.numpy as jnp
from jax import lax
from jax.experimental import pallas as pl
from jax.experimental.pallas import tpu as pltpu
from jax.sharding import PartitionSpec as P

cut_radius = 5.0
sqrt_three = 1.7320508075688772
pi = 3.141592653589793

f32 = jnp.float32
bf16 = jnp.bfloat16

BLOCK = 32
DEPTH = 8
EXTRA = 16
PACK_LIMIT = 63 * 1024 * 1024 + 512 * 1024
UNROLL_G = 8
UNROLL_H = 8
UNROLL_F = 8
UNROLL_B = 8
UNROLL_E = 8
UNROLL_D = 8
UNROLL_S = 8


def swapped(value, axis, odd):
    count = lax.axis_size(axis)
    partner = [((i + odd) ^ 1) - odd for i in range(count)]
    pairs = [(i, j) for i, j in enumerate(partner) if 0 <= j < count]
    return lax.ppermute(value, axis, pairs)


def iota(shape, dim):
    return lax.broadcasted_iota(jnp.int32, shape, dim)


def dot(a, b, ca=1, cb=0):
    return lax.dot_general(a, b, (((ca,), (cb,)), ((), ())), preferred_element_type=f32)


def parts(value, count):
    out = []
    for _ in range(count):
        head = value.astype(bf16).astype(f32)
        out.append(head)
        value = value - head
    return out


def stack_rows(rows, height):
    lanes = rows[0].shape[1]
    at = iota((height, lanes), 0)
    out = jnp.zeros((height, lanes), f32)
    for idx, row in enumerate(rows):
        out = jnp.where(at == idx, jnp.broadcast_to(row, (height, lanes)), out)
    return out


def sigmoid(x):
    return 1.0 / (1.0 + jnp.exp(-x))


POS, COUNT, SPECIES, READ, LEFT, RIGHT, GAIN = 0, 3, 4, 5, 6, 7, 8


def list_rows(small_ref, odd, ghosts):
    left, right = small_ref[LEFT : LEFT + 1, :ghosts], small_ref[RIGHT : RIGHT + 1, :ghosts]
    return jnp.where(odd, left, right), jnp.where(odd, right, left)


def gain_weight(small_ref):
    return small_ref[GAIN:, :] * small_ref[READ : READ + 1, :]


def pack_kernel(
    odd_ref,
    pos_hbm,
    cnt_hbm,
    spec_hbm,
    read_hbm,
    sl_hbm,
    sr_hbm,
    gain_hbm,
    feat_hbm,
    mix_hbm,
    own_ref,
    a_ref,
    b_ref,
    edir_ref,
    small_ref,
    pos,
    cnt,
    spec,
    read,
    sl,
    sr,
    gain,
    feat,
    mix,
    sems,
):
    hbm = (feat_hbm, mix_hbm, pos_hbm, sl_hbm, sr_hbm, cnt_hbm, spec_hbm, read_hbm, gain_hbm)
    here = (feat, mix, pos, sl, sr, cnt, spec, read, gain)
    copies = [pltpu.make_async_copy(src, dst, sems.at[k]) for k, (src, dst) in enumerate(zip(hbm, here))]
    for copy in copies:
        copy.start()
    for copy in copies:
        copy.wait()
    small_ref[POS : POS + 3, :] = pos[...]
    small_ref[COUNT : COUNT + 1, :] = cnt[...].astype(f32)
    small_ref[SPECIES : SPECIES + 1, :] = spec[...].astype(f32)
    small_ref[READ : READ + 1, :] = read[...]
    for at, lst in ((LEFT, sl), (RIGHT, sr)):
        small_ref[at : at + 1, :] = jnp.full((1, small_ref.shape[1]), -1.0, f32)
        small_ref[at : at + 1, : lst.shape[1]] = lst[...].astype(f32)
    small_ref[GAIN:, :] = gain[...]
    chans, atoms = own_ref.shape[0] - EXTRA, own_ref.shape[1]
    ghosts = a_ref.shape[0] - EXTRA
    mixed = dot(feat[...], mix[...]).astype(bf16)
    rows = [p[d : d + 1, :] for p in parts(small_ref[POS : POS + 3, :], 3) for d in range(3)]
    rows = stack_rows(rows, EXTRA).astype(bf16)
    for lst, out in zip(list_rows(small_ref, odd_ref[0] == 1, ghosts), (a_ref, b_ref)):
        pick = (iota((atoms, ghosts), 0).astype(f32) == lst).astype(f32).astype(bf16)
        out[:ghosts, :] = dot(pick, mixed, 0, 0).astype(bf16)
        out[ghosts:, :ghosts] = dot(rows, pick).astype(bf16)
        out[ghosts:, ghosts:] = jnp.zeros((EXTRA, chans - ghosts), bf16)
    own_ref[:chans, :] = dot(mix[...], feat[...], 0, 1).astype(bf16)
    own_ref[chans:, :] = rows
    weight = gain_weight(small_ref)
    kinds = weight.shape[0]
    direct = jnp.zeros((kinds, atoms), f32)
    for p in parts(weight, 3):
        direct += dot(p.astype(bf16), feat[...], 1, 1)
    mine = iota((kinds, atoms), 0).astype(f32) == small_ref[SPECIES : SPECIES + 1, :]
    edir_ref[...] = jnp.sum(jnp.where(mine, direct, 0.0), axis=0, keepdims=True)


def sort_kernel(ghosts, odd_ref, small_ref, nb_ref, nbt_ref, self_ref, rank_ref):
    slots, atoms = nb_ref.shape
    cnt_row = small_ref[COUNT : COUNT + 1, :]
    up, across = iota((atoms, atoms), 0), iota((atoms, atoms), 1)
    cnt_col = jnp.sum(jnp.where(up == across, cnt_row, 0.0), axis=1, keepdims=True)
    ahead_row = (cnt_col > cnt_row) | ((cnt_col == cnt_row) & (up < across))
    ahead_col = (cnt_row > cnt_col) | ((cnt_row == cnt_col) & (across < up))
    rank_row = jnp.sum(ahead_row.astype(f32), axis=0, keepdims=True)
    rank_col = jnp.sum(ahead_col.astype(f32), axis=1, keepdims=True)
    rank_ref[...] = rank_row
    nb = nb_ref[...]
    odd = odd_ref[0]
    to_left = jnp.where(odd == 1, 0, atoms)
    to_right = jnp.where(odd == 1, atoms - ghosts, -ghosts)
    nb = jnp.where(nb >= atoms + ghosts, nb + to_right, jnp.where(nb >= atoms, nb + to_left, nb))
    nbt = nb.astype(f32)
    high = jnp.floor(nbt * (1.0 / 256.0))
    low = nbt - high * 256.0
    rows = [p[d : d + 1, :] for p in parts(small_ref[POS : POS + 3, :], 3) for d in range(3)] + [cnt_row]
    left = jnp.concatenate([high, low, stack_rows(rows, EXTRA)], axis=0).astype(bf16)
    lane_atom = (across % BLOCK).astype(f32)
    lane_slot = iota((slots, atoms), 1) // BLOCK
    mine = lane_slot == (iota((slots, atoms), 0) % DEPTH)
    depth_at = iota((slots // DEPTH, atoms), 0) * DEPTH + iota((slots // DEPTH, atoms), 1) // BLOCK
    groups = slots // DEPTH
    for b in range(atoms // BLOCK):
        pick = (rank_col - float(b * BLOCK) == lane_atom).astype(f32).astype(bf16)
        got = dot(left, pick)
        ids = got[:slots] * 256.0 + got[slots : 2 * slots]
        tail = got[2 * slots :]
        ids = jnp.sum(jnp.where(mine, ids, 0.0).reshape(groups, DEPTH, atoms), axis=1)
        ids = jnp.where(depth_at.astype(f32) < tail[9:10], ids, -1.0)
        nbt_ref[b * groups : (b + 1) * groups, :] = ids
        self_ref[b] = tail[0:8] + tail[3:11] + tail[6:14]


def tile_loop(depth_ref, list_ref, blocks, groups):
    def list_group(j, live):
        need = (depth_ref[j] + (BLOCK - 1)) // BLOCK

        def put(b, state):
            front, back = state
            is_live = b < need

            @pl.when(is_live)
            def _():
                list_ref[front] = b * groups + j

            @pl.when(jnp.logical_not(is_live))
            def _():
                list_ref[back] = b * groups + j

            step = is_live.astype(jnp.int32)
            return front + step, back - (1 - step)

        return lax.fori_loop(0, blocks, put, live)

    state = (jnp.int32(0), jnp.int32(blocks * groups - 1))
    live, _ = lax.fori_loop(0, groups, list_group, state)

    def over_tiles(body, unroll):
        def step(i, carry):
            for u in range(unroll):
                body(list_ref[i * unroll + u])
            return carry

        lax.fori_loop(0, (live + (unroll - 1)) // unroll, step, 0)

    return over_tiles


def selection(ids, up, sections):
    one, zero = jnp.ones((), bf16), jnp.zeros((), bf16)
    pieces = []
    for s in sections:
        row = jnp.broadcast_to((ids - float(s * up.shape[0])).astype(bf16), up.shape)
        pieces.append(jnp.where(row == up, one, zero))
    return jnp.concatenate(pieces, axis=0)


def fill_section(table, low, rec_ref, chans, atoms):
    ghosts = rec_ref.shape[0] - EXTRA
    table[:chans, low : low + ghosts] = jnp.transpose(rec_ref[:ghosts, :].astype(f32)).astype(bf16)
    table[chans:, low : low + ghosts] = rec_ref[ghosts:, :ghosts]
    table[:, low + ghosts : low + atoms] = jnp.zeros((chans + EXTRA, atoms - ghosts), bf16)


def early_kernel(depth_ref, own_ref, arec_ref, nbt_ref, g_ref, near_ref, list_ref, table, rank_up):
    high, atoms = own_ref.shape
    chans = high - EXTRA
    tiles = nbt_ref.shape[0]
    blocks = atoms // BLOCK
    over_tiles = tile_loop(depth_ref, list_ref, blocks, tiles // blocks)
    rank_up[...] = iota((atoms, atoms), 0).astype(f32).astype(bf16)
    table[:, :atoms] = own_ref[...]
    fill_section(table, atoms, arec_ref, chans, atoms)

    def gather(t):
        got = dot(table[...], selection(nbt_ref[pl.ds(t, 1), :], rank_up[...], (0, 1)))
        g_ref[t] = got[:chans].astype(bf16)
        tail = got[chans:]
        near = tail[0:8] + tail[3:11] + tail[6:14]
        for d in range(3):
            near_ref[d, pl.ds(t, 1), :] = near[d : d + 1]

    over_tiles(gather, UNROLL_G)


def main_kernel(
    depth_ref,
    gpart_ref,
    near_ref,
    brec_ref,
    nbt_ref,
    self_ref,
    rank_ref,
    edir_ref,
    rin_ref,
    rout_ref,
    pw_ref,
    small_ref,
    en_ref,
    dgbuf,
    spos_ref,
    gb_ref,
    list_ref,
    table,
    drbuf,
    gbuf,
    rbuf,
    ybuf,
    abuf,
    dabuf,
    zbuf,
    dfold,
    acc,
    dvec,
    harm,
    radc,
    sinb,
    cosb,
    dsil,
    hidb,
    dharm,
    dbas,
    wout_t,
    rank_up,
):
    tiles, chans, atoms = gpart_ref.shape
    high = chans + EXTRA
    blocks = atoms // BLOCK
    groups = tiles // blocks
    hid_n = rout_ref.shape[0]
    nbasis = rin_ref.shape[0]
    scale = 1.0 / (groups * DEPTH)

    over_tiles = tile_loop(depth_ref, list_ref, blocks, groups)

    ghosts = brec_ref.shape[0] - EXTRA
    fill_section(table, 0, brec_ref, chans, atoms)
    rank_up[...] = iota((atoms, atoms), 0).astype(f32).astype(bf16)
    wout_t[...] = jnp.transpose(rout_ref[...].astype(f32)).astype(bf16)
    dvec[...] = jnp.zeros(dvec.shape, f32)
    dharm[...] = jnp.zeros(dharm.shape, f32)
    dbas[...] = jnp.zeros(dbas.shape, f32)
    abuf[...] = jnp.zeros(abuf.shape, f32)
    zbuf[...] = jnp.zeros(zbuf.shape, f32)
    acc[...] = jnp.zeros(acc.shape, f32)
    def gather(t):
        got = dot(table[...], selection(nbt_ref[pl.ds(t, 1), :], rank_up[...], (2,)))
        gbuf[t] = gpart_ref[t] + got[:chans].astype(bf16)
        tail = got[chans:]
        near = tail[0:8] + tail[3:11] + tail[6:14]
        away = near - self_ref[t // groups]
        for d in range(3):
            dvec[d, pl.ds(t, 1), :] = near_ref[d, pl.ds(t, 1), :] + away[d : d + 1]

    over_tiles(gather, UNROLL_G)

    dx, dy, dz = dvec[0], dvec[1], dvec[2]
    r2 = dx * dx + dy * dy + dz * dz
    dist = jnp.sqrt(r2 + 0.25)
    inv = 1.0 / dist
    env = jnp.maximum(1.0 - r2 * (1.0 / (cut_radius * cut_radius)), 0.0)
    env2 = env * env
    ux, uy, uz = dx * inv, dy * inv, dz * inv
    radc[0] = dist * (0.5 / cut_radius)
    radc[1] = env2 * inv
    harm[0] = ux
    harm[1] = uy
    harm[2] = uz
    harm[3] = sqrt_three * ux * uy
    harm[4] = sqrt_three * uy * uz
    harm[5] = 0.5 * (3.0 * uz * uz - (ux * ux + uy * uy + uz * uz))
    harm[6] = sqrt_three * ux * uz
    harm[7] = 0.5 * sqrt_three * (ux * ux - uy * uy)

    lanes = atoms
    same = iota((BLOCK, lanes), 0) == (iota((BLOCK, lanes), 1) % BLOCK)
    seg = jnp.where(same, 1.0, 0.0).astype(bf16)
    rin_hi, rin_lo = parts(rin_ref[...], 2)
    rin_t = jnp.concatenate([rin_hi, rin_lo, rin_hi, jnp.zeros_like(rin_hi)], axis=0).astype(bf16)
    rin_b = jnp.concatenate([rin_hi, rin_lo], axis=0).astype(bf16)
    order = (iota((nbasis, lanes), 0) + 1).astype(f32)

    def hidden(t):
        turn = order * radc[0, pl.ds(t, 1), :]
        half = pi * (turn - jnp.floor(turn + 0.5))
        sq = half * half
        s = half * (
            1.0
            + sq
            * (
                -1.0 / 6
                + sq * (1.0 / 120 + sq * (-1.0 / 5040 + sq * (1.0 / 362880 + sq * (-1.0 / 39916800))))
            )
        )
        c = 1.0 + sq * (
            -0.5
            + sq
            * (
                1.0 / 24
                + sq * (-1.0 / 720 + sq * (1.0 / 40320 + sq * (-1.0 / 3628800 + sq * (1.0 / 479001600))))
            )
        )
        sn, cs = 2.0 * s * c, 1.0 - 2.0 * s * s
        sinb[t] = sn
        cosb[t] = cs * order
        basis = sn * radc[1, pl.ds(t, 1), :]
        b_hi, b_lo = parts(basis, 2)
        b_all = jnp.concatenate([b_hi, b_hi, b_lo, jnp.zeros_like(b_hi)], axis=0).astype(bf16)
        pre = dot(rin_t, b_all, 0, 0)
        sig = sigmoid(pre)
        dsil[t] = sig * (1.0 + pre * (1.0 - sig))
        hidb[t] = (pre * sig).astype(bf16)
        for m in range(8):
            row = jnp.broadcast_to(harm[m, pl.ds(t, 1), :], (BLOCK, lanes))
            ybuf[t, m * BLOCK : (m + 1) * BLOCK, :] = jnp.where(same, row, 0.0).astype(bf16)

    def forward(t):
        radial = dot(wout_t[...], hidb[t]).astype(bf16)
        rbuf[t] = radial
        g = gbuf[t]
        b = t // groups
        zbuf[b] += dot(seg, radial[:chans] * g, 1, 1)
        abuf[b, : 3 * BLOCK, :] += dot(
            ybuf[t, : 3 * BLOCK, :], radial[chans : 2 * chans] * g, 1, 1
        )
        abuf[b, 3 * BLOCK :, :] += dot(ybuf[t, 3 * BLOCK :, :], radial[2 * chans :] * g, 1, 1)

    over_tiles(hidden, UNROLL_H)
    over_tiles(forward, UNROLL_F)

    def alpha(lm):
        return abuf[:, (lm - 1) * BLOCK : lm * BLOCK, :].reshape(atoms, chans) * scale

    seg_half = seg[:, : lanes // 2]
    inv_l = [zbuf[...].reshape(atoms, chans) * scale]
    for ms in (range(1, 4), range(4, 9)):
        total = None
        for lm in ms:
            a = alpha(lm)
            total = a * a if total is None else total + a * a
        inv_l.append(total)
    p = None
    for l in range(3):
        term = dot(inv_l[l].astype(bf16), pw_ref[l * chans : (l + 1) * chans, :])
        p = term if p is None else p + term
    sig = sigmoid(p)
    read = small_ref[READ : READ + 1, :]
    e_col = jnp.sum(p * sig * read, axis=1, keepdims=True)
    place = rank_ref[...] == iota((atoms, atoms), 0).astype(f32)
    en_ref[...] = (
        jnp.sum(jnp.where(place, jnp.broadcast_to(e_col, (atoms, atoms)), 0.0), axis=0, keepdims=True)
        + edir_ref[...]
    )
    dp = (read * sig * (1.0 + p * (1.0 - sig))).astype(bf16)
    for l, ms in enumerate((range(1), range(1, 4), range(4, 9))):
        dinv = dot(dp, pw_ref[l * chans : (l + 1) * chans, :], 1, 1) * scale
        if l == 0:
            dinv = dinv.astype(bf16)
            for b in range(blocks):
                dfold[b] = dot(dinv[b * BLOCK : (b + 1) * BLOCK, :], seg_half, 0, 0).astype(bf16)
        for lm in ms if l else ():
            da = 2.0 * alpha(lm) * dinv
            dabuf[:, (lm - 1) * BLOCK : lm * BLOCK, :] = da.reshape(blocks, BLOCK, chans).astype(bf16)

    def backward(t):
        b = t // groups
        g = gbuf[t]
        ends = (0, 3, 8)
        half = dfold[b]
        dterm = jnp.concatenate([half, half], axis=1)
        dg = dterm * rbuf[t, :chans, :]
        drbuf[t, :chans, :] = dterm * g
        for l in (1, 2):
            lo, hi = ends[l - 1] * BLOCK, ends[l] * BLOCK
            da = dabuf[b, lo:hi, :]
            dterm = dot(da, ybuf[t, lo:hi, :], 0, 0).astype(bf16)
            radial = rbuf[t, l * chans : (l + 1) * chans, :]
            dg = dg + dterm * radial
            drbuf[t, l * chans : (l + 1) * chans, :] = dterm * g
            cross = dot(da, radial * g)
            for m in range(2 * l + 1):
                mine = jnp.where(same, cross[m * BLOCK : (m + 1) * BLOCK, :], 0.0)
                dharm[ends[l - 1] + m, pl.ds(t, 1), :] = jnp.sum(mine, axis=0, keepdims=True)
        dgbuf[t, :chans, :] = dg

    def enter(t):
        hidb[t] = (dot(rout_ref[...], drbuf[t]) * dsil[t]).astype(bf16)

    def dhidden(t):
        both = dot(rin_b, hidb[t])
        dbasis = both[:nbasis] + both[nbasis:]
        dbas[0, pl.ds(t, 1), :] = jnp.sum(dbasis * sinb[t], axis=0, keepdims=True)
        dbas[1, pl.ds(t, 1), :] = jnp.sum(dbasis * cosb[t], axis=0, keepdims=True)

    over_tiles(backward, UNROLL_B)
    over_tiles(enter, UNROLL_E)
    over_tiles(dhidden, UNROLL_D)

    dx, dy, dz = dvec[0], dvec[1], dvec[2]
    r2 = dx * dx + dy * dy + dz * dz
    inv = 1.0 / jnp.sqrt(r2 + 0.25)
    env = jnp.maximum(1.0 - r2 * (1.0 / (cut_radius * cut_radius)), 0.0)
    env2 = env * env
    ux, uy, uz = harm[0], harm[1], harm[2]
    gx = dharm[0] + sqrt_three * (uy * dharm[3] + uz * dharm[6] + ux * dharm[7]) - ux * dharm[5]
    gy = dharm[1] + sqrt_three * (ux * dharm[3] + uz * dharm[4] - uy * dharm[7]) - uy * dharm[5]
    gz = dharm[2] + sqrt_three * (uy * dharm[4] + ux * dharm[6]) + 2.0 * uz * dharm[5]
    dinv = dbas[0] * env2 + gx * dx + gy * dy + gz * dz
    ddist = radc[1] * (pi / cut_radius) * dbas[1] - inv * inv * dinv
    dr2 = 0.5 * inv * ddist - dbas[0] * inv * env * (2.0 / (cut_radius * cut_radius))
    slope = []
    for d, (grad, delta) in enumerate(((gx, dx), (gy, dy), (gz, dz))):
        value = grad * inv + 2.0 * delta * dr2
        slope.append(value)
        dvec[d] = value

    self_rows = []
    lane_block = iota((blocks, lanes), 1) // BLOCK
    for value in slope:
        folded = jnp.sum(value.reshape(blocks, groups, lanes), axis=1)
        by = lanes // 2
        while by >= BLOCK:
            folded = folded + pltpu.roll(folded, by, 1)
            by //= 2
        self_rows.append(
            jnp.sum(jnp.where(lane_block == iota((blocks, lanes), 0), folded, 0.0), axis=0, keepdims=True)
        )
    split = [parts(row, 3) for row in self_rows]
    rows = [split[d][k] for k in range(3) for d in range(3)]
    place = jnp.where(rank_ref[...] == iota((atoms, atoms), 0).astype(f32), 1.0, 0.0).astype(bf16)
    back = dot(stack_rows(rows, EXTRA).astype(bf16), place)
    spos_ref[...] = back[0:8] + back[3:11] + back[6:14]

    def scatter(t):
        rows = []
        for d in range(3):
            rows.append(parts(dvec[d, pl.ds(t, 1), :], 2))
        rows = [rows[d][k] for k in range(2) for d in range(3)]
        dgbuf[t, chans:, :] = stack_rows(rows, EXTRA).astype(bf16)
        acc[...] += dot(dgbuf[t], selection(nbt_ref[pl.ds(t, 1), :], rank_up[...], (2,)), 1, 1)

    over_tiles(scatter, UNROLL_S)

    pack_adjoint(acc, 0, gb_ref, chans, atoms)


def pack_adjoint(acc, low, out, chans, atoms):
    ghosts = out.shape[0] - EXTRA
    out[:ghosts, :] = jnp.transpose(acc[:chans, low : low + ghosts]).astype(bf16)
    tail = acc[chans:, low : low + atoms]
    pieces = parts(tail[0:8] + tail[3:11], 2)
    rows = [q[d : d + 1] for q in pieces for d in range(3)]
    out[ghosts:, :] = stack_rows(rows, EXTRA).astype(bf16)


def late_kernel(
    depth_ref,
    odd_ref,
    dg_ref,
    nbt_ref,
    spos_ref,
    small_ref,
    mix_ref,
    ga_ref,
    dpos_ref,
    grad_ref,
    pick_ref,
    list_ref,
    acc,
    rank_up,
):
    tiles, high, atoms = dg_ref.shape
    chans = high - EXTRA
    blocks = atoms // BLOCK
    ghosts = ga_ref.shape[0] - EXTRA
    over_tiles = tile_loop(depth_ref, list_ref, blocks, tiles // blocks)
    rank_up[...] = iota((atoms, atoms), 0).astype(f32).astype(bf16)
    acc[...] = jnp.zeros(acc.shape, f32)

    def scatter(t):
        acc[...] += dot(dg_ref[t], selection(nbt_ref[pl.ds(t, 1), :], rank_up[...], (0, 1)), 1, 1)

    over_tiles(scatter, UNROLL_S)
    pack_adjoint(acc, atoms, ga_ref, chans, atoms)
    tail = acc[chans:, :atoms]
    dpos_ref[...] = tail[0:8] + tail[3:11] - spos_ref[...]
    for k, lst in enumerate(list_rows(small_ref, odd_ref[0] == 1, ghosts)):
        pick_ref[k] = (iota((atoms, ghosts), 0).astype(f32) == lst).astype(f32).astype(bf16)
    weight = gain_weight(small_ref)
    kinds = weight.shape[0]
    chosen = (iota((kinds, atoms), 0).astype(f32) == small_ref[SPECIES : SPECIES + 1, :]).astype(f32)
    grad = None
    for q in parts(weight, 3):
        part = dot(chosen.astype(bf16), q.astype(bf16), 0, 0)
        grad = part if grad is None else grad + part
    for q in parts(acc[:chans, :atoms], 2):
        grad += dot(q.astype(bf16), mix_ref[...], 0, 1)
    grad_ref[...] = grad


def final_kernel(own_ref, dpos_ref, a_ref, b_ref, pick_ref, mix_ref, force_ref, grad_ref):
    ghosts = pick_ref.shape[2]
    total, tail = None, None
    for k, rec in enumerate((a_ref, b_ref)):
        pick = pick_ref[k]
        part, last = dot(rec[:ghosts, :], pick, 0, 1), dot(rec[ghosts:, :ghosts], pick, 1, 1)
        total = part if total is None else total + part
        tail = last if tail is None else tail + last
    pos = dpos_ref[...] + tail[0:8] + tail[3:11]
    force_ref[...] = -pos[:3]
    grad = own_ref[...]
    for q in parts(total, 2):
        grad += dot(q.astype(bf16), mix_ref[...], 0, 1)
    grad_ref[...] = grad


def vmem(count):
    return [pl.BlockSpec(memory_space=pltpu.VMEM)] * count


def per_device(
    positions,
    features,
    species,
    neighbours,
    near_count,
    send_left,
    send_right,
    radial_in,
    radial_out,
    mix_weight,
    product_weight,
    species_gain,
    readout,
):
    atoms, chans = features.shape
    ghosts = send_left.shape[0]
    slots = neighbours.shape[1]
    nbasis, hid_n = radial_in.shape
    blocks, groups = atoms // BLOCK, slots // DEPTH
    tiles = blocks * groups
    high = chans + EXTRA
    rows = [row.reshape(1, atoms) for row in (near_count, species, readout)]
    lists = [row.reshape(1, ghosts) for row in (send_left, send_right)]
    inputs = [positions] + rows + lists + [species_gain, features, mix_weight]
    shape = jax.ShapeDtypeStruct
    params = pltpu.CompilerParams(vmem_limit_bytes=44 * 1024 * 1024)
    small = pltpu.CompilerParams(vmem_limit_bytes=16 * 1024 * 1024)

    odd = (lax.axis_index("dom") % 2).astype(jnp.int32).reshape(1)
    smem = [pl.BlockSpec(memory_space=pltpu.SMEM)]
    own, to_a, to_b, edir, table = pl.pallas_call(
        pack_kernel,
        out_shape=[shape((high, atoms), bf16)]
        + [shape((ghosts + EXTRA, chans), bf16)] * 2
        + [shape((1, atoms), f32), shape((GAIN + species_gain.shape[0], atoms), f32)],
        in_specs=smem + [pl.BlockSpec(memory_space=pltpu.HBM)] * 9,
        out_specs=vmem(5),
        scratch_shapes=[pltpu.VMEM(x.shape, x.dtype) for x in inputs] + [pltpu.SemaphoreType.DMA((9,))],
        compiler_params=pltpu.CompilerParams(vmem_limit_bytes=PACK_LIMIT),
        cost_estimate=pl.CostEstimate(flops=2_000_000_000, bytes_accessed=6_000_000, transcendentals=0),
        name="pack",
    )(odd, *inputs)
    from_a = swapped(to_a, "dom", 0)
    from_b = swapped(to_b, "dom", 1)

    nbt, self_pos, rank = pl.pallas_call(
        functools.partial(sort_kernel, ghosts),
        out_shape=[
            shape((tiles, atoms), f32),
            shape((blocks, 8, atoms), f32),
            shape((1, atoms), f32),
        ],
        in_specs=smem + vmem(2),
        out_specs=vmem(3),
        compiler_params=small,
        cost_estimate=pl.CostEstimate(flops=200_000_000, bytes_accessed=2_000_000, transcendentals=0),
        name="sort",
    )(odd, table, neighbours.T)
    depth = jnp.sum(
        (near_count[None, :] > DEPTH * jnp.arange(groups)[:, None]).astype(jnp.int32), axis=1
    ).astype(jnp.int32)

    scratch = [
        pltpu.SMEM((tiles,), jnp.int32),
        pltpu.VMEM((high, atoms), bf16),
        pltpu.VMEM((tiles, 3 * chans, atoms), bf16),
        pltpu.VMEM((tiles, chans, atoms), bf16),
        pltpu.VMEM((tiles, 3 * chans, atoms), bf16),
        pltpu.VMEM((tiles, 8 * BLOCK, atoms), bf16),
        pltpu.VMEM((blocks, 8 * BLOCK, chans), f32),
        pltpu.VMEM((blocks, 8 * BLOCK, chans), bf16),
        pltpu.VMEM((blocks, BLOCK, chans), f32),
        pltpu.VMEM((blocks, chans, atoms // 2), bf16),
        pltpu.VMEM((high, atoms), f32),
        pltpu.VMEM((3, tiles, atoms), f32),
        pltpu.VMEM((8, tiles, atoms), f32),
        pltpu.VMEM((2, tiles, atoms), f32),
        pltpu.VMEM((tiles, nbasis, atoms), f32),
        pltpu.VMEM((tiles, nbasis, atoms), f32),
        pltpu.VMEM((tiles, hid_n, atoms), f32),
        pltpu.VMEM((tiles, hid_n, atoms), bf16),
        pltpu.VMEM((8, tiles, atoms), f32),
        pltpu.VMEM((2, tiles, atoms), f32),
        pltpu.VMEM((3 * chans, hid_n), bf16),
        pltpu.VMEM((atoms, atoms), bf16),
    ]
    picked, near = pl.pallas_call(
        early_kernel,
        out_shape=[shape((tiles, chans, atoms), bf16), shape((3, tiles, atoms), f32)],
        in_specs=smem + vmem(3),
        out_specs=vmem(2),
        scratch_shapes=[
            pltpu.SMEM((tiles,), jnp.int32),
            pltpu.VMEM((high, 2 * atoms), bf16),
            pltpu.VMEM((atoms, atoms), bf16),
        ],
        compiler_params=small,
        cost_estimate=pl.CostEstimate(flops=2_000_000_000, bytes_accessed=6_000_000, transcendentals=0),
        name="early",
    )(depth, own, from_a, nbt)
    energies, dg, self_grad, ghost_b = pl.pallas_call(
        main_kernel,
        out_shape=[
            shape((1, atoms), f32),
            shape((tiles, high, atoms), bf16),
            shape((8, atoms), f32),
            shape((ghosts + EXTRA, chans), bf16),
        ],
        in_specs=smem + vmem(11),
        out_specs=vmem(4),
        scratch_shapes=scratch,
        compiler_params=params,
        name="interact",
    )(
        depth,
        picked,
        near,
        from_b,
        nbt,
        self_pos,
        rank,
        edir,
        radial_in,
        radial_out,
        product_weight,
        table,
    )
    back_b = swapped(ghost_b, "dom", 1)
    ghost_a, dpos, grad_own, picks = pl.pallas_call(
        late_kernel,
        out_shape=[
            shape((ghosts + EXTRA, chans), bf16),
            shape((8, atoms), f32),
            shape((atoms, chans), f32),
            shape((2, atoms, ghosts), bf16),
        ],
        in_specs=smem + smem + vmem(5),
        out_specs=vmem(4),
        scratch_shapes=[
            pltpu.SMEM((tiles,), jnp.int32),
            pltpu.VMEM((high, 2 * atoms), f32),
            pltpu.VMEM((atoms, atoms), bf16),
        ],
        compiler_params=small,
        cost_estimate=pl.CostEstimate(flops=2_000_000_000, bytes_accessed=6_000_000, transcendentals=0),
        name="late",
    )(depth, odd, dg, nbt, self_grad, table, mix_weight)
    back_a = swapped(ghost_a, "dom", 0)
    forces, feature_grad = pl.pallas_call(
        final_kernel,
        out_shape=[shape((3, atoms), f32), shape((atoms, chans), f32)],
        in_specs=vmem(6),
        out_specs=vmem(2),
        compiler_params=small,
        name="finish",
    )(grad_own, dpos, back_a, back_b, picks, mix_weight)
    return (energies.reshape(atoms), forces, feature_grad)


def solution(mesh):
    placed = (
        P(None, ("groups", "dom")),
        P(("groups", "dom"), None),
        P(("groups", "dom")),
        P(("groups", "dom"), None),
        P(("groups", "dom")),
        P(("groups", "dom")),
        P(("groups", "dom")),
        P(),
        P(),
        P(),
        P(),
        P(),
        P(),
    )
    return jax.shard_map(
        per_device,
        mesh=mesh,
        in_specs=placed,
        out_specs=(P(("groups", "dom")), P(None, ("groups", "dom")), P(("groups", "dom"), None)),
        check_vma=False,
    )
```

```python
import functools

import jax
import jax.numpy as jnp
from jax import lax
from jax.experimental import pallas as pl
from jax.experimental.pallas import tpu as pltpu
from jax.sharding import PartitionSpec as P

cut_radius = 5.0
sqrt_three = 1.7320508075688772
pi = 3.141592653589793

f32 = jnp.float32
bf16 = jnp.bfloat16

BLOCK = 32
DEPTH = 8
EXTRA = 16
PACK_LIMIT = 63 * 1024 * 1024
LAG = 4
LAG_B = 1
UNROLL_G = 8
UNROLL_H = 8
UNROLL_F = 8
UNROLL_B = 8
UNROLL_E = 8
UNROLL_D = 8
UNROLL_S = 8


def swapped(value, axis, odd):
    count = lax.axis_size(axis)
    partner = [((i + odd) ^ 1) - odd for i in range(count)]
    pairs = [(i, j) for i, j in enumerate(partner) if 0 <= j < count]
    return lax.ppermute(value, axis, pairs)


def iota(shape, dim):
    return lax.broadcasted_iota(jnp.int32, shape, dim)


def dot(a, b, ca=1, cb=0):
    return lax.dot_general(a, b, (((ca,), (cb,)), ((), ())), preferred_element_type=f32)


def parts(value, count):
    out = []
    for _ in range(count):
        head = value.astype(bf16).astype(f32)
        out.append(head)
        value = value - head
    return out


def stack_rows(rows, height):
    lanes = rows[0].shape[1]
    at = iota((height, lanes), 0)
    out = jnp.zeros((height, lanes), f32)
    for idx, row in enumerate(rows):
        out = jnp.where(at == idx, jnp.broadcast_to(row, (height, lanes)), out)
    return out


def sigmoid(x):
    return 1.0 / (1.0 + jnp.exp(-x))


POS, COUNT, SPECIES, READ, LEFT, RIGHT, GAIN = 0, 3, 4, 5, 6, 7, 8


def list_rows(small_ref, odd, ghosts):
    left, right = small_ref[LEFT : LEFT + 1, :ghosts], small_ref[RIGHT : RIGHT + 1, :ghosts]
    return jnp.where(odd, left, right), jnp.where(odd, right, left)


def gain_weight(small_ref):
    return small_ref[GAIN:, :] * small_ref[READ : READ + 1, :]


def pack_kernel(
    odd_ref,
    pos_hbm,
    cnt_hbm,
    spec_hbm,
    read_hbm,
    sl_hbm,
    sr_hbm,
    gain_hbm,
    feat_hbm,
    mix_hbm,
    a_ref,
    b_ref,
    small_ref,
    pos,
    cnt,
    spec,
    read,
    sl,
    sr,
    gain,
    feat,
    mix,
    sems,
):
    hbm = (feat_hbm, mix_hbm, pos_hbm, sl_hbm, sr_hbm, cnt_hbm, spec_hbm, read_hbm, gain_hbm)
    here = (feat, mix, pos, sl, sr, cnt, spec, read, gain)
    copies = [pltpu.make_async_copy(src, dst, sems.at[k]) for k, (src, dst) in enumerate(zip(hbm, here))]
    for copy in copies:
        copy.start()
    for copy in copies:
        copy.wait()
    small_ref[POS : POS + 3, :] = pos[...]
    small_ref[COUNT : COUNT + 1, :] = cnt[...].astype(f32)
    small_ref[SPECIES : SPECIES + 1, :] = spec[...].astype(f32)
    small_ref[READ : READ + 1, :] = read[...]
    for at, lst in ((LEFT, sl), (RIGHT, sr)):
        small_ref[at : at + 1, :] = jnp.full((1, small_ref.shape[1]), -1.0, f32)
        small_ref[at : at + 1, : lst.shape[1]] = lst[...].astype(f32)
    small_ref[GAIN:, :] = gain[...]
    atoms, chans = feat.shape
    ghosts = a_ref.shape[0] - EXTRA
    mixed = dot(feat[...], mix[...]).astype(bf16)
    rows = [p[d : d + 1, :] for p in parts(small_ref[POS : POS + 3, :], 3) for d in range(3)]
    rows = stack_rows(rows, EXTRA).astype(bf16)
    for lst, out in zip(list_rows(small_ref, odd_ref[0] == 1, ghosts), (a_ref, b_ref)):
        pick = (iota((atoms, ghosts), 0).astype(f32) == lst).astype(f32).astype(bf16)
        out[:ghosts, :] = dot(pick, mixed, 0, 0).astype(bf16)
        out[ghosts:, :ghosts] = dot(rows, pick).astype(bf16)
        out[ghosts:, ghosts:] = jnp.zeros((EXTRA, chans - ghosts), bf16)


def sort_kernel(
    ghosts,
    odd_ref,
    depth_ref,
    small_ref,
    nb_ref,
    feat,
    mix,
    nbt_ref,
    self_ref,
    rank_ref,
    own_ref,
    edir_ref,
    list_ref,
):
    slots, atoms = nb_ref.shape
    chans = feat.shape[1]
    list_tiles(depth_ref, list_ref, atoms // BLOCK, slots // DEPTH)
    cnt_row = small_ref[COUNT : COUNT + 1, :]
    up, across = iota((atoms, atoms), 0), iota((atoms, atoms), 1)
    cnt_col = jnp.sum(jnp.where(up == across, cnt_row, 0.0), axis=1, keepdims=True)
    ahead_row = (cnt_col > cnt_row) | ((cnt_col == cnt_row) & (up < across))
    ahead_col = (cnt_row > cnt_col) | ((cnt_row == cnt_col) & (across < up))
    rank_row = jnp.sum(ahead_row.astype(f32), axis=0, keepdims=True)
    rank_col = jnp.sum(ahead_col.astype(f32), axis=1, keepdims=True)
    rank_ref[...] = rank_row
    nb = nb_ref[...]
    odd = odd_ref[0]
    to_left = jnp.where(odd == 1, 0, atoms)
    to_right = jnp.where(odd == 1, atoms - ghosts, -ghosts)
    nb = jnp.where(nb >= atoms + ghosts, nb + to_right, jnp.where(nb >= atoms, nb + to_left, nb))
    nbt = nb.astype(f32)
    high = jnp.floor(nbt * (1.0 / 256.0))
    low = nbt - high * 256.0
    rows = [p[d : d + 1, :] for p in parts(small_ref[POS : POS + 3, :], 3) for d in range(3)]
    left = jnp.concatenate([high, low, stack_rows(rows + [cnt_row], EXTRA)], axis=0).astype(bf16)
    lane_atom = (across % BLOCK).astype(f32)
    lane_slot = iota((slots, atoms), 1) // BLOCK
    mine = lane_slot == (iota((slots, atoms), 0) % DEPTH)
    depth_at = iota((slots // DEPTH, atoms), 0) * DEPTH + iota((slots // DEPTH, atoms), 1) // BLOCK
    groups = slots // DEPTH
    for b in range(atoms // BLOCK):
        pick = (rank_col - float(b * BLOCK) == lane_atom).astype(f32).astype(bf16)
        got = dot(left, pick)
        ids = got[:slots] * 256.0 + got[slots : 2 * slots]
        tail = got[2 * slots :]
        ids = jnp.sum(jnp.where(mine, ids, 0.0).reshape(groups, DEPTH, atoms), axis=1)
        ids = jnp.where(depth_at.astype(f32) < tail[9:10], ids, -1.0)
        nbt_ref[b * groups : (b + 1) * groups, :] = ids
        self_ref[b] = tail[0:8] + tail[3:11] + tail[6:14]
    own_ref[:chans, :] = dot(mix[...], feat[...], 0, 1).astype(bf16)
    own_ref[chans:, :] = stack_rows(rows, EXTRA).astype(bf16)
    weight = gain_weight(small_ref)
    kinds = weight.shape[0]
    direct = jnp.zeros((kinds, atoms), f32)
    for p in parts(weight, 3):
        direct += dot(p.astype(bf16), feat[...], 1, 1)
    mine = iota((kinds, atoms), 0).astype(f32) == small_ref[SPECIES : SPECIES + 1, :]
    edir_ref[...] = jnp.sum(jnp.where(mine, direct, 0.0), axis=0, keepdims=True)


def list_tiles(depth_ref, list_ref, blocks, groups):
    def list_group(j, live):
        need = (depth_ref[j] + (BLOCK - 1)) // BLOCK

        def put(b, state):
            front, back = state
            is_live = b < need
            list_ref[jnp.where(is_live, front, back)] = b * groups + j
            step = is_live.astype(jnp.int32)
            return front + step, back - (1 - step)

        return lax.fori_loop(0, blocks, put, live)

    state = (jnp.int32(0), jnp.int32(blocks * groups - 1))
    live, _ = lax.fori_loop(0, groups, list_group, state)
    list_ref[blocks * groups] = live


def tile_loop(list_ref):
    live = list_ref[list_ref.shape[0] - 1]

    def over_tiles(body, unroll):
        def step(i, carry):
            body([list_ref[i * unroll + u] for u in range(unroll)])
            return carry

        lax.fori_loop(0, (live + (unroll - 1)) // unroll, step, 0)

    return over_tiles


def each(body):
    def bodies(tiles):
        for t in tiles:
            body(t)

    return bodies


def selection(ids, up, sections):
    one, zero = jnp.ones((), bf16), jnp.zeros((), bf16)
    pieces = []
    for s in sections:
        row = jnp.broadcast_to((ids - float(s * up.shape[0])).astype(bf16), up.shape)
        pieces.append(jnp.where(row == up, one, zero))
    return jnp.concatenate(pieces, axis=0)


def fill_section(table, low, rec_ref, chans, atoms):
    ghosts = rec_ref.shape[0] - EXTRA
    table[:chans, low : low + ghosts] = jnp.transpose(rec_ref[:ghosts, :].astype(f32)).astype(bf16)
    table[chans:, low : low + ghosts] = rec_ref[ghosts:, :ghosts]
    table[:, low + ghosts : low + atoms] = jnp.zeros((chans + EXTRA, atoms - ghosts), bf16)


def early_kernel(list_ref, own_ref, arec_ref, nbt_ref, g_ref, near_ref, table, rank_up):
    high, atoms = own_ref.shape
    chans = high - EXTRA
    tiles = nbt_ref.shape[0]
    blocks = atoms // BLOCK
    over_tiles = tile_loop(list_ref)
    rank_up[...] = iota((atoms, atoms), 0).astype(f32).astype(bf16)
    table[:, :atoms] = own_ref[...]
    fill_section(table, atoms, arec_ref, chans, atoms)

    def gather(t):
        got = dot(table[...], selection(nbt_ref[pl.ds(t, 1), :], rank_up[...], (0, 1)))
        g_ref[t] = got[:chans].astype(bf16)
        tail = got[chans:]
        near = tail[0:8] + tail[3:11] + tail[6:14]
        for d in range(3):
            near_ref[d, pl.ds(t, 1), :] = near[d : d + 1]

    over_tiles(each(gather), UNROLL_G)


def main_kernel(
    list_ref,
    gpart_ref,
    near_ref,
    brec_ref,
    nbt_ref,
    self_ref,
    rank_ref,
    edir_ref,
    rin_ref,
    rout_ref,
    pw_ref,
    small_ref,
    en_ref,
    dgbuf,
    spos_ref,
    gb_ref,
    table,
    drbuf,
    gbuf,
    rbuf,
    ybuf,
    abuf,
    dabuf,
    zbuf,
    dfold,
    acc,
    dvec,
    harm,
    radc,
    sinb,
    cosb,
    dsil,
    hidb,
    dharm,
    dbas,
    wout_t,
    rank_up,
):
    tiles, chans, atoms = gpart_ref.shape
    high = chans + EXTRA
    blocks = atoms // BLOCK
    groups = tiles // blocks
    hid_n = rout_ref.shape[0]
    nbasis = rin_ref.shape[0]
    scale = 1.0 / (groups * DEPTH)

    over_tiles = tile_loop(list_ref)

    ghosts = brec_ref.shape[0] - EXTRA
    fill_section(table, 0, brec_ref, chans, atoms)
    rank_up[...] = iota((atoms, atoms), 0).astype(f32).astype(bf16)
    wout_t[...] = jnp.transpose(rout_ref[...].astype(f32)).astype(bf16)
    dvec[...] = jnp.zeros(dvec.shape, f32)
    dharm[...] = jnp.zeros(dharm.shape, f32)
    dbas[...] = jnp.zeros(dbas.shape, f32)
    abuf[...] = jnp.zeros(abuf.shape, f32)
    zbuf[...] = jnp.zeros(zbuf.shape, f32)
    acc[...] = jnp.zeros(acc.shape, f32)
    def gather(t):
        got = dot(table[...], selection(nbt_ref[pl.ds(t, 1), :], rank_up[...], (2,)))
        gbuf[t] = gpart_ref[t] + got[:chans].astype(bf16)
        tail = got[chans:]
        near = tail[0:8] + tail[3:11] + tail[6:14]
        away = near - self_ref[t // groups]
        for d in range(3):
            dvec[d, pl.ds(t, 1), :] = near_ref[d, pl.ds(t, 1), :] + away[d : d + 1]

    over_tiles(each(gather), UNROLL_G)

    dx, dy, dz = dvec[0], dvec[1], dvec[2]
    r2 = dx * dx + dy * dy + dz * dz
    dist = jnp.sqrt(r2 + 0.25)
    inv = 1.0 / dist
    env = jnp.maximum(1.0 - r2 * (1.0 / (cut_radius * cut_radius)), 0.0)
    env2 = env * env
    ux, uy, uz = dx * inv, dy * inv, dz * inv
    radc[0] = dist * (0.5 / cut_radius)
    radc[1] = env2 * inv
    harm[0] = ux
    harm[1] = uy
    harm[2] = uz
    harm[3] = sqrt_three * ux * uy
    harm[4] = sqrt_three * uy * uz
    harm[5] = 0.5 * (3.0 * uz * uz - (ux * ux + uy * uy + uz * uz))
    harm[6] = sqrt_three * ux * uz
    harm[7] = 0.5 * sqrt_three * (ux * ux - uy * uy)

    lanes = atoms
    same = iota((BLOCK, lanes), 0) == (iota((BLOCK, lanes), 1) % BLOCK)
    seg = jnp.where(same, 1.0, 0.0).astype(bf16)
    rin_hi, rin_lo = parts(rin_ref[...], 2)
    rin_t = jnp.concatenate([rin_hi, rin_lo, rin_hi, jnp.zeros_like(rin_hi)], axis=0).astype(bf16)
    rin_b = jnp.concatenate([rin_hi, rin_lo], axis=0).astype(bf16)
    order = (iota((nbasis, lanes), 0) + 1).astype(f32)

    def hidden(t):
        turn = order * radc[0, pl.ds(t, 1), :]
        half = pi * (turn - jnp.floor(turn + 0.5))
        sq = half * half
        s = half * (
            1.0
            + sq
            * (
                -1.0 / 6
                + sq * (1.0 / 120 + sq * (-1.0 / 5040 + sq * (1.0 / 362880 + sq * (-1.0 / 39916800))))
            )
        )
        c = 1.0 + sq * (
            -0.5
            + sq
            * (
                1.0 / 24
                + sq * (-1.0 / 720 + sq * (1.0 / 40320 + sq * (-1.0 / 3628800 + sq * (1.0 / 479001600))))
            )
        )
        sn, cs = 2.0 * s * c, 1.0 - 2.0 * s * s
        sinb[t] = sn
        cosb[t] = cs * order
        basis = sn * radc[1, pl.ds(t, 1), :]
        b_hi, b_lo = parts(basis, 2)
        b_all = jnp.concatenate([b_hi, b_hi, b_lo, jnp.zeros_like(b_hi)], axis=0).astype(bf16)
        pre = dot(rin_t, b_all, 0, 0)
        sig = sigmoid(pre)
        dsil[t] = sig * (1.0 + pre * (1.0 - sig))
        hidb[t] = (pre * sig).astype(bf16)
        for m in range(8):
            row = jnp.broadcast_to(harm[m, pl.ds(t, 1), :], (BLOCK, lanes))
            ybuf[t, m * BLOCK : (m + 1) * BLOCK, :] = jnp.where(same, row, 0.0).astype(bf16)

    ends = (0, 3, 8)
    seg_half = seg[:, : lanes // 2]

    def radial_part(t, l):
        value = dot(wout_t[l * chans : (l + 1) * chans, :], hidb[t]).astype(bf16)
        rbuf[t, l * chans : (l + 1) * chans, :] = value
        return value * gbuf[t]

    def alpha_part(t, l, term):
        b = t // groups
        if l == 0:
            zbuf[b] += dot(seg_half, term[:, : lanes // 2] + term[:, lanes // 2 :], 1, 1)
        else:
            lo, hi = ends[l - 1] * BLOCK, ends[l] * BLOCK
            abuf[b, lo:hi, :] += dot(ybuf[t, lo:hi, :], term, 1, 1)

    def forward(tiles):
        waiting = []
        for t in tiles:
            for l in range(3):
                waiting.append((t, l, radial_part(t, l)))
                if len(waiting) > LAG:
                    alpha_part(*waiting.pop(0))
        for item in waiting:
            alpha_part(*item)

    over_tiles(each(hidden), UNROLL_H)
    over_tiles(forward, UNROLL_F)

    def alpha(lm):
        return abuf[:, (lm - 1) * BLOCK : lm * BLOCK, :].reshape(atoms, chans) * scale

    seg_half = seg[:, : lanes // 2]
    inv_l = [zbuf[...].reshape(atoms, chans) * scale]
    for ms in (range(1, 4), range(4, 9)):
        total = None
        for lm in ms:
            a = alpha(lm)
            total = a * a if total is None else total + a * a
        inv_l.append(total)
    p = None
    for l in range(3):
        term = dot(inv_l[l].astype(bf16), pw_ref[l * chans : (l + 1) * chans, :])
        p = term if p is None else p + term
    sig = sigmoid(p)
    read = small_ref[READ : READ + 1, :]
    e_col = jnp.sum(p * sig * read, axis=1, keepdims=True)
    place = rank_ref[...] == iota((atoms, atoms), 0).astype(f32)
    en_ref[...] = (
        jnp.sum(jnp.where(place, jnp.broadcast_to(e_col, (atoms, atoms)), 0.0), axis=0, keepdims=True)
        + edir_ref[...]
    )
    dp = (read * sig * (1.0 + p * (1.0 - sig))).astype(bf16)
    for l, ms in enumerate((range(1), range(1, 4), range(4, 9))):
        dinv = dot(dp, pw_ref[l * chans : (l + 1) * chans, :], 1, 1) * scale
        if l == 0:
            dinv = dinv.astype(bf16)
            for b in range(blocks):
                dfold[b] = dot(dinv[b * BLOCK : (b + 1) * BLOCK, :], seg_half, 0, 0).astype(bf16)
        for lm in ms if l else ():
            da = 2.0 * alpha(lm) * dinv
            dabuf[:, (lm - 1) * BLOCK : lm * BLOCK, :] = da.reshape(blocks, BLOCK, chans).astype(bf16)

    def term_part(t, l):
        b = t // groups
        g = gbuf[t]
        radial = rbuf[t, l * chans : (l + 1) * chans, :]
        if l == 0:
            half = dfold[b]
            dterm = jnp.concatenate([half, half], axis=1)
        else:
            lo, hi = ends[l - 1] * BLOCK, ends[l] * BLOCK
            da = dabuf[b, lo:hi, :]
            dterm = dot(da, ybuf[t, lo:hi, :], 0, 0).astype(bf16)
            cross = dot(da, radial * g)
            for m in range(2 * l + 1):
                mine = jnp.where(same, cross[m * BLOCK : (m + 1) * BLOCK, :], 0.0)
                dharm[ends[l - 1] + m, pl.ds(t, 1), :] = jnp.sum(mine, axis=0, keepdims=True)
        return dterm * g, dterm * radial

    def enter_part(t, terms):
        dg = terms[0][1] + terms[1][1] + terms[2][1]
        dgbuf[t, :chans, :] = dg
        dhid = None
        for l in range(3):
            part = dot(rout_ref[:, l * chans : (l + 1) * chans], terms[l][0])
            dhid = part if dhid is None else dhid + part
        hidb[t] = (dhid * dsil[t]).astype(bf16)

    def backward(tiles):
        waiting = []
        for t in tiles:
            waiting.append((t, [term_part(t, l) for l in range(3)]))
            if len(waiting) > LAG_B:
                enter_part(*waiting.pop(0))
        for item in waiting:
            enter_part(*item)

    def dhidden(t):
        both = dot(rin_b, hidb[t])
        dbasis = both[:nbasis] + both[nbasis:]
        dbas[0, pl.ds(t, 1), :] = jnp.sum(dbasis * sinb[t], axis=0, keepdims=True)
        dbas[1, pl.ds(t, 1), :] = jnp.sum(dbasis * cosb[t], axis=0, keepdims=True)

    over_tiles(backward, UNROLL_B)
    over_tiles(each(dhidden), UNROLL_D)

    dx, dy, dz = dvec[0], dvec[1], dvec[2]
    r2 = dx * dx + dy * dy + dz * dz
    inv = 1.0 / jnp.sqrt(r2 + 0.25)
    env = jnp.maximum(1.0 - r2 * (1.0 / (cut_radius * cut_radius)), 0.0)
    env2 = env * env
    ux, uy, uz = harm[0], harm[1], harm[2]
    gx = dharm[0] + sqrt_three * (uy * dharm[3] + uz * dharm[6] + ux * dharm[7]) - ux * dharm[5]
    gy = dharm[1] + sqrt_three * (ux * dharm[3] + uz * dharm[4] - uy * dharm[7]) - uy * dharm[5]
    gz = dharm[2] + sqrt_three * (uy * dharm[4] + ux * dharm[6]) + 2.0 * uz * dharm[5]
    dinv = dbas[0] * env2 + gx * dx + gy * dy + gz * dz
    ddist = radc[1] * (pi / cut_radius) * dbas[1] - inv * inv * dinv
    dr2 = 0.5 * inv * ddist - dbas[0] * inv * env * (2.0 / (cut_radius * cut_radius))
    slope = []
    for d, (grad, delta) in enumerate(((gx, dx), (gy, dy), (gz, dz))):
        value = grad * inv + 2.0 * delta * dr2
        slope.append(value)
        dvec[d] = value

    self_rows = []
    lane_block = iota((blocks, lanes), 1) // BLOCK
    for value in slope:
        folded = jnp.sum(value.reshape(blocks, groups, lanes), axis=1)
        by = lanes // 2
        while by >= BLOCK:
            folded = folded + pltpu.roll(folded, by, 1)
            by //= 2
        self_rows.append(
            jnp.sum(jnp.where(lane_block == iota((blocks, lanes), 0), folded, 0.0), axis=0, keepdims=True)
        )
    split = [parts(row, 3) for row in self_rows]
    rows = [split[d][k] for k in range(3) for d in range(3)]
    place = jnp.where(rank_ref[...] == iota((atoms, atoms), 0).astype(f32), 1.0, 0.0).astype(bf16)
    back = dot(stack_rows(rows, EXTRA).astype(bf16), place)
    spos_ref[...] = back[0:8] + back[3:11] + back[6:14]

    def scatter(t):
        rows = []
        for d in range(3):
            rows.append(parts(dvec[d, pl.ds(t, 1), :], 2))
        rows = [rows[d][k] for k in range(2) for d in range(3)]
        dgbuf[t, chans:, :] = stack_rows(rows, EXTRA).astype(bf16)
        acc[...] += dot(dgbuf[t], selection(nbt_ref[pl.ds(t, 1), :], rank_up[...], (2,)), 1, 1)

    over_tiles(each(scatter), UNROLL_S)

    pack_adjoint(acc, 0, gb_ref, chans, atoms)


def pack_adjoint(acc, low, out, chans, atoms):
    ghosts = out.shape[0] - EXTRA
    out[:ghosts, :] = jnp.transpose(acc[:chans, low : low + ghosts]).astype(bf16)
    tail = acc[chans:, low : low + atoms]
    pieces = parts(tail[0:8] + tail[3:11], 2)
    rows = [q[d : d + 1] for q in pieces for d in range(3)]
    out[ghosts:, :] = stack_rows(rows, EXTRA).astype(bf16)


def late_kernel(
    list_ref, odd_ref, dg_ref, nbt_ref, spos_ref, small_ref, mix_ref, ga_ref, dpos_ref, grad_ref, pick_ref, acc, rank_up
):
    _, high, atoms = dg_ref.shape
    chans = high - EXTRA
    ghosts = pick_ref.shape[2]
    rank_up[...] = iota(rank_up.shape, 0).astype(f32).astype(bf16)
    acc[...] = jnp.zeros(acc.shape, f32)

    def scatter(t):
        chosen = selection(nbt_ref[pl.ds(t, 1), :], rank_up[...], (0, 1))
        acc[...] += dot(dg_ref[t], chosen, 1, 1)

    over_tiles = tile_loop(list_ref)
    over_tiles(each(scatter), UNROLL_S)
    pack_adjoint(acc, atoms, ga_ref, chans, atoms)
    tail = acc[chans:, :atoms]
    dpos_ref[...] = tail[0:8] + tail[3:11] - spos_ref[...]
    for k, lst in enumerate(list_rows(small_ref, odd_ref[0] == 1, ghosts)):
        pick_ref[k] = (iota((atoms, ghosts), 0).astype(f32) == lst).astype(f32).astype(bf16)
    weight = gain_weight(small_ref)
    kinds = weight.shape[0]
    chosen = (iota((kinds, atoms), 0).astype(f32) == small_ref[SPECIES : SPECIES + 1, :]).astype(f32)
    grad = None
    for q in parts(weight, 3):
        part = dot(chosen.astype(bf16), q.astype(bf16), 0, 0)
        grad = part if grad is None else grad + part
    for q in parts(acc[:chans, :atoms], 2):
        grad += dot(q.astype(bf16), mix_ref[...], 0, 1)
    grad_ref[...] = grad


def final_kernel(own_ref, dpos_ref, a_ref, b_ref, pick_ref, mix_ref, force_ref, grad_ref):
    ghosts = pick_ref.shape[2]
    total, tail = None, None
    for k, rec in enumerate((a_ref, b_ref)):
        pick = pick_ref[k]
        part, last = dot(rec[:ghosts, :], pick, 0, 1), dot(rec[ghosts:, :ghosts], pick, 1, 1)
        total = part if total is None else total + part
        tail = last if tail is None else tail + last
    pos = dpos_ref[...] + tail[0:8] + tail[3:11]
    force_ref[...] = -pos[:3]
    grad = own_ref[...]
    for q in parts(total, 2):
        grad += dot(q.astype(bf16), mix_ref[...], 0, 1)
    grad_ref[...] = grad


def vmem(count):
    return [pl.BlockSpec(memory_space=pltpu.VMEM)] * count


def per_device(
    positions,
    features,
    species,
    neighbours,
    near_count,
    send_left,
    send_right,
    radial_in,
    radial_out,
    mix_weight,
    product_weight,
    species_gain,
    readout,
):
    atoms, chans = features.shape
    ghosts = send_left.shape[0]
    slots = neighbours.shape[1]
    nbasis, hid_n = radial_in.shape
    blocks, groups = atoms // BLOCK, slots // DEPTH
    tiles = blocks * groups
    high = chans + EXTRA
    rows = [row.reshape(1, atoms) for row in (near_count, species, readout)]
    lists = [row.reshape(1, ghosts) for row in (send_left, send_right)]
    inputs = [positions] + rows + lists + [species_gain, features, mix_weight]
    shape = jax.ShapeDtypeStruct
    params = pltpu.CompilerParams(vmem_limit_bytes=44 * 1024 * 1024)
    small = pltpu.CompilerParams(vmem_limit_bytes=16 * 1024 * 1024)

    odd = (lax.axis_index("dom") % 2).astype(jnp.int32).reshape(1)
    smem = [pl.BlockSpec(memory_space=pltpu.SMEM)]
    to_a, to_b, table = pl.pallas_call(
        pack_kernel,
        out_shape=[shape((ghosts + EXTRA, chans), bf16)] * 2
        + [shape((GAIN + species_gain.shape[0], atoms), f32)],
        in_specs=smem + [pl.BlockSpec(memory_space=pltpu.HBM)] * 9,
        out_specs=vmem(3),
        scratch_shapes=[pltpu.VMEM(x.shape, x.dtype) for x in inputs] + [pltpu.SemaphoreType.DMA((9,))],
        compiler_params=pltpu.CompilerParams(vmem_limit_bytes=PACK_LIMIT),
        cost_estimate=pl.CostEstimate(flops=2_000_000_000, bytes_accessed=6_000_000, transcendentals=0),
        name="pack",
    )(odd, *inputs)
    from_a = swapped(to_a, "dom", 0)
    from_b = swapped(to_b, "dom", 1)

    depth = jnp.sum(
        (near_count[None, :] > DEPTH * jnp.arange(groups)[:, None]).astype(jnp.int32), axis=1
    ).astype(jnp.int32)
    nbt, self_pos, rank, own, edir, order = pl.pallas_call(
        functools.partial(sort_kernel, ghosts),
        out_shape=[
            shape((tiles, atoms), f32),
            shape((blocks, 8, atoms), f32),
            shape((1, atoms), f32),
            shape((high, atoms), bf16),
            shape((1, atoms), f32),
            shape((tiles + 1,), jnp.int32),
        ],
        in_specs=smem + smem + vmem(4),
        out_specs=vmem(5) + smem,
        compiler_params=small,
        cost_estimate=pl.CostEstimate(flops=200_000_000, bytes_accessed=2_000_000, transcendentals=0),
        name="sort",
    )(odd, depth, table, neighbours.T, features, mix_weight)
    scratch = [
        pltpu.VMEM((high, atoms), bf16),
        pltpu.VMEM((tiles, 3 * chans, atoms), bf16),
        pltpu.VMEM((tiles, chans, atoms), bf16),
        pltpu.VMEM((tiles, 3 * chans, atoms), bf16),
        pltpu.VMEM((tiles, 8 * BLOCK, atoms), bf16),
        pltpu.VMEM((blocks, 8 * BLOCK, chans), f32),
        pltpu.VMEM((blocks, 8 * BLOCK, chans), bf16),
        pltpu.VMEM((blocks, BLOCK, chans), f32),
        pltpu.VMEM((blocks, chans, atoms // 2), bf16),
        pltpu.VMEM((high, atoms), f32),
        pltpu.VMEM((3, tiles, atoms), f32),
        pltpu.VMEM((8, tiles, atoms), f32),
        pltpu.VMEM((2, tiles, atoms), f32),
        pltpu.VMEM((tiles, nbasis, atoms), f32),
        pltpu.VMEM((tiles, nbasis, atoms), f32),
        pltpu.VMEM((tiles, hid_n, atoms), f32),
        pltpu.VMEM((tiles, hid_n, atoms), bf16),
        pltpu.VMEM((8, tiles, atoms), f32),
        pltpu.VMEM((2, tiles, atoms), f32),
        pltpu.VMEM((3 * chans, hid_n), bf16),
        pltpu.VMEM((atoms, atoms), bf16),
    ]
    picked, near = pl.pallas_call(
        early_kernel,
        out_shape=[shape((tiles, chans, atoms), bf16), shape((3, tiles, atoms), f32)],
        in_specs=smem + vmem(3),
        out_specs=vmem(2),
        scratch_shapes=[
            pltpu.VMEM((high, 2 * atoms), bf16),
            pltpu.VMEM((atoms, atoms), bf16),
        ],
        compiler_params=small,
        cost_estimate=pl.CostEstimate(flops=2_000_000_000, bytes_accessed=6_000_000, transcendentals=0),
        name="early",
    )(order, own, from_a, nbt)
    energies, dg, self_grad, ghost_b = pl.pallas_call(
        main_kernel,
        out_shape=[
            shape((1, atoms), f32),
            shape((tiles, high, atoms), bf16),
            shape((8, atoms), f32),
            shape((ghosts + EXTRA, chans), bf16),
        ],
        in_specs=smem + vmem(11),
        out_specs=vmem(4),
        scratch_shapes=scratch,
        compiler_params=params,
        name="interact",
    )(
        order,
        picked,
        near,
        from_b,
        nbt,
        self_pos,
        rank,
        edir,
        radial_in,
        radial_out,
        product_weight,
        table,
    )
    back_b = swapped(ghost_b, "dom", 1)
    ghost_a, dpos, grad_own, picks = pl.pallas_call(
        late_kernel,
        out_shape=[
            shape((ghosts + EXTRA, chans), bf16),
            shape((8, atoms), f32),
            shape((atoms, chans), f32),
            shape((2, atoms, ghosts), bf16),
        ],
        in_specs=smem + smem + vmem(5),
        out_specs=vmem(4),
        scratch_shapes=[pltpu.VMEM((high, 2 * atoms), f32), pltpu.VMEM((atoms, atoms), bf16)],
        compiler_params=small,
        cost_estimate=pl.CostEstimate(flops=2_000_000_000, bytes_accessed=6_000_000, transcendentals=0),
        name="late",
    )(order, odd, dg, nbt, self_grad, table, mix_weight)
    back_a = swapped(ghost_a, "dom", 0)
    forces, feature_grad = pl.pallas_call(
        final_kernel,
        out_shape=[shape((3, atoms), f32), shape((atoms, chans), f32)],
        in_specs=vmem(6),
        out_specs=vmem(2),
        compiler_params=small,
        name="finish",
    )(grad_own, dpos, back_a, back_b, picks, mix_weight)
    return (energies.reshape(atoms), forces, feature_grad)


def solution(mesh):
    placed = (
        P(None, ("groups", "dom")),
        P(("groups", "dom"), None),
        P(("groups", "dom")),
        P(("groups", "dom"), None),
        P(("groups", "dom")),
        P(("groups", "dom")),
        P(("groups", "dom")),
        P(),
        P(),
        P(),
        P(),
        P(),
        P(),
    )
    return jax.shard_map(
        per_device,
        mesh=mesh,
        in_specs=placed,
        out_specs=(P(("groups", "dom")), P(None, ("groups", "dom")), P(("groups", "dom"), None)),
        check_vma=False,
    )
```

```python
import functools

import jax
import jax.numpy as jnp
from jax import lax
from jax.experimental import pallas as pl
from jax.experimental.pallas import tpu as pltpu
from jax.sharding import PartitionSpec as P

cut_radius = 5.0
sqrt_three = 1.7320508075688772
pi = 3.141592653589793

f32 = jnp.float32
bf16 = jnp.bfloat16

BLOCK = 32
DEPTH = 8
EXTRA = 16
PACK_LIMIT = 63 * 1024 * 1024
LAG = 4
LAG_B = 1
UNROLL_G = 8
UNROLL_H = 8
UNROLL_F = 8
UNROLL_B = 8
UNROLL_E = 8
UNROLL_D = 8
UNROLL_S = 8


def swapped(value, axis, odd):
    count = lax.axis_size(axis)
    partner = [((i + odd) ^ 1) - odd for i in range(count)]
    pairs = [(i, j) for i, j in enumerate(partner) if 0 <= j < count]
    return lax.ppermute(value, axis, pairs)


def iota(shape, dim):
    return lax.broadcasted_iota(jnp.int32, shape, dim)


def dot(a, b, ca=1, cb=0):
    return lax.dot_general(a, b, (((ca,), (cb,)), ((), ())), preferred_element_type=f32)


def parts(value, count):
    out = []
    for _ in range(count):
        head = value.astype(bf16).astype(f32)
        out.append(head)
        value = value - head
    return out


def stack_rows(rows, height):
    lanes = rows[0].shape[1]
    at = iota((height, lanes), 0)
    out = jnp.zeros((height, lanes), f32)
    for idx, row in enumerate(rows):
        out = jnp.where(at == idx, jnp.broadcast_to(row, (height, lanes)), out)
    return out


def sigmoid(x):
    return 1.0 / (1.0 + jnp.exp(-x))


POS, COUNT, SPECIES, READ, LEFT, RIGHT, GAIN = 0, 3, 4, 5, 6, 7, 8


def list_rows(small_ref, odd, ghosts):
    left, right = small_ref[LEFT : LEFT + 1, :ghosts], small_ref[RIGHT : RIGHT + 1, :ghosts]
    return jnp.where(odd, left, right), jnp.where(odd, right, left)


def gain_weight(small_ref):
    return small_ref[GAIN:, :] * small_ref[READ : READ + 1, :]


def pack_kernel(
    odd_ref,
    pos_hbm,
    cnt_hbm,
    spec_hbm,
    read_hbm,
    sl_hbm,
    sr_hbm,
    gain_hbm,
    feat_hbm,
    mix_hbm,
    a_ref,
    b_ref,
    small_ref,
    pos,
    cnt,
    spec,
    read,
    sl,
    sr,
    gain,
    feat,
    mix,
    sems,
):
    hbm = (feat_hbm, mix_hbm, pos_hbm, sl_hbm, sr_hbm, cnt_hbm, spec_hbm, read_hbm, gain_hbm)
    here = (feat, mix, pos, sl, sr, cnt, spec, read, gain)
    copies = [pltpu.make_async_copy(src, dst, sems.at[k]) for k, (src, dst) in enumerate(zip(hbm, here))]
    for copy in copies:
        copy.start()
    for copy in copies[:5]:
        copy.wait()
    small_ref[POS : POS + 3, :] = pos[...]
    for at, lst in ((LEFT, sl), (RIGHT, sr)):
        small_ref[at : at + 1, :] = jnp.full((1, small_ref.shape[1]), -1.0, f32)
        small_ref[at : at + 1, : lst.shape[1]] = lst[...].astype(f32)
    atoms, chans = feat.shape
    ghosts = a_ref.shape[0] - EXTRA
    mixed = dot(feat[...], mix[...]).astype(bf16)
    rows = [p[d : d + 1, :] for p in parts(small_ref[POS : POS + 3, :], 3) for d in range(3)]
    rows = stack_rows(rows, EXTRA).astype(bf16)
    for lst, out in zip(list_rows(small_ref, odd_ref[0] == 1, ghosts), (a_ref, b_ref)):
        pick = (iota((atoms, ghosts), 0).astype(f32) == lst).astype(f32).astype(bf16)
        out[:ghosts, :] = dot(pick, mixed, 0, 0).astype(bf16)
        out[ghosts:, :ghosts] = dot(rows, pick).astype(bf16)
        out[ghosts:, ghosts:] = jnp.zeros((EXTRA, chans - ghosts), bf16)
    for copy in copies[5:]:
        copy.wait()
    small_ref[COUNT : COUNT + 1, :] = cnt[...].astype(f32)
    small_ref[SPECIES : SPECIES + 1, :] = spec[...].astype(f32)
    small_ref[READ : READ + 1, :] = read[...]
    small_ref[GAIN:, :] = gain[...]


def sort_kernel(
    ghosts,
    odd_ref,
    depth_ref,
    pos_ref,
    cnt_ref,
    spec_ref,
    read_ref,
    gain_ref,
    nb_ref,
    feat,
    mix,
    nbt_ref,
    self_ref,
    rank_ref,
    own_ref,
    edir_ref,
    list_ref,
):
    slots, atoms = nb_ref.shape
    chans = feat.shape[1]
    list_tiles(depth_ref, list_ref, atoms // BLOCK, slots // DEPTH)
    cnt_row = cnt_ref[...].astype(f32)
    up, across = iota((atoms, atoms), 0), iota((atoms, atoms), 1)
    cnt_col = jnp.sum(jnp.where(up == across, cnt_row, 0.0), axis=1, keepdims=True)
    ahead_row = (cnt_col > cnt_row) | ((cnt_col == cnt_row) & (up < across))
    ahead_col = (cnt_row > cnt_col) | ((cnt_row == cnt_col) & (across < up))
    rank_row = jnp.sum(ahead_row.astype(f32), axis=0, keepdims=True)
    rank_col = jnp.sum(ahead_col.astype(f32), axis=1, keepdims=True)
    rank_ref[...] = rank_row
    nb = nb_ref[...]
    odd = odd_ref[0]
    to_left = jnp.where(odd == 1, 0, atoms)
    to_right = jnp.where(odd == 1, atoms - ghosts, -ghosts)
    nb = jnp.where(nb >= atoms + ghosts, nb + to_right, jnp.where(nb >= atoms, nb + to_left, nb))
    nbt = nb.astype(f32)
    high = jnp.floor(nbt * (1.0 / 256.0))
    low = nbt - high * 256.0
    rows = [p[d : d + 1, :] for p in parts(pos_ref[...], 3) for d in range(3)]
    left = jnp.concatenate([high, low, stack_rows(rows + [cnt_row], EXTRA)], axis=0).astype(bf16)
    lane_atom = (across % BLOCK).astype(f32)
    lane_slot = iota((slots, atoms), 1) // BLOCK
    mine = lane_slot == (iota((slots, atoms), 0) % DEPTH)
    depth_at = iota((slots // DEPTH, atoms), 0) * DEPTH + iota((slots // DEPTH, atoms), 1) // BLOCK
    groups = slots // DEPTH
    for b in range(atoms // BLOCK):
        pick = (rank_col - float(b * BLOCK) == lane_atom).astype(f32).astype(bf16)
        got = dot(left, pick)
        ids = got[:slots] * 256.0 + got[slots : 2 * slots]
        tail = got[2 * slots :]
        ids = jnp.sum(jnp.where(mine, ids, 0.0).reshape(groups, DEPTH, atoms), axis=1)
        ids = jnp.where(depth_at.astype(f32) < tail[9:10], ids, -1.0)
        nbt_ref[b * groups : (b + 1) * groups, :] = ids
        self_ref[b] = tail[0:8] + tail[3:11] + tail[6:14]
    own_ref[:chans, :] = dot(mix[...], feat[...], 0, 1).astype(bf16)
    own_ref[chans:, :] = stack_rows(rows, EXTRA).astype(bf16)
    weight = gain_ref[...] * read_ref[...]
    kinds = weight.shape[0]
    direct = jnp.zeros((kinds, atoms), f32)
    for p in parts(weight, 3):
        direct += dot(p.astype(bf16), feat[...], 1, 1)
    mine = iota((kinds, atoms), 0).astype(f32) == spec_ref[...].astype(f32)
    edir_ref[...] = jnp.sum(jnp.where(mine, direct, 0.0), axis=0, keepdims=True)


def list_tiles(depth_ref, list_ref, blocks, groups):
    def list_group(j, live):
        need = (depth_ref[j] + (BLOCK - 1)) // BLOCK

        def put(b, state):
            front, back = state
            is_live = b < need
            list_ref[jnp.where(is_live, front, back)] = b * groups + j
            step = is_live.astype(jnp.int32)
            return front + step, back - (1 - step)

        return lax.fori_loop(0, blocks, put, live)

    state = (jnp.int32(0), jnp.int32(blocks * groups - 1))
    live, _ = lax.fori_loop(0, groups, list_group, state)
    list_ref[blocks * groups] = live


def tile_loop(list_ref):
    live = list_ref[list_ref.shape[0] - 1]

    def over_tiles(body, unroll):
        def step(i, carry):
            body([list_ref[i * unroll + u] for u in range(unroll)])
            return carry

        lax.fori_loop(0, (live + (unroll - 1)) // unroll, step, 0)

    return over_tiles


def each(body):
    def bodies(tiles):
        for t in tiles:
            body(t)

    return bodies


def selection(ids, up, sections):
    one, zero = jnp.ones((), bf16), jnp.zeros((), bf16)
    pieces = []
    for s in sections:
        row = jnp.broadcast_to((ids - float(s * up.shape[0])).astype(bf16), up.shape)
        pieces.append(jnp.where(row == up, one, zero))
    return jnp.concatenate(pieces, axis=0)


def fill_section(table, low, rec_ref, chans, atoms):
    ghosts = rec_ref.shape[0] - EXTRA
    table[:chans, low : low + ghosts] = jnp.transpose(rec_ref[:ghosts, :].astype(f32)).astype(bf16)
    table[chans:, low : low + ghosts] = rec_ref[ghosts:, :ghosts]
    table[:, low + ghosts : low + atoms] = jnp.zeros((chans + EXTRA, atoms - ghosts), bf16)


def early_kernel(list_ref, own_ref, arec_ref, nbt_ref, g_ref, near_ref, table, rank_up):
    high, atoms = own_ref.shape
    chans = high - EXTRA
    tiles = nbt_ref.shape[0]
    blocks = atoms // BLOCK
    over_tiles = tile_loop(list_ref)
    rank_up[...] = iota((atoms, atoms), 0).astype(f32).astype(bf16)
    table[:, :atoms] = own_ref[...]
    fill_section(table, atoms, arec_ref, chans, atoms)

    def gather(t):
        got = dot(table[...], selection(nbt_ref[pl.ds(t, 1), :], rank_up[...], (0, 1)))
        g_ref[t] = got[:chans].astype(bf16)
        tail = got[chans:]
        near = tail[0:8] + tail[3:11] + tail[6:14]
        for d in range(3):
            near_ref[d, pl.ds(t, 1), :] = near[d : d + 1]

    over_tiles(each(gather), UNROLL_G)


def main_kernel(
    list_ref,
    gpart_ref,
    near_ref,
    brec_ref,
    nbt_ref,
    self_ref,
    rank_ref,
    edir_ref,
    rin_ref,
    rout_ref,
    pw_ref,
    small_ref,
    en_ref,
    dgbuf,
    spos_ref,
    gb_ref,
    table,
    drbuf,
    gbuf,
    rbuf,
    ybuf,
    abuf,
    dabuf,
    zbuf,
    dfold,
    acc,
    dvec,
    harm,
    radc,
    sinb,
    cosb,
    dsil,
    hidb,
    dharm,
    dbas,
    wout_t,
    rank_up,
):
    tiles, chans, atoms = gpart_ref.shape
    high = chans + EXTRA
    blocks = atoms // BLOCK
    groups = tiles // blocks
    hid_n = rout_ref.shape[0]
    nbasis = rin_ref.shape[0]
    scale = 1.0 / (groups * DEPTH)

    over_tiles = tile_loop(list_ref)

    ghosts = brec_ref.shape[0] - EXTRA
    fill_section(table, 0, brec_ref, chans, atoms)
    rank_up[...] = iota((atoms, atoms), 0).astype(f32).astype(bf16)
    wout_t[...] = jnp.transpose(rout_ref[...].astype(f32)).astype(bf16)
    dvec[...] = jnp.zeros(dvec.shape, f32)
    dharm[...] = jnp.zeros(dharm.shape, f32)
    dbas[...] = jnp.zeros(dbas.shape, f32)
    abuf[...] = jnp.zeros(abuf.shape, f32)
    zbuf[...] = jnp.zeros(zbuf.shape, f32)
    acc[...] = jnp.zeros(acc.shape, f32)
    def gather(t):
        got = dot(table[...], selection(nbt_ref[pl.ds(t, 1), :], rank_up[...], (2,)))
        gbuf[t] = gpart_ref[t] + got[:chans].astype(bf16)
        tail = got[chans:]
        near = tail[0:8] + tail[3:11] + tail[6:14]
        away = near - self_ref[t // groups]
        for d in range(3):
            dvec[d, pl.ds(t, 1), :] = near_ref[d, pl.ds(t, 1), :] + away[d : d + 1]

    over_tiles(each(gather), UNROLL_G)

    dx, dy, dz = dvec[0], dvec[1], dvec[2]
    r2 = dx * dx + dy * dy + dz * dz
    dist = jnp.sqrt(r2 + 0.25)
    inv = 1.0 / dist
    env = jnp.maximum(1.0 - r2 * (1.0 / (cut_radius * cut_radius)), 0.0)
    env2 = env * env
    ux, uy, uz = dx * inv, dy * inv, dz * inv
    radc[0] = dist * (0.5 / cut_radius)
    radc[1] = env2 * inv
    harm[0] = ux
    harm[1] = uy
    harm[2] = uz
    harm[3] = sqrt_three * ux * uy
    harm[4] = sqrt_three * uy * uz
    harm[5] = 0.5 * (3.0 * uz * uz - (ux * ux + uy * uy + uz * uz))
    harm[6] = sqrt_three * ux * uz
    harm[7] = 0.5 * sqrt_three * (ux * ux - uy * uy)

    lanes = atoms
    same = iota((BLOCK, lanes), 0) == (iota((BLOCK, lanes), 1) % BLOCK)
    seg = jnp.where(same, 1.0, 0.0).astype(bf16)
    rin_hi, rin_lo = parts(rin_ref[...], 2)
    rin_t = jnp.concatenate([rin_hi, rin_lo, rin_hi, jnp.zeros_like(rin_hi)], axis=0).astype(bf16)
    rin_b = jnp.concatenate([rin_hi, rin_lo], axis=0).astype(bf16)
    order = (iota((nbasis, lanes), 0) + 1).astype(f32)

    def hidden(t):
        turn = order * radc[0, pl.ds(t, 1), :]
        half = pi * (turn - jnp.floor(turn + 0.5))
        sq = half * half
        s = half * (
            1.0
            + sq
            * (
                -1.0 / 6
                + sq * (1.0 / 120 + sq * (-1.0 / 5040 + sq * (1.0 / 362880 + sq * (-1.0 / 39916800))))
            )
        )
        c = 1.0 + sq * (
            -0.5
            + sq
            * (
                1.0 / 24
                + sq * (-1.0 / 720 + sq * (1.0 / 40320 + sq * (-1.0 / 3628800 + sq * (1.0 / 479001600))))
            )
        )
        sn, cs = 2.0 * s * c, 1.0 - 2.0 * s * s
        sinb[t] = sn
        cosb[t] = cs * order
        basis = sn * radc[1, pl.ds(t, 1), :]
        b_hi, b_lo = parts(basis, 2)
        b_all = jnp.concatenate([b_hi, b_hi, b_lo, jnp.zeros_like(b_hi)], axis=0).astype(bf16)
        pre = dot(rin_t, b_all, 0, 0)
        sig = sigmoid(pre)
        dsil[t] = sig * (1.0 + pre * (1.0 - sig))
        hidb[t] = (pre * sig).astype(bf16)
        for m in range(8):
            row = jnp.broadcast_to(harm[m, pl.ds(t, 1), :].astype(bf16), (BLOCK, lanes))
            ybuf[t, m * BLOCK : (m + 1) * BLOCK, :] = seg * row

    ends = (0, 3, 8)
    seg_half = seg[:, : lanes // 2]

    def radial_part(t, l):
        value = dot(wout_t[l * chans : (l + 1) * chans, :], hidb[t]).astype(bf16)
        rbuf[t, l * chans : (l + 1) * chans, :] = value
        return value * gbuf[t]

    def alpha_part(t, l, term):
        b = t // groups
        if l == 0:
            zbuf[b] += dot(seg_half, term[:, : lanes // 2] + term[:, lanes // 2 :], 1, 1)
        else:
            lo, hi = ends[l - 1] * BLOCK, ends[l] * BLOCK
            abuf[b, lo:hi, :] += dot(ybuf[t, lo:hi, :], term, 1, 1)

    def forward(tiles):
        waiting = []
        for t in tiles:
            for l in range(3):
                waiting.append((t, l, radial_part(t, l)))
                if len(waiting) > LAG:
                    alpha_part(*waiting.pop(0))
        for item in waiting:
            alpha_part(*item)

    over_tiles(each(hidden), UNROLL_H)
    over_tiles(forward, UNROLL_F)

    def alpha(lm):
        return abuf[:, (lm - 1) * BLOCK : lm * BLOCK, :].reshape(atoms, chans) * scale

    seg_half = seg[:, : lanes // 2]
    inv_l = [zbuf[...].reshape(atoms, chans) * scale]
    for ms in (range(1, 4), range(4, 9)):
        total = None
        for lm in ms:
            a = alpha(lm)
            total = a * a if total is None else total + a * a
        inv_l.append(total)
    p = None
    for l in range(3):
        term = dot(inv_l[l].astype(bf16), pw_ref[l * chans : (l + 1) * chans, :])
        p = term if p is None else p + term
    sig = sigmoid(p)
    read = small_ref[READ : READ + 1, :]
    e_col = jnp.sum(p * sig * read, axis=1, keepdims=True)
    place = rank_ref[...] == iota((atoms, atoms), 0).astype(f32)
    en_ref[...] = (
        jnp.sum(jnp.where(place, jnp.broadcast_to(e_col, (atoms, atoms)), 0.0), axis=0, keepdims=True)
        + edir_ref[...]
    )
    dp = (read * sig * (1.0 + p * (1.0 - sig))).astype(bf16)
    for l, ms in enumerate((range(1), range(1, 4), range(4, 9))):
        dinv = dot(dp, pw_ref[l * chans : (l + 1) * chans, :], 1, 1) * scale
        if l == 0:
            dinv = dinv.astype(bf16)
            for b in range(blocks):
                dfold[b] = dot(dinv[b * BLOCK : (b + 1) * BLOCK, :], seg_half, 0, 0).astype(bf16)
        for lm in ms if l else ():
            da = 2.0 * alpha(lm) * dinv
            dabuf[:, (lm - 1) * BLOCK : lm * BLOCK, :] = da.reshape(blocks, BLOCK, chans).astype(bf16)

    def term_part(t, l):
        b = t // groups
        g = gbuf[t]
        radial = rbuf[t, l * chans : (l + 1) * chans, :]
        if l == 0:
            half = dfold[b]
            dterm = jnp.concatenate([half, half], axis=1)
        else:
            lo, hi = ends[l - 1] * BLOCK, ends[l] * BLOCK
            da = dabuf[b, lo:hi, :]
            dterm = dot(da, ybuf[t, lo:hi, :], 0, 0).astype(bf16)
            cross = dot(da, radial * g)
            for m in range(2 * l + 1):
                mine = jnp.where(same, cross[m * BLOCK : (m + 1) * BLOCK, :], 0.0)
                dharm[ends[l - 1] + m, pl.ds(t, 1), :] = jnp.sum(mine, axis=0, keepdims=True)
        return dterm * g, dterm * radial

    def enter_part(t, terms):
        dg = terms[0][1] + terms[1][1] + terms[2][1]
        dgbuf[t, :chans, :] = dg
        dhid = None
        for l in range(3):
            part = dot(rout_ref[:, l * chans : (l + 1) * chans], terms[l][0])
            dhid = part if dhid is None else dhid + part
        hidb[t] = (dhid * dsil[t]).astype(bf16)

    def backward(tiles):
        waiting = []
        for t in tiles:
            waiting.append((t, [term_part(t, l) for l in range(3)]))
            if len(waiting) > LAG_B:
                enter_part(*waiting.pop(0))
        for item in waiting:
            enter_part(*item)

    def dhidden(t):
        both = dot(rin_b, hidb[t])
        dbasis = both[:nbasis] + both[nbasis:]
        dbas[0, pl.ds(t, 1), :] = jnp.sum(dbasis * sinb[t], axis=0, keepdims=True)
        dbas[1, pl.ds(t, 1), :] = jnp.sum(dbasis * cosb[t], axis=0, keepdims=True)

    over_tiles(backward, UNROLL_B)
    over_tiles(each(dhidden), UNROLL_D)

    dx, dy, dz = dvec[0], dvec[1], dvec[2]
    r2 = dx * dx + dy * dy + dz * dz
    inv = 1.0 / jnp.sqrt(r2 + 0.25)
    env = jnp.maximum(1.0 - r2 * (1.0 / (cut_radius * cut_radius)), 0.0)
    env2 = env * env
    ux, uy, uz = harm[0], harm[1], harm[2]
    gx = dharm[0] + sqrt_three * (uy * dharm[3] + uz * dharm[6] + ux * dharm[7]) - ux * dharm[5]
    gy = dharm[1] + sqrt_three * (ux * dharm[3] + uz * dharm[4] - uy * dharm[7]) - uy * dharm[5]
    gz = dharm[2] + sqrt_three * (uy * dharm[4] + ux * dharm[6]) + 2.0 * uz * dharm[5]
    dinv = dbas[0] * env2 + gx * dx + gy * dy + gz * dz
    ddist = radc[1] * (pi / cut_radius) * dbas[1] - inv * inv * dinv
    dr2 = 0.5 * inv * ddist - dbas[0] * inv * env * (2.0 / (cut_radius * cut_radius))
    slope = []
    for d, (grad, delta) in enumerate(((gx, dx), (gy, dy), (gz, dz))):
        value = grad * inv + 2.0 * delta * dr2
        slope.append(value)
        dvec[d] = value

    self_rows = []
    lane_block = iota((blocks, lanes), 1) // BLOCK
    for value in slope:
        folded = jnp.sum(value.reshape(blocks, groups, lanes), axis=1)
        by = lanes // 2
        while by >= BLOCK:
            folded = folded + pltpu.roll(folded, by, 1)
            by //= 2
        self_rows.append(
            jnp.sum(jnp.where(lane_block == iota((blocks, lanes), 0), folded, 0.0), axis=0, keepdims=True)
        )
    split = [parts(row, 3) for row in self_rows]
    rows = [split[d][k] for k in range(3) for d in range(3)]
    place = jnp.where(rank_ref[...] == iota((atoms, atoms), 0).astype(f32), 1.0, 0.0).astype(bf16)
    back = dot(stack_rows(rows, EXTRA).astype(bf16), place)
    spos_ref[...] = back[0:8] + back[3:11] + back[6:14]

    def scatter(t):
        rows = []
        for d in range(3):
            rows.append(parts(dvec[d, pl.ds(t, 1), :], 2))
        rows = [rows[d][k] for k in range(2) for d in range(3)]
        dgbuf[t, chans:, :] = stack_rows(rows, EXTRA).astype(bf16)
        acc[...] += dot(dgbuf[t], selection(nbt_ref[pl.ds(t, 1), :], rank_up[...], (2,)), 1, 1)

    over_tiles(each(scatter), UNROLL_S)

    pack_adjoint(acc, 0, gb_ref, chans, atoms)


def pack_adjoint(acc, low, out, chans, atoms):
    ghosts = out.shape[0] - EXTRA
    out[:ghosts, :] = jnp.transpose(acc[:chans, low : low + ghosts]).astype(bf16)
    tail = acc[chans:, low : low + atoms]
    pieces = parts(tail[0:8] + tail[3:11], 2)
    rows = [q[d : d + 1] for q in pieces for d in range(3)]
    out[ghosts:, :] = stack_rows(rows, EXTRA).astype(bf16)


def late_kernel(
    list_ref, odd_ref, dg_ref, nbt_ref, spos_ref, small_ref, mix_ref, ga_ref, dpos_ref, grad_ref, pick_ref, acc, rank_up
):
    _, high, atoms = dg_ref.shape
    chans = high - EXTRA
    ghosts = pick_ref.shape[2]
    rank_up[...] = iota(rank_up.shape, 0).astype(f32).astype(bf16)
    acc[...] = jnp.zeros(acc.shape, f32)

    def scatter(t):
        chosen = selection(nbt_ref[pl.ds(t, 1), :], rank_up[...], (0, 1))
        acc[...] += dot(dg_ref[t], chosen, 1, 1)

    over_tiles = tile_loop(list_ref)
    over_tiles(each(scatter), UNROLL_S)
    pack_adjoint(acc, atoms, ga_ref, chans, atoms)
    tail = acc[chans:, :atoms]
    dpos_ref[...] = tail[0:8] + tail[3:11] - spos_ref[...]
    for k, lst in enumerate(list_rows(small_ref, odd_ref[0] == 1, ghosts)):
        pick_ref[k] = (iota((atoms, ghosts), 0).astype(f32) == lst).astype(f32).astype(bf16)
    weight = gain_weight(small_ref)
    kinds = weight.shape[0]
    chosen = (iota((kinds, atoms), 0).astype(f32) == small_ref[SPECIES : SPECIES + 1, :]).astype(f32)
    grad = None
    for q in parts(weight, 3):
        part = dot(chosen.astype(bf16), q.astype(bf16), 0, 0)
        grad = part if grad is None else grad + part
    for q in parts(acc[:chans, :atoms], 2):
        grad += dot(q.astype(bf16), mix_ref[...], 0, 1)
    grad_ref[...] = grad


def final_kernel(own_ref, dpos_ref, a_ref, b_ref, pick_ref, mix_ref, force_ref, grad_ref):
    ghosts = pick_ref.shape[2]
    total, tail = None, None
    for k, rec in enumerate((a_ref, b_ref)):
        pick = pick_ref[k]
        part, last = dot(rec[:ghosts, :], pick, 0, 1), dot(rec[ghosts:, :ghosts], pick, 1, 1)
        total = part if total is None else total + part
        tail = last if tail is None else tail + last
    pos = dpos_ref[...] + tail[0:8] + tail[3:11]
    force_ref[...] = -pos[:3]
    grad = own_ref[...]
    grad += dot(total.astype(bf16), mix_ref[...], 0, 1)
    grad_ref[...] = grad


def vmem(count):
    return [pl.BlockSpec(memory_space=pltpu.VMEM)] * count


def per_device(
    positions,
    features,
    species,
    neighbours,
    near_count,
    send_left,
    send_right,
    radial_in,
    radial_out,
    mix_weight,
    product_weight,
    species_gain,
    readout,
):
    atoms, chans = features.shape
    ghosts = send_left.shape[0]
    slots = neighbours.shape[1]
    nbasis, hid_n = radial_in.shape
    blocks, groups = atoms // BLOCK, slots // DEPTH
    tiles = blocks * groups
    high = chans + EXTRA
    rows = [row.reshape(1, atoms) for row in (near_count, species, readout)]
    lists = [row.reshape(1, ghosts) for row in (send_left, send_right)]
    inputs = [positions] + rows + lists + [species_gain, features, mix_weight]
    shape = jax.ShapeDtypeStruct
    params = pltpu.CompilerParams(vmem_limit_bytes=44 * 1024 * 1024)
    small = pltpu.CompilerParams(vmem_limit_bytes=16 * 1024 * 1024)

    odd = (lax.axis_index("dom") % 2).astype(jnp.int32).reshape(1)
    smem = [pl.BlockSpec(memory_space=pltpu.SMEM)]
    to_a, to_b, table = pl.pallas_call(
        pack_kernel,
        out_shape=[shape((ghosts + EXTRA, chans), bf16)] * 2
        + [shape((GAIN + species_gain.shape[0], atoms), f32)],
        in_specs=smem + [pl.BlockSpec(memory_space=pltpu.HBM)] * 9,
        out_specs=vmem(3),
        scratch_shapes=[pltpu.VMEM(x.shape, x.dtype) for x in inputs] + [pltpu.SemaphoreType.DMA((9,))],
        compiler_params=pltpu.CompilerParams(vmem_limit_bytes=PACK_LIMIT),
        cost_estimate=pl.CostEstimate(flops=2_000_000_000, bytes_accessed=6_000_000, transcendentals=0),
        name="pack",
    )(odd, *inputs)
    from_a = swapped(to_a, "dom", 0)
    from_b = swapped(to_b, "dom", 1)

    depth = jnp.sum(
        (near_count[None, :] > DEPTH * jnp.arange(groups)[:, None]).astype(jnp.int32), axis=1
    ).astype(jnp.int32)
    nbt, self_pos, rank, own, edir, order = pl.pallas_call(
        functools.partial(sort_kernel, ghosts),
        out_shape=[
            shape((tiles, atoms), f32),
            shape((blocks, 8, atoms), f32),
            shape((1, atoms), f32),
            shape((high, atoms), bf16),
            shape((1, atoms), f32),
            shape((tiles + 1,), jnp.int32),
        ],
        in_specs=smem + smem + vmem(8),
        out_specs=vmem(5) + smem,
        compiler_params=small,
        cost_estimate=pl.CostEstimate(flops=200_000_000, bytes_accessed=2_000_000, transcendentals=0),
        name="sort",
    )(odd, depth, positions, rows[0], rows[1], rows[2], species_gain, neighbours.T, features, mix_weight)
    scratch = [
        pltpu.VMEM((high, atoms), bf16),
        pltpu.VMEM((tiles, 3 * chans, atoms), bf16),
        pltpu.VMEM((tiles, chans, atoms), bf16),
        pltpu.VMEM((tiles, 3 * chans, atoms), bf16),
        pltpu.VMEM((tiles, 8 * BLOCK, atoms), bf16),
        pltpu.VMEM((blocks, 8 * BLOCK, chans), f32),
        pltpu.VMEM((blocks, 8 * BLOCK, chans), bf16),
        pltpu.VMEM((blocks, BLOCK, chans), f32),
        pltpu.VMEM((blocks, chans, atoms // 2), bf16),
        pltpu.VMEM((high, atoms), f32),
        pltpu.VMEM((3, tiles, atoms), f32),
        pltpu.VMEM((8, tiles, atoms), f32),
        pltpu.VMEM((2, tiles, atoms), f32),
        pltpu.VMEM((tiles, nbasis, atoms), f32),
        pltpu.VMEM((tiles, nbasis, atoms), f32),
        pltpu.VMEM((tiles, hid_n, atoms), f32),
        pltpu.VMEM((tiles, hid_n, atoms), bf16),
        pltpu.VMEM((8, tiles, atoms), f32),
        pltpu.VMEM((2, tiles, atoms), f32),
        pltpu.VMEM((3 * chans, hid_n), bf16),
        pltpu.VMEM((atoms, atoms), bf16),
    ]
    picked, near = pl.pallas_call(
        early_kernel,
        out_shape=[shape((tiles, chans, atoms), bf16), shape((3, tiles, atoms), f32)],
        in_specs=smem + vmem(3),
        out_specs=vmem(2),
        scratch_shapes=[
            pltpu.VMEM((high, 2 * atoms), bf16),
            pltpu.VMEM((atoms, atoms), bf16),
        ],
        compiler_params=small,
        cost_estimate=pl.CostEstimate(flops=2_000_000_000, bytes_accessed=6_000_000, transcendentals=0),
        name="early",
    )(order, own, from_a, nbt)
    energies, dg, self_grad, ghost_b = pl.pallas_call(
        main_kernel,
        out_shape=[
            shape((1, atoms), f32),
            shape((tiles, high, atoms), bf16),
            shape((8, atoms), f32),
            shape((ghosts + EXTRA, chans), bf16),
        ],
        in_specs=smem + vmem(11),
        out_specs=vmem(4),
        scratch_shapes=scratch,
        compiler_params=params,
        name="interact",
    )(
        order,
        picked,
        near,
        from_b,
        nbt,
        self_pos,
        rank,
        edir,
        radial_in,
        radial_out,
        product_weight,
        table,
    )
    back_b = swapped(ghost_b, "dom", 1)
    ghost_a, dpos, grad_own, picks = pl.pallas_call(
        late_kernel,
        out_shape=[
            shape((ghosts + EXTRA, chans), bf16),
            shape((8, atoms), f32),
            shape((atoms, chans), f32),
            shape((2, atoms, ghosts), bf16),
        ],
        in_specs=smem + smem + vmem(5),
        out_specs=vmem(4),
        scratch_shapes=[pltpu.VMEM((high, 2 * atoms), f32), pltpu.VMEM((atoms, atoms), bf16)],
        compiler_params=small,
        cost_estimate=pl.CostEstimate(flops=2_000_000_000, bytes_accessed=6_000_000, transcendentals=0),
        name="late",
    )(order, odd, dg, nbt, self_grad, table, mix_weight)
    back_a = swapped(ghost_a, "dom", 0)
    forces, feature_grad = pl.pallas_call(
        final_kernel,
        out_shape=[shape((3, atoms), f32), shape((atoms, chans), f32)],
        in_specs=vmem(6),
        out_specs=vmem(2),
        compiler_params=small,
        name="finish",
    )(grad_own, dpos, back_a, back_b, picks, mix_weight)
    return (energies.reshape(atoms), forces, feature_grad)


def solution(mesh):
    placed = (
        P(None, ("groups", "dom")),
        P(("groups", "dom"), None),
        P(("groups", "dom")),
        P(("groups", "dom"), None),
        P(("groups", "dom")),
        P(("groups", "dom")),
        P(("groups", "dom")),
        P(),
        P(),
        P(),
        P(),
        P(),
        P(),
    )
    return jax.shard_map(
        per_device,
        mesh=mesh,
        in_specs=placed,
        out_specs=(P(("groups", "dom")), P(None, ("groups", "dom")), P(("groups", "dom"), None)),
        check_vma=False,
    )
```

```python
import functools

import jax
import jax.numpy as jnp
from jax import lax
from jax.experimental import pallas as pl
from jax.experimental.pallas import tpu as pltpu
from jax.sharding import PartitionSpec as P

cut_radius = 5.0
sqrt_three = 1.7320508075688772
pi = 3.141592653589793

f32 = jnp.float32
bf16 = jnp.bfloat16

BLOCK = 32
DEPTH = 8
EXTRA = 16
PACK_LIMIT = 63 * 1024 * 1024
LAG = 4
LAG_B = 3
UNROLL_G = 8
UNROLL_H = 8
UNROLL_F = 8
UNROLL_B = 8
UNROLL_E = 8
UNROLL_D = 8
UNROLL_S = 8


def swapped(value, axis, odd):
    count = lax.axis_size(axis)
    partner = [((i + odd) ^ 1) - odd for i in range(count)]
    pairs = [(i, j) for i, j in enumerate(partner) if 0 <= j < count]
    return lax.ppermute(value, axis, pairs)


def iota(shape, dim):
    return lax.broadcasted_iota(jnp.int32, shape, dim)


def dot(a, b, ca=1, cb=0):
    return lax.dot_general(a, b, (((ca,), (cb,)), ((), ())), preferred_element_type=f32)


def parts(value, count):
    out = []
    for _ in range(count):
        head = value.astype(bf16).astype(f32)
        out.append(head)
        value = value - head
    return out


def stack_rows(rows, height):
    lanes = rows[0].shape[1]
    at = iota((height, lanes), 0)
    out = jnp.zeros((height, lanes), f32)
    for idx, row in enumerate(rows):
        out = jnp.where(at == idx, jnp.broadcast_to(row, (height, lanes)), out)
    return out


def sigmoid(x):
    return 1.0 / (1.0 + jnp.exp(-x))


POS, COUNT, SPECIES, READ, LEFT, RIGHT, GAIN = 0, 3, 4, 5, 6, 7, 8


def list_rows(small_ref, odd, ghosts):
    left, right = small_ref[LEFT : LEFT + 1, :ghosts], small_ref[RIGHT : RIGHT + 1, :ghosts]
    return jnp.where(odd, left, right), jnp.where(odd, right, left)


def gain_weight(small_ref):
    return small_ref[GAIN:, :] * small_ref[READ : READ + 1, :]


def pack_kernel(
    odd_ref,
    pos_hbm,
    cnt_hbm,
    spec_hbm,
    read_hbm,
    sl_hbm,
    sr_hbm,
    gain_hbm,
    feat_hbm,
    mix_hbm,
    a_ref,
    b_ref,
    small_ref,
    pos,
    cnt,
    spec,
    read,
    sl,
    sr,
    gain,
    feat,
    mix,
    sems,
):
    hbm = (feat_hbm, mix_hbm, pos_hbm, sl_hbm, sr_hbm, cnt_hbm, spec_hbm, read_hbm, gain_hbm)
    here = (feat, mix, pos, sl, sr, cnt, spec, read, gain)
    copies = [pltpu.make_async_copy(src, dst, sems.at[k]) for k, (src, dst) in enumerate(zip(hbm, here))]
    for copy in copies:
        copy.start()
    for copy in copies[:5]:
        copy.wait()
    small_ref[POS : POS + 3, :] = pos[...]
    for at, lst in ((LEFT, sl), (RIGHT, sr)):
        small_ref[at : at + 1, :] = jnp.full((1, small_ref.shape[1]), -1.0, f32)
        small_ref[at : at + 1, : lst.shape[1]] = lst[...].astype(f32)
    atoms, chans = feat.shape
    ghosts = a_ref.shape[0] - EXTRA
    mixed = dot(feat[...], mix[...]).astype(bf16)
    rows = [p[d : d + 1, :] for p in parts(small_ref[POS : POS + 3, :], 3) for d in range(3)]
    rows = stack_rows(rows, EXTRA).astype(bf16)
    for lst, out in zip(list_rows(small_ref, odd_ref[0] == 1, ghosts), (a_ref, b_ref)):
        pick = (iota((atoms, ghosts), 0).astype(f32) == lst).astype(f32).astype(bf16)
        out[:ghosts, :] = dot(pick, mixed, 0, 0).astype(bf16)
        out[ghosts:, :ghosts] = dot(rows, pick).astype(bf16)
        out[ghosts:, ghosts:] = jnp.zeros((EXTRA, chans - ghosts), bf16)
    for copy in copies[5:]:
        copy.wait()
    small_ref[COUNT : COUNT + 1, :] = cnt[...].astype(f32)
    small_ref[SPECIES : SPECIES + 1, :] = spec[...].astype(f32)
    small_ref[READ : READ + 1, :] = read[...]
    small_ref[GAIN:, :] = gain[...]


def sort_kernel(
    ghosts,
    odd_ref,
    depth_ref,
    pos_ref,
    cnt_ref,
    spec_ref,
    read_ref,
    gain_ref,
    nb_ref,
    feat,
    mix,
    nbt_ref,
    self_ref,
    rank_ref,
    own_ref,
    edir_ref,
    list_ref,
):
    slots, atoms = nb_ref.shape
    chans = feat.shape[1]
    list_tiles(depth_ref, list_ref, atoms // BLOCK, slots // DEPTH)
    cnt_row = cnt_ref[...].astype(f32)
    up, across = iota((atoms, atoms), 0), iota((atoms, atoms), 1)
    cnt_col = jnp.sum(jnp.where(up == across, cnt_row, 0.0), axis=1, keepdims=True)
    ahead_row = (cnt_col > cnt_row) | ((cnt_col == cnt_row) & (up < across))
    ahead_col = (cnt_row > cnt_col) | ((cnt_row == cnt_col) & (across < up))
    rank_row = jnp.sum(ahead_row.astype(f32), axis=0, keepdims=True)
    rank_col = jnp.sum(ahead_col.astype(f32), axis=1, keepdims=True)
    rank_ref[...] = rank_row
    nb = nb_ref[...]
    odd = odd_ref[0]
    to_left = jnp.where(odd == 1, 0, atoms)
    to_right = jnp.where(odd == 1, atoms - ghosts, -ghosts)
    nb = jnp.where(nb >= atoms + ghosts, nb + to_right, jnp.where(nb >= atoms, nb + to_left, nb))
    nbt = nb.astype(f32)
    high = jnp.floor(nbt * (1.0 / 256.0))
    low = nbt - high * 256.0
    rows = [p[d : d + 1, :] for p in parts(pos_ref[...], 3) for d in range(3)]
    left = jnp.concatenate([high, low, stack_rows(rows + [cnt_row], EXTRA)], axis=0).astype(bf16)
    lane_atom = (across % BLOCK).astype(f32)
    lane_slot = iota((slots, atoms), 1) // BLOCK
    mine = lane_slot == (iota((slots, atoms), 0) % DEPTH)
    depth_at = iota((slots // DEPTH, atoms), 0) * DEPTH + iota((slots // DEPTH, atoms), 1) // BLOCK
    groups = slots // DEPTH
    for b in range(atoms // BLOCK):
        pick = (rank_col - float(b * BLOCK) == lane_atom).astype(f32).astype(bf16)
        got = dot(left, pick)
        ids = got[:slots] * 256.0 + got[slots : 2 * slots]
        tail = got[2 * slots :]
        ids = jnp.sum(jnp.where(mine, ids, 0.0).reshape(groups, DEPTH, atoms), axis=1)
        ids = jnp.where(depth_at.astype(f32) < tail[9:10], ids, -1.0)
        nbt_ref[b * groups : (b + 1) * groups, :] = ids
        self_ref[b] = tail[0:8] + tail[3:11] + tail[6:14]
    own_ref[:chans, :] = dot(mix[...], feat[...], 0, 1).astype(bf16)
    own_ref[chans:, :] = stack_rows(rows, EXTRA).astype(bf16)
    weight = gain_ref[...] * read_ref[...]
    kinds = weight.shape[0]
    direct = jnp.zeros((kinds, atoms), f32)
    for p in parts(weight, 3):
        direct += dot(p.astype(bf16), feat[...], 1, 1)
    mine = iota((kinds, atoms), 0).astype(f32) == spec_ref[...].astype(f32)
    edir_ref[...] = jnp.sum(jnp.where(mine, direct, 0.0), axis=0, keepdims=True)


def list_tiles(depth_ref, list_ref, blocks, groups):
    def list_group(j, live):
        need = (depth_ref[j] + (BLOCK - 1)) // BLOCK

        def put(b, state):
            front, back = state
            is_live = b < need
            list_ref[jnp.where(is_live, front, back)] = b * groups + j
            step = is_live.astype(jnp.int32)
            return front + step, back - (1 - step)

        return lax.fori_loop(0, blocks, put, live)

    state = (jnp.int32(0), jnp.int32(blocks * groups - 1))
    live, _ = lax.fori_loop(0, groups, list_group, state)
    list_ref[blocks * groups] = live


def tile_loop(list_ref):
    live = list_ref[list_ref.shape[0] - 1]

    def over_tiles(body, unroll):
        def step(i, carry):
            body([list_ref[i * unroll + u] for u in range(unroll)])
            return carry

        lax.fori_loop(0, (live + (unroll - 1)) // unroll, step, 0)

    return over_tiles


def each(body):
    def bodies(tiles):
        for t in tiles:
            body(t)

    return bodies


def selection(ids, up, sections):
    one, zero = jnp.ones((), bf16), jnp.zeros((), bf16)
    pieces = []
    for s in sections:
        row = jnp.broadcast_to((ids - float(s * up.shape[0])).astype(bf16), up.shape)
        pieces.append(jnp.where(row == up, one, zero))
    return jnp.concatenate(pieces, axis=0)


def fill_section(table, low, rec_ref, chans, atoms):
    ghosts = rec_ref.shape[0] - EXTRA
    table[:chans, low : low + ghosts] = jnp.transpose(rec_ref[:ghosts, :].astype(f32)).astype(bf16)
    table[chans:, low : low + ghosts] = rec_ref[ghosts:, :ghosts]
    table[:, low + ghosts : low + atoms] = jnp.zeros((chans + EXTRA, atoms - ghosts), bf16)


def early_kernel(list_ref, own_ref, arec_ref, nbt_ref, g_ref, near_ref, table, rank_up):
    high, atoms = own_ref.shape
    chans = high - EXTRA
    tiles = nbt_ref.shape[0]
    blocks = atoms // BLOCK
    over_tiles = tile_loop(list_ref)
    rank_up[...] = iota((atoms, atoms), 0).astype(f32).astype(bf16)
    table[:, :atoms] = own_ref[...]
    fill_section(table, atoms, arec_ref, chans, atoms)

    def gather(t):
        got = dot(table[...], selection(nbt_ref[pl.ds(t, 1), :], rank_up[...], (0, 1)))
        g_ref[t] = got[:chans].astype(bf16)
        tail = got[chans:]
        near = tail[0:8] + tail[3:11] + tail[6:14]
        for d in range(3):
            near_ref[d, pl.ds(t, 1), :] = near[d : d + 1]

    over_tiles(each(gather), UNROLL_G)


def main_kernel(
    list_ref,
    gpart_ref,
    near_ref,
    brec_ref,
    nbt_ref,
    self_ref,
    rank_ref,
    edir_ref,
    rin_ref,
    rout_ref,
    pw_ref,
    small_ref,
    en_ref,
    dgbuf,
    spos_ref,
    gb_ref,
    table,
    drbuf,
    gbuf,
    rbuf,
    ybuf,
    abuf,
    dabuf,
    zbuf,
    dfold,
    acc,
    dvec,
    harm,
    radc,
    sinb,
    cosb,
    dsil,
    hidb,
    dharm,
    dbas,
    wout_t,
    rank_up,
):
    tiles, chans, atoms = gpart_ref.shape
    high = chans + EXTRA
    blocks = atoms // BLOCK
    groups = tiles // blocks
    hid_n = rout_ref.shape[0]
    nbasis = rin_ref.shape[0]
    scale = 1.0 / (groups * DEPTH)

    over_tiles = tile_loop(list_ref)

    ghosts = brec_ref.shape[0] - EXTRA
    fill_section(table, 0, brec_ref, chans, atoms)
    rank_up[...] = iota((atoms, atoms), 0).astype(f32).astype(bf16)
    wout_t[...] = jnp.transpose(rout_ref[...].astype(f32)).astype(bf16)
    dvec[...] = jnp.zeros(dvec.shape, f32)
    dharm[...] = jnp.zeros(dharm.shape, f32)
    dbas[...] = jnp.zeros(dbas.shape, f32)
    abuf[...] = jnp.zeros(abuf.shape, f32)
    zbuf[...] = jnp.zeros(zbuf.shape, f32)
    acc[...] = jnp.zeros(acc.shape, f32)
    def gather(t):
        got = dot(table[...], selection(nbt_ref[pl.ds(t, 1), :], rank_up[...], (2,)))
        gbuf[t] = gpart_ref[t] + got[:chans].astype(bf16)
        tail = got[chans:]
        near = tail[0:8] + tail[3:11] + tail[6:14]
        away = near - self_ref[t // groups]
        for d in range(3):
            dvec[d, pl.ds(t, 1), :] = near_ref[d, pl.ds(t, 1), :] + away[d : d + 1]

    over_tiles(each(gather), UNROLL_G)

    dx, dy, dz = dvec[0], dvec[1], dvec[2]
    r2 = dx * dx + dy * dy + dz * dz
    dist = jnp.sqrt(r2 + 0.25)
    inv = 1.0 / dist
    env = jnp.maximum(1.0 - r2 * (1.0 / (cut_radius * cut_radius)), 0.0)
    env2 = env * env
    ux, uy, uz = dx * inv, dy * inv, dz * inv
    radc[0] = dist * (0.5 / cut_radius)
    radc[1] = env2 * inv
    harm[0] = ux
    harm[1] = uy
    harm[2] = uz
    harm[3] = sqrt_three * ux * uy
    harm[4] = sqrt_three * uy * uz
    harm[5] = 0.5 * (3.0 * uz * uz - (ux * ux + uy * uy + uz * uz))
    harm[6] = sqrt_three * ux * uz
    harm[7] = 0.5 * sqrt_three * (ux * ux - uy * uy)

    lanes = atoms
    same = iota((BLOCK, lanes), 0) == (iota((BLOCK, lanes), 1) % BLOCK)
    seg = jnp.where(same, 1.0, 0.0).astype(bf16)
    rin_hi, rin_lo = parts(rin_ref[...], 2)
    rin_t = jnp.concatenate([rin_hi, rin_lo, rin_hi, jnp.zeros_like(rin_hi)], axis=0).astype(bf16)
    rin_b = jnp.concatenate([rin_hi, rin_lo], axis=0).astype(bf16)
    order = (iota((nbasis, lanes), 0) + 1).astype(f32)

    def hidden(t):
        turn = order * radc[0, pl.ds(t, 1), :]
        half = pi * (turn - jnp.floor(turn + 0.5))
        sq = half * half
        s = half * (
            1.0
            + sq
            * (
                -1.0 / 6
                + sq * (1.0 / 120 + sq * (-1.0 / 5040 + sq * (1.0 / 362880 + sq * (-1.0 / 39916800))))
            )
        )
        c = 1.0 + sq * (
            -0.5
            + sq
            * (
                1.0 / 24
                + sq * (-1.0 / 720 + sq * (1.0 / 40320 + sq * (-1.0 / 3628800 + sq * (1.0 / 479001600))))
            )
        )
        sn, cs = 2.0 * s * c, 1.0 - 2.0 * s * s
        sinb[t] = sn
        cosb[t] = cs * order
        basis = sn * radc[1, pl.ds(t, 1), :]
        b_hi, b_lo = parts(basis, 2)
        b_all = jnp.concatenate([b_hi, b_hi, b_lo, jnp.zeros_like(b_hi)], axis=0).astype(bf16)
        pre = dot(rin_t, b_all, 0, 0)
        sig = sigmoid(pre)
        dsil[t] = sig * (1.0 + pre * (1.0 - sig))
        hidb[t] = (pre * sig).astype(bf16)
        for m in range(8):
            row = jnp.broadcast_to(harm[m, pl.ds(t, 1), :].astype(bf16), (BLOCK, lanes))
            ybuf[t, m * BLOCK : (m + 1) * BLOCK, :] = seg * row

    ends = (0, 3, 8)
    seg_half = seg[:, : lanes // 2]

    def radial_part(t, l):
        value = dot(wout_t[l * chans : (l + 1) * chans, :], hidb[t]).astype(bf16)
        rbuf[t, l * chans : (l + 1) * chans, :] = value
        return value * gbuf[t]

    def alpha_part(t, l, term):
        b = t // groups
        if l == 0:
            zbuf[b] += dot(seg_half, term[:, : lanes // 2] + term[:, lanes // 2 :], 1, 1)
        else:
            lo, hi = ends[l - 1] * BLOCK, ends[l] * BLOCK
            abuf[b, lo:hi, :] += dot(ybuf[t, lo:hi, :], term, 1, 1)

    def forward(tiles):
        waiting = []
        for t in tiles:
            for l in range(3):
                waiting.append((t, l, radial_part(t, l)))
                if len(waiting) > LAG:
                    alpha_part(*waiting.pop(0))
        for item in waiting:
            alpha_part(*item)

    over_tiles(each(hidden), UNROLL_H)
    over_tiles(forward, UNROLL_F)

    def alpha(lm):
        return abuf[:, (lm - 1) * BLOCK : lm * BLOCK, :].reshape(atoms, chans) * scale

    seg_half = seg[:, : lanes // 2]
    inv_l = [zbuf[...].reshape(atoms, chans) * scale]
    for ms in (range(1, 4), range(4, 9)):
        total = None
        for lm in ms:
            a = alpha(lm)
            total = a * a if total is None else total + a * a
        inv_l.append(total)
    p = None
    for l in range(3):
        term = dot(inv_l[l].astype(bf16), pw_ref[l * chans : (l + 1) * chans, :])
        p = term if p is None else p + term
    sig = sigmoid(p)
    read = small_ref[READ : READ + 1, :]
    e_col = jnp.sum(p * sig * read, axis=1, keepdims=True)
    place = rank_ref[...] == iota((atoms, atoms), 0).astype(f32)
    en_ref[...] = (
        jnp.sum(jnp.where(place, jnp.broadcast_to(e_col, (atoms, atoms)), 0.0), axis=0, keepdims=True)
        + edir_ref[...]
    )
    dp = (read * sig * (1.0 + p * (1.0 - sig))).astype(bf16)
    for l, ms in enumerate((range(1), range(1, 4), range(4, 9))):
        dinv = dot(dp, pw_ref[l * chans : (l + 1) * chans, :], 1, 1) * scale
        if l == 0:
            dinv = dinv.astype(bf16)
            for b in range(blocks):
                dfold[b] = dot(dinv[b * BLOCK : (b + 1) * BLOCK, :], seg_half, 0, 0).astype(bf16)
        for lm in ms if l else ():
            da = 2.0 * alpha(lm) * dinv
            dabuf[:, (lm - 1) * BLOCK : lm * BLOCK, :] = da.reshape(blocks, BLOCK, chans).astype(bf16)

    def term_part(t, l):
        b = t // groups
        g = gbuf[t]
        radial = rbuf[t, l * chans : (l + 1) * chans, :]
        if l == 0:
            half = dfold[b]
            dterm = jnp.concatenate([half, half], axis=1)
        else:
            lo, hi = ends[l - 1] * BLOCK, ends[l] * BLOCK
            da = dabuf[b, lo:hi, :]
            dterm = dot(da, ybuf[t, lo:hi, :], 0, 0).astype(bf16)
            cross = dot(da, radial * g)
            for m in range(2 * l + 1):
                mine = jnp.where(same, cross[m * BLOCK : (m + 1) * BLOCK, :], 0.0)
                dharm[ends[l - 1] + m, pl.ds(t, 1), :] = jnp.sum(mine, axis=0, keepdims=True)
        return dterm * g, dterm * radial

    def backward(tiles):
        waiting, grads, enters = [], {}, {}

        def enter_part(t, l, term):
            part = dot(rout_ref[:, l * chans : (l + 1) * chans], term)
            total = enters.pop(t, None)
            total = part if total is None else total + part
            if l == 2:
                hidb[tiles[t]] = (total * dsil[tiles[t]]).astype(bf16)
            else:
                enters[t] = total

        for u, t in enumerate(tiles):
            for l in range(3):
                term, part = term_part(t, l)
                grads[u] = part if l == 0 else grads[u] + part
                if l == 2:
                    dgbuf[t, :chans, :] = grads.pop(u)
                waiting.append((u, l, term))
                if len(waiting) > LAG_B:
                    enter_part(*waiting.pop(0))
        for item in waiting:
            enter_part(*item)

    def dhidden(t):
        both = dot(rin_b, hidb[t])
        dbasis = both[:nbasis] + both[nbasis:]
        dbas[0, pl.ds(t, 1), :] = jnp.sum(dbasis * sinb[t], axis=0, keepdims=True)
        dbas[1, pl.ds(t, 1), :] = jnp.sum(dbasis * cosb[t], axis=0, keepdims=True)

    over_tiles(backward, UNROLL_B)
    over_tiles(each(dhidden), UNROLL_D)

    dx, dy, dz = dvec[0], dvec[1], dvec[2]
    r2 = dx * dx + dy * dy + dz * dz
    inv = 1.0 / jnp.sqrt(r2 + 0.25)
    env = jnp.maximum(1.0 - r2 * (1.0 / (cut_radius * cut_radius)), 0.0)
    env2 = env * env
    ux, uy, uz = harm[0], harm[1], harm[2]
    gx = dharm[0] + sqrt_three * (uy * dharm[3] + uz * dharm[6] + ux * dharm[7]) - ux * dharm[5]
    gy = dharm[1] + sqrt_three * (ux * dharm[3] + uz * dharm[4] - uy * dharm[7]) - uy * dharm[5]
    gz = dharm[2] + sqrt_three * (uy * dharm[4] + ux * dharm[6]) + 2.0 * uz * dharm[5]
    dinv = dbas[0] * env2 + gx * dx + gy * dy + gz * dz
    ddist = radc[1] * (pi / cut_radius) * dbas[1] - inv * inv * dinv
    dr2 = 0.5 * inv * ddist - dbas[0] * inv * env * (2.0 / (cut_radius * cut_radius))
    slope = []
    for d, (grad, delta) in enumerate(((gx, dx), (gy, dy), (gz, dz))):
        value = grad * inv + 2.0 * delta * dr2
        slope.append(value)
        dvec[d] = value

    self_rows = []
    lane_block = iota((blocks, lanes), 1) // BLOCK
    for value in slope:
        folded = jnp.sum(value.reshape(blocks, groups, lanes), axis=1)
        by = lanes // 2
        while by >= BLOCK:
            folded = folded + pltpu.roll(folded, by, 1)
            by //= 2
        self_rows.append(
            jnp.sum(jnp.where(lane_block == iota((blocks, lanes), 0), folded, 0.0), axis=0, keepdims=True)
        )
    split = [parts(row, 3) for row in self_rows]
    rows = [split[d][k] for k in range(3) for d in range(3)]
    place = jnp.where(rank_ref[...] == iota((atoms, atoms), 0).astype(f32), 1.0, 0.0).astype(bf16)
    back = dot(stack_rows(rows, EXTRA).astype(bf16), place)
    spos_ref[...] = back[0:8] + back[3:11] + back[6:14]

    def scatter(t):
        rows = []
        for d in range(3):
            rows.append(parts(dvec[d, pl.ds(t, 1), :], 2))
        rows = [rows[d][k] for k in range(2) for d in range(3)]
        dgbuf[t, chans:, :] = stack_rows(rows, EXTRA).astype(bf16)
        acc[...] += dot(dgbuf[t], selection(nbt_ref[pl.ds(t, 1), :], rank_up[...], (2,)), 1, 1)

    over_tiles(each(scatter), UNROLL_S)

    pack_adjoint(acc, 0, gb_ref, chans, atoms)


def pack_adjoint(acc, low, out, chans, atoms):
    ghosts = out.shape[0] - EXTRA
    out[:ghosts, :] = jnp.transpose(acc[:chans, low : low + ghosts]).astype(bf16)
    tail = acc[chans:, low : low + atoms]
    pieces = parts(tail[0:8] + tail[3:11], 2)
    rows = [q[d : d + 1] for q in pieces for d in range(3)]
    out[ghosts:, :] = stack_rows(rows, EXTRA).astype(bf16)


def late_kernel(
    list_ref, odd_ref, dg_ref, nbt_ref, spos_ref, small_ref, mix_ref, ga_ref, dpos_ref, grad_ref, pick_ref, acc, rank_up
):
    _, high, atoms = dg_ref.shape
    chans = high - EXTRA
    ghosts = pick_ref.shape[2]
    rank_up[...] = iota(rank_up.shape, 0).astype(f32).astype(bf16)
    acc[...] = jnp.zeros(acc.shape, f32)

    def scatter(t):
        chosen = selection(nbt_ref[pl.ds(t, 1), :], rank_up[...], (0, 1))
        acc[...] += dot(dg_ref[t], chosen, 1, 1)

    over_tiles = tile_loop(list_ref)
    over_tiles(each(scatter), UNROLL_S)
    pack_adjoint(acc, atoms, ga_ref, chans, atoms)
    tail = acc[chans:, :atoms]
    dpos_ref[...] = tail[0:8] + tail[3:11] - spos_ref[...]
    for k, lst in enumerate(list_rows(small_ref, odd_ref[0] == 1, ghosts)):
        pick_ref[k] = (iota((atoms, ghosts), 0).astype(f32) == lst).astype(f32).astype(bf16)
    weight = gain_weight(small_ref)
    kinds = weight.shape[0]
    chosen = (iota((kinds, atoms), 0).astype(f32) == small_ref[SPECIES : SPECIES + 1, :]).astype(f32)
    grad = None
    for q in parts(weight, 3):
        part = dot(chosen.astype(bf16), q.astype(bf16), 0, 0)
        grad = part if grad is None else grad + part
    for q in parts(acc[:chans, :atoms], 2):
        grad += dot(q.astype(bf16), mix_ref[...], 0, 1)
    grad_ref[...] = grad


def final_kernel(own_ref, dpos_ref, a_ref, b_ref, pick_ref, mix_ref, force_ref, grad_ref):
    ghosts = pick_ref.shape[2]
    total, tail = None, None
    for k, rec in enumerate((a_ref, b_ref)):
        pick = pick_ref[k]
        part, last = dot(rec[:ghosts, :], pick, 0, 1), dot(rec[ghosts:, :ghosts], pick, 1, 1)
        total = part if total is None else total + part
        tail = last if tail is None else tail + last
    pos = dpos_ref[...] + tail[0:8] + tail[3:11]
    force_ref[...] = -pos[:3]
    grad = own_ref[...]
    grad += dot(total.astype(bf16), mix_ref[...], 0, 1)
    grad_ref[...] = grad


def vmem(count):
    return [pl.BlockSpec(memory_space=pltpu.VMEM)] * count


def per_device(
    positions,
    features,
    species,
    neighbours,
    near_count,
    send_left,
    send_right,
    radial_in,
    radial_out,
    mix_weight,
    product_weight,
    species_gain,
    readout,
):
    atoms, chans = features.shape
    ghosts = send_left.shape[0]
    slots = neighbours.shape[1]
    nbasis, hid_n = radial_in.shape
    blocks, groups = atoms // BLOCK, slots // DEPTH
    tiles = blocks * groups
    high = chans + EXTRA
    rows = [row.reshape(1, atoms) for row in (near_count, species, readout)]
    lists = [row.reshape(1, ghosts) for row in (send_left, send_right)]
    inputs = [positions] + rows + lists + [species_gain, features, mix_weight]
    shape = jax.ShapeDtypeStruct
    params = pltpu.CompilerParams(vmem_limit_bytes=44 * 1024 * 1024)
    small = pltpu.CompilerParams(vmem_limit_bytes=16 * 1024 * 1024)

    odd = (lax.axis_index("dom") % 2).astype(jnp.int32).reshape(1)
    smem = [pl.BlockSpec(memory_space=pltpu.SMEM)]
    to_a, to_b, table = pl.pallas_call(
        pack_kernel,
        out_shape=[shape((ghosts + EXTRA, chans), bf16)] * 2
        + [shape((GAIN + species_gain.shape[0], atoms), f32)],
        in_specs=smem + [pl.BlockSpec(memory_space=pltpu.HBM)] * 9,
        out_specs=vmem(3),
        scratch_shapes=[pltpu.VMEM(x.shape, x.dtype) for x in inputs] + [pltpu.SemaphoreType.DMA((9,))],
        compiler_params=pltpu.CompilerParams(vmem_limit_bytes=PACK_LIMIT),
        cost_estimate=pl.CostEstimate(flops=2_000_000_000, bytes_accessed=6_000_000, transcendentals=0),
        name="pack",
    )(odd, *inputs)
    from_a = swapped(to_a, "dom", 0)
    from_b = swapped(to_b, "dom", 1)

    depth = jnp.sum(
        (near_count[None, :] > DEPTH * jnp.arange(groups)[:, None]).astype(jnp.int32), axis=1
    ).astype(jnp.int32)
    nbt, self_pos, rank, own, edir, order = pl.pallas_call(
        functools.partial(sort_kernel, ghosts),
        out_shape=[
            shape((tiles, atoms), f32),
            shape((blocks, 8, atoms), f32),
            shape((1, atoms), f32),
            shape((high, atoms), bf16),
            shape((1, atoms), f32),
            shape((tiles + 1,), jnp.int32),
        ],
        in_specs=smem + smem + vmem(8),
        out_specs=vmem(5) + smem,
        compiler_params=small,
        cost_estimate=pl.CostEstimate(flops=200_000_000, bytes_accessed=2_000_000, transcendentals=0),
        name="sort",
    )(odd, depth, positions, rows[0], rows[1], rows[2], species_gain, neighbours.T, features, mix_weight)
    scratch = [
        pltpu.VMEM((high, atoms), bf16),
        pltpu.VMEM((tiles, 3 * chans, atoms), bf16),
        pltpu.VMEM((tiles, chans, atoms), bf16),
        pltpu.VMEM((tiles, 3 * chans, atoms), bf16),
        pltpu.VMEM((tiles, 8 * BLOCK, atoms), bf16),
        pltpu.VMEM((blocks, 8 * BLOCK, chans), f32),
        pltpu.VMEM((blocks, 8 * BLOCK, chans), bf16),
        pltpu.VMEM((blocks, BLOCK, chans), f32),
        pltpu.VMEM((blocks, chans, atoms // 2), bf16),
        pltpu.VMEM((high, atoms), f32),
        pltpu.VMEM((3, tiles, atoms), f32),
        pltpu.VMEM((8, tiles, atoms), f32),
        pltpu.VMEM((2, tiles, atoms), f32),
        pltpu.VMEM((tiles, nbasis, atoms), f32),
        pltpu.VMEM((tiles, nbasis, atoms), f32),
        pltpu.VMEM((tiles, hid_n, atoms), f32),
        pltpu.VMEM((tiles, hid_n, atoms), bf16),
        pltpu.VMEM((8, tiles, atoms), f32),
        pltpu.VMEM((2, tiles, atoms), f32),
        pltpu.VMEM((3 * chans, hid_n), bf16),
        pltpu.VMEM((atoms, atoms), bf16),
    ]
    picked, near = pl.pallas_call(
        early_kernel,
        out_shape=[shape((tiles, chans, atoms), bf16), shape((3, tiles, atoms), f32)],
        in_specs=smem + vmem(3),
        out_specs=vmem(2),
        scratch_shapes=[
            pltpu.VMEM((high, 2 * atoms), bf16),
            pltpu.VMEM((atoms, atoms), bf16),
        ],
        compiler_params=small,
        cost_estimate=pl.CostEstimate(flops=2_000_000_000, bytes_accessed=6_000_000, transcendentals=0),
        name="early",
    )(order, own, from_a, nbt)
    energies, dg, self_grad, ghost_b = pl.pallas_call(
        main_kernel,
        out_shape=[
            shape((1, atoms), f32),
            shape((tiles, high, atoms), bf16),
            shape((8, atoms), f32),
            shape((ghosts + EXTRA, chans), bf16),
        ],
        in_specs=smem + vmem(11),
        out_specs=vmem(4),
        scratch_shapes=scratch,
        compiler_params=params,
        name="interact",
    )(
        order,
        picked,
        near,
        from_b,
        nbt,
        self_pos,
        rank,
        edir,
        radial_in,
        radial_out,
        product_weight,
        table,
    )
    back_b = swapped(ghost_b, "dom", 1)
    ghost_a, dpos, grad_own, picks = pl.pallas_call(
        late_kernel,
        out_shape=[
            shape((ghosts + EXTRA, chans), bf16),
            shape((8, atoms), f32),
            shape((atoms, chans), f32),
            shape((2, atoms, ghosts), bf16),
        ],
        in_specs=smem + smem + vmem(5),
        out_specs=vmem(4),
        scratch_shapes=[pltpu.VMEM((high, 2 * atoms), f32), pltpu.VMEM((atoms, atoms), bf16)],
        compiler_params=small,
        cost_estimate=pl.CostEstimate(flops=2_000_000_000, bytes_accessed=6_000_000, transcendentals=0),
        name="late",
    )(order, odd, dg, nbt, self_grad, table, mix_weight)
    back_a = swapped(ghost_a, "dom", 0)
    forces, feature_grad = pl.pallas_call(
        final_kernel,
        out_shape=[shape((3, atoms), f32), shape((atoms, chans), f32)],
        in_specs=vmem(6),
        out_specs=vmem(2),
        compiler_params=small,
        name="finish",
    )(grad_own, dpos, back_a, back_b, picks, mix_weight)
    return (energies.reshape(atoms), forces, feature_grad)


def solution(mesh):
    placed = (
        P(None, ("groups", "dom")),
        P(("groups", "dom"), None),
        P(("groups", "dom")),
        P(("groups", "dom"), None),
        P(("groups", "dom")),
        P(("groups", "dom")),
        P(("groups", "dom")),
        P(),
        P(),
        P(),
        P(),
        P(),
        P(),
    )
    return jax.shard_map(
        per_device,
        mesh=mesh,
        in_specs=placed,
        out_specs=(P(("groups", "dom")), P(None, ("groups", "dom")), P(("groups", "dom"), None)),
        check_vma=False,
    )
```

```python
import functools

import jax
import jax.numpy as jnp
from jax import lax
from jax.experimental import pallas as pl
from jax.experimental.pallas import tpu as pltpu
from jax.sharding import PartitionSpec as P

cut_radius = 5.0
sqrt_three = 1.7320508075688772
pi = 3.141592653589793

f32 = jnp.float32
bf16 = jnp.bfloat16

BLOCK = 32
DEPTH = 8
EXTRA = 16
PACK_LIMIT = 63 * 1024 * 1024
LAG = 4
LAG_B = 3
UNROLL_G = 8
UNROLL_H = 8
UNROLL_F = 8
UNROLL_B = 8
UNROLL_E = 8
UNROLL_D = 8
UNROLL_S = 8


def swapped(value, axis, odd):
    count = lax.axis_size(axis)
    partner = [((i + odd) ^ 1) - odd for i in range(count)]
    pairs = [(i, j) for i, j in enumerate(partner) if 0 <= j < count]
    return lax.ppermute(value, axis, pairs)


def iota(shape, dim):
    return lax.broadcasted_iota(jnp.int32, shape, dim)


def dot(a, b, ca=1, cb=0):
    return lax.dot_general(a, b, (((ca,), (cb,)), ((), ())), preferred_element_type=f32)


def parts(value, count):
    out = []
    for _ in range(count):
        head = value.astype(bf16).astype(f32)
        out.append(head)
        value = value - head
    return out


def stack_rows(rows, height):
    lanes = rows[0].shape[1]
    at = iota((height, lanes), 0)
    out = jnp.zeros((height, lanes), f32)
    for idx, row in enumerate(rows):
        out = jnp.where(at == idx, jnp.broadcast_to(row, (height, lanes)), out)
    return out


def sigmoid(x):
    return 1.0 / (1.0 + jnp.exp(-x))


POS, COUNT, SPECIES, READ, LEFT, RIGHT, GAIN = 0, 3, 4, 5, 6, 7, 8


def list_rows(small_ref, odd, ghosts):
    left, right = small_ref[LEFT : LEFT + 1, :ghosts], small_ref[RIGHT : RIGHT + 1, :ghosts]
    return jnp.where(odd, left, right), jnp.where(odd, right, left)


def gain_weight(small_ref):
    return small_ref[GAIN:, :] * small_ref[READ : READ + 1, :]


def pack_kernel(
    odd_ref,
    pos_hbm,
    cnt_hbm,
    spec_hbm,
    read_hbm,
    sl_hbm,
    sr_hbm,
    gain_hbm,
    feat_hbm,
    mix_hbm,
    a_ref,
    b_ref,
    small_ref,
    pos,
    cnt,
    spec,
    read,
    sl,
    sr,
    gain,
    feat,
    mix,
    sems,
):
    hbm = (feat_hbm, mix_hbm, pos_hbm, sl_hbm, sr_hbm, cnt_hbm, spec_hbm, read_hbm, gain_hbm)
    here = (feat, mix, pos, sl, sr, cnt, spec, read, gain)
    copies = [pltpu.make_async_copy(src, dst, sems.at[k]) for k, (src, dst) in enumerate(zip(hbm, here))]
    for copy in copies:
        copy.start()
    for copy in copies[:5]:
        copy.wait()
    small_ref[POS : POS + 3, :] = pos[...]
    for at, lst in ((LEFT, sl), (RIGHT, sr)):
        small_ref[at : at + 1, :] = jnp.full((1, small_ref.shape[1]), -1.0, f32)
        small_ref[at : at + 1, : lst.shape[1]] = lst[...].astype(f32)
    atoms, chans = feat.shape
    ghosts = a_ref.shape[0] - EXTRA
    mixed = dot(feat[...], mix[...]).astype(bf16)
    rows = [p[d : d + 1, :] for p in parts(small_ref[POS : POS + 3, :], 3) for d in range(3)]
    rows = stack_rows(rows, EXTRA).astype(bf16)
    for lst, out in zip(list_rows(small_ref, odd_ref[0] == 1, ghosts), (a_ref, b_ref)):
        pick = (iota((atoms, ghosts), 0).astype(f32) == lst).astype(f32).astype(bf16)
        out[:ghosts, :] = dot(pick, mixed, 0, 0).astype(bf16)
        out[ghosts:, :ghosts] = dot(rows, pick).astype(bf16)
        out[ghosts:, ghosts:] = jnp.zeros((EXTRA, chans - ghosts), bf16)
    for copy in copies[5:]:
        copy.wait()
    small_ref[COUNT : COUNT + 1, :] = cnt[...].astype(f32)
    small_ref[SPECIES : SPECIES + 1, :] = spec[...].astype(f32)
    small_ref[READ : READ + 1, :] = read[...]
    small_ref[GAIN:, :] = gain[...]


def sort_kernel(
    ghosts,
    odd_ref,
    depth_ref,
    pos_ref,
    cnt_ref,
    spec_ref,
    read_ref,
    gain_ref,
    nb_ref,
    feat,
    mix,
    nbt_ref,
    self_ref,
    rank_ref,
    own_ref,
    edir_ref,
    list_ref,
):
    slots, atoms = nb_ref.shape
    chans = feat.shape[1]
    list_tiles(depth_ref, list_ref, atoms // BLOCK, slots // DEPTH)
    cnt_row = cnt_ref[...].astype(f32)
    up, across = iota((atoms, atoms), 0), iota((atoms, atoms), 1)
    cnt_col = jnp.sum(jnp.where(up == across, cnt_row, 0.0), axis=1, keepdims=True)
    ahead_row = (cnt_col > cnt_row) | ((cnt_col == cnt_row) & (up < across))
    ahead_col = (cnt_row > cnt_col) | ((cnt_row == cnt_col) & (across < up))
    rank_row = jnp.sum(ahead_row.astype(f32), axis=0, keepdims=True)
    rank_col = jnp.sum(ahead_col.astype(f32), axis=1, keepdims=True)
    rank_ref[...] = rank_row
    nb = nb_ref[...]
    odd = odd_ref[0]
    to_left = jnp.where(odd == 1, 0, atoms)
    to_right = jnp.where(odd == 1, atoms - ghosts, -ghosts)
    nb = jnp.where(nb >= atoms + ghosts, nb + to_right, jnp.where(nb >= atoms, nb + to_left, nb))
    nbt = nb.astype(f32)
    high = jnp.floor(nbt * (1.0 / 256.0))
    low = nbt - high * 256.0
    rows = [p[d : d + 1, :] for p in parts(pos_ref[...], 3) for d in range(3)]
    left = jnp.concatenate([high, low, stack_rows(rows + [cnt_row], EXTRA)], axis=0).astype(bf16)
    lane_atom = (across % BLOCK).astype(f32)
    lane_slot = iota((slots, atoms), 1) // BLOCK
    mine = lane_slot == (iota((slots, atoms), 0) % DEPTH)
    depth_at = iota((slots // DEPTH, atoms), 0) * DEPTH + iota((slots // DEPTH, atoms), 1) // BLOCK
    groups = slots // DEPTH
    for b in range(atoms // BLOCK):
        pick = (rank_col - float(b * BLOCK) == lane_atom).astype(f32).astype(bf16)
        got = dot(left, pick)
        ids = got[:slots] * 256.0 + got[slots : 2 * slots]
        tail = got[2 * slots :]
        ids = jnp.sum(jnp.where(mine, ids, 0.0).reshape(groups, DEPTH, atoms), axis=1)
        ids = jnp.where(depth_at.astype(f32) < tail[9:10], ids, -1.0)
        nbt_ref[b * groups : (b + 1) * groups, :] = ids
        self_ref[b] = tail[0:8] + tail[3:11] + tail[6:14]
    own_ref[:chans, :] = dot(mix[...], feat[...], 0, 1).astype(bf16)
    own_ref[chans:, :] = stack_rows(rows, EXTRA).astype(bf16)
    weight = gain_ref[...] * read_ref[...]
    kinds = weight.shape[0]
    direct = jnp.zeros((kinds, atoms), f32)
    for p in parts(weight, 3):
        direct += dot(p.astype(bf16), feat[...], 1, 1)
    mine = iota((kinds, atoms), 0).astype(f32) == spec_ref[...].astype(f32)
    edir_ref[...] = jnp.sum(jnp.where(mine, direct, 0.0), axis=0, keepdims=True)


def list_tiles(depth_ref, list_ref, blocks, groups):
    def list_group(j, live):
        need = (depth_ref[j] + (BLOCK - 1)) // BLOCK

        def put(b, state):
            front, back = state
            is_live = b < need
            list_ref[jnp.where(is_live, front, back)] = b * groups + j
            step = is_live.astype(jnp.int32)
            return front + step, back - (1 - step)

        return lax.fori_loop(0, blocks, put, live)

    state = (jnp.int32(0), jnp.int32(blocks * groups - 1))
    live, _ = lax.fori_loop(0, groups, list_group, state)
    list_ref[blocks * groups] = live


def tile_loop(list_ref):
    live = list_ref[list_ref.shape[0] - 1]

    def over_tiles(body, unroll):
        def step(i, carry):
            body([list_ref[i * unroll + u] for u in range(unroll)])
            return carry

        lax.fori_loop(0, (live + (unroll - 1)) // unroll, step, 0)

    return over_tiles


def each(body):
    def bodies(tiles):
        for t in tiles:
            body(t)

    return bodies


def selection(ids, up, sections):
    one, zero = jnp.ones((), bf16), jnp.zeros((), bf16)
    pieces = []
    for s in sections:
        row = jnp.broadcast_to((ids - float(s * up.shape[0])).astype(bf16), up.shape)
        pieces.append(jnp.where(row == up, one, zero))
    return jnp.concatenate(pieces, axis=0)


def fill_section(table, low, rec_ref, chans, atoms):
    ghosts = rec_ref.shape[0] - EXTRA
    table[:chans, low : low + ghosts] = jnp.transpose(rec_ref[:ghosts, :].astype(f32)).astype(bf16)
    table[chans:, low : low + ghosts] = rec_ref[ghosts:, :ghosts]
    table[:, low + ghosts : low + atoms] = jnp.zeros((chans + EXTRA, atoms - ghosts), bf16)


def early_kernel(list_ref, own_ref, arec_ref, nbt_ref, g_ref, near_ref, table, rank_up):
    high, atoms = own_ref.shape
    chans = high - EXTRA
    tiles = nbt_ref.shape[0]
    blocks = atoms // BLOCK
    over_tiles = tile_loop(list_ref)
    rank_up[...] = iota((atoms, atoms), 0).astype(f32).astype(bf16)
    table[:, :atoms] = own_ref[...]
    fill_section(table, atoms, arec_ref, chans, atoms)

    def gather(t):
        got = dot(table[...], selection(nbt_ref[pl.ds(t, 1), :], rank_up[...], (0, 1)))
        g_ref[t] = got[:chans].astype(bf16)
        tail = got[chans:]
        near = tail[0:8] + tail[3:11] + tail[6:14]
        for d in range(3):
            near_ref[d, pl.ds(t, 1), :] = near[d : d + 1]

    over_tiles(each(gather), UNROLL_G)


def main_kernel(
    list_ref,
    gpart_ref,
    near_ref,
    brec_ref,
    nbt_ref,
    self_ref,
    rank_ref,
    edir_ref,
    rin_ref,
    rout_ref,
    pw_ref,
    small_ref,
    en_ref,
    dgbuf,
    spos_ref,
    gb_ref,
    table,
    drbuf,
    gbuf,
    rbuf,
    ybuf,
    abuf,
    dabuf,
    zbuf,
    dfold,
    acc,
    dvec,
    harm,
    radc,
    sinb,
    cosb,
    dsil,
    hidb,
    dharm,
    dbas,
    wout_t,
    rank_up,
):
    tiles, chans, atoms = gpart_ref.shape
    high = chans + EXTRA
    blocks = atoms // BLOCK
    groups = tiles // blocks
    hid_n = rout_ref.shape[0]
    nbasis = rin_ref.shape[0]
    scale = 1.0 / (groups * DEPTH)

    over_tiles = tile_loop(list_ref)

    ghosts = brec_ref.shape[0] - EXTRA
    fill_section(table, 0, brec_ref, chans, atoms)
    rank_up[...] = iota((atoms, atoms), 0).astype(f32).astype(bf16)
    wout_t[...] = jnp.transpose(rout_ref[...].astype(f32)).astype(bf16)
    dvec[...] = jnp.zeros(dvec.shape, f32)
    dharm[...] = jnp.zeros(dharm.shape, f32)
    dbas[...] = jnp.zeros(dbas.shape, f32)
    abuf[...] = jnp.zeros(abuf.shape, f32)
    zbuf[...] = jnp.zeros(zbuf.shape, f32)
    acc[...] = jnp.zeros(acc.shape, f32)
    def gather(t):
        got = dot(table[...], selection(nbt_ref[pl.ds(t, 1), :], rank_up[...], (2,)))
        gbuf[t] = gpart_ref[t] + got[:chans].astype(bf16)
        tail = got[chans:]
        near = tail[0:8] + tail[3:11] + tail[6:14]
        away = near - self_ref[t // groups]
        for d in range(3):
            dvec[d, pl.ds(t, 1), :] = near_ref[d, pl.ds(t, 1), :] + away[d : d + 1]

    over_tiles(each(gather), UNROLL_G)

    dx, dy, dz = dvec[0], dvec[1], dvec[2]
    r2 = dx * dx + dy * dy + dz * dz
    dist = jnp.sqrt(r2 + 0.25)
    inv = 1.0 / dist
    env = jnp.maximum(1.0 - r2 * (1.0 / (cut_radius * cut_radius)), 0.0)
    env2 = env * env
    ux, uy, uz = dx * inv, dy * inv, dz * inv
    radc[0] = dist * (0.5 / cut_radius)
    radc[1] = env2 * inv
    harm[0] = ux
    harm[1] = uy
    harm[2] = uz
    harm[3] = sqrt_three * ux * uy
    harm[4] = sqrt_three * uy * uz
    harm[5] = 0.5 * (3.0 * uz * uz - (ux * ux + uy * uy + uz * uz))
    harm[6] = sqrt_three * ux * uz
    harm[7] = 0.5 * sqrt_three * (ux * ux - uy * uy)

    lanes = atoms
    same = iota((BLOCK, lanes), 0) == (iota((BLOCK, lanes), 1) % BLOCK)
    seg = jnp.where(same, 1.0, 0.0).astype(bf16)
    rin_hi, rin_lo = parts(rin_ref[...], 2)
    rin_t = jnp.concatenate([rin_hi, rin_lo, rin_hi, jnp.zeros_like(rin_hi)], axis=0).astype(bf16)
    rin_b = jnp.concatenate([rin_hi, rin_lo], axis=0).astype(bf16)
    order = (iota((nbasis, lanes), 0) + 1).astype(f32)

    def hidden(t):
        turn = order * radc[0, pl.ds(t, 1), :]
        half = pi * (turn - jnp.floor(turn + 0.5))
        sq = half * half
        s = half * (
            1.0
            + sq
            * (
                -1.0 / 6
                + sq * (1.0 / 120 + sq * (-1.0 / 5040 + sq * (1.0 / 362880 + sq * (-1.0 / 39916800))))
            )
        )
        c = 1.0 + sq * (
            -0.5
            + sq
            * (
                1.0 / 24
                + sq * (-1.0 / 720 + sq * (1.0 / 40320 + sq * (-1.0 / 3628800 + sq * (1.0 / 479001600))))
            )
        )
        sn, cs = 2.0 * s * c, 1.0 - 2.0 * s * s
        sinb[t] = sn
        cosb[t] = cs * order
        basis = sn * radc[1, pl.ds(t, 1), :]
        b_hi, b_lo = parts(basis, 2)
        b_all = jnp.concatenate([b_hi, b_hi, b_lo, jnp.zeros_like(b_hi)], axis=0).astype(bf16)
        pre = dot(rin_t, b_all, 0, 0)
        sig = sigmoid(pre)
        dsil[t] = sig * (1.0 + pre * (1.0 - sig))
        hidb[t] = (pre * sig).astype(bf16)
        for m in range(8):
            row = jnp.broadcast_to(harm[m, pl.ds(t, 1), :].astype(bf16), (BLOCK, lanes))
            ybuf[t, m * BLOCK : (m + 1) * BLOCK, :] = seg * row

    ends = (0, 3, 8)
    seg_half = seg[:, : lanes // 2]

    def radial_part(t, l):
        value = dot(wout_t[l * chans : (l + 1) * chans, :], hidb[t]).astype(bf16)
        rbuf[t, l * chans : (l + 1) * chans, :] = value
        return value * gbuf[t]

    def alpha_part(t, l, term):
        b = t // groups
        if l == 0:
            zbuf[b] += dot(seg_half, term[:, : lanes // 2] + term[:, lanes // 2 :], 1, 1)
        else:
            lo, hi = ends[l - 1] * BLOCK, ends[l] * BLOCK
            abuf[b, lo:hi, :] += dot(ybuf[t, lo:hi, :], term, 1, 1)

    def forward(tiles):
        waiting = []
        for t in tiles:
            for l in range(3):
                waiting.append((t, l, radial_part(t, l)))
                if len(waiting) > LAG:
                    alpha_part(*waiting.pop(0))
        for item in waiting:
            alpha_part(*item)

    over_tiles(each(hidden), UNROLL_H)
    over_tiles(forward, UNROLL_F)

    def alpha(lm):
        return abuf[:, (lm - 1) * BLOCK : lm * BLOCK, :].reshape(atoms, chans) * scale

    seg_half = seg[:, : lanes // 2]
    inv_l = [zbuf[...].reshape(atoms, chans) * scale]
    for ms in (range(1, 4), range(4, 9)):
        total = None
        for lm in ms:
            a = alpha(lm)
            total = a * a if total is None else total + a * a
        inv_l.append(total)
    p = None
    for l in range(3):
        term = dot(inv_l[l].astype(bf16), pw_ref[l * chans : (l + 1) * chans, :])
        p = term if p is None else p + term
    sig = sigmoid(p)
    read = small_ref[READ : READ + 1, :]
    e_col = jnp.sum(p * sig * read, axis=1, keepdims=True)
    place = rank_ref[...] == iota((atoms, atoms), 0).astype(f32)
    en_ref[...] = (
        jnp.sum(jnp.where(place, jnp.broadcast_to(e_col, (atoms, atoms)), 0.0), axis=0, keepdims=True)
        + edir_ref[...]
    )
    dp = (read * sig * (1.0 + p * (1.0 - sig))).astype(bf16)
    for l, ms in enumerate((range(1), range(1, 4), range(4, 9))):
        dinv = dot(dp, pw_ref[l * chans : (l + 1) * chans, :], 1, 1) * scale
        if l == 0:
            dinv = dinv.astype(bf16)
            for b in range(blocks):
                dfold[b] = dot(dinv[b * BLOCK : (b + 1) * BLOCK, :], seg_half, 0, 0).astype(bf16)
        for lm in ms if l else ():
            da = 2.0 * alpha(lm) * dinv
            dabuf[:, (lm - 1) * BLOCK : lm * BLOCK, :] = da.reshape(blocks, BLOCK, chans).astype(bf16)

    def term_part(t, l):
        b = t // groups
        g = gbuf[t]
        radial = rbuf[t, l * chans : (l + 1) * chans, :]
        if l == 0:
            half = dfold[b]
            dterm = jnp.concatenate([half, half], axis=1)
        else:
            lo, hi = ends[l - 1] * BLOCK, ends[l] * BLOCK
            da = dabuf[b, lo:hi, :]
            dterm = dot(da, ybuf[t, lo:hi, :], 0, 0).astype(bf16)
            cross = dot(da, radial * g)
            for m in range(2 * l + 1):
                mine = jnp.where(same, cross[m * BLOCK : (m + 1) * BLOCK, :], 0.0)
                dharm[ends[l - 1] + m, pl.ds(t, 1), :] = jnp.sum(mine, axis=0, keepdims=True)
        return dterm * g, dterm * radial

    def backward(tiles):
        waiting, grads, enters = [], {}, {}

        def enter_part(t, l, term):
            part = dot(rout_ref[:, l * chans : (l + 1) * chans], term)
            total = enters.pop(t, None)
            total = part if total is None else total + part
            if l == 2:
                hidb[tiles[t]] = (total * dsil[tiles[t]]).astype(bf16)
            else:
                enters[t] = total

        for u, t in enumerate(tiles):
            for l in range(3):
                term, part = term_part(t, l)
                grads[u] = part if l == 0 else grads[u] + part
                if l == 2:
                    dgbuf[t, :chans, :] = grads.pop(u)
                waiting.append((u, l, term))
                if len(waiting) > LAG_B:
                    enter_part(*waiting.pop(0))
        for item in waiting:
            enter_part(*item)

    def dhidden(t):
        both = dot(rin_b, hidb[t])
        dbasis = both[:nbasis] + both[nbasis:]
        dbas[0, pl.ds(t, 1), :] = jnp.sum(dbasis * sinb[t], axis=0, keepdims=True)
        dbas[1, pl.ds(t, 1), :] = jnp.sum(dbasis * cosb[t], axis=0, keepdims=True)

    over_tiles(backward, UNROLL_B)
    over_tiles(each(dhidden), UNROLL_D)

    dx, dy, dz = dvec[0], dvec[1], dvec[2]
    r2 = dx * dx + dy * dy + dz * dz
    inv = 1.0 / jnp.sqrt(r2 + 0.25)
    env = jnp.maximum(1.0 - r2 * (1.0 / (cut_radius * cut_radius)), 0.0)
    env2 = env * env
    ux, uy, uz = harm[0], harm[1], harm[2]
    gx = dharm[0] + sqrt_three * (uy * dharm[3] + uz * dharm[6] + ux * dharm[7]) - ux * dharm[5]
    gy = dharm[1] + sqrt_three * (ux * dharm[3] + uz * dharm[4] - uy * dharm[7]) - uy * dharm[5]
    gz = dharm[2] + sqrt_three * (uy * dharm[4] + ux * dharm[6]) + 2.0 * uz * dharm[5]
    dinv = dbas[0] * env2 + gx * dx + gy * dy + gz * dz
    ddist = radc[1] * (pi / cut_radius) * dbas[1] - inv * inv * dinv
    dr2 = 0.5 * inv * ddist - dbas[0] * inv * env * (2.0 / (cut_radius * cut_radius))
    slope = []
    for d, (grad, delta) in enumerate(((gx, dx), (gy, dy), (gz, dz))):
        value = grad * inv + 2.0 * delta * dr2
        slope.append(value)
        dvec[d] = value

    self_rows = []
    lane_block = iota((blocks, lanes), 1) // BLOCK
    for value in slope:
        folded = jnp.sum(value.reshape(blocks, groups, lanes), axis=1)
        by = lanes // 2
        while by >= BLOCK:
            folded = folded + pltpu.roll(folded, by, 1)
            by //= 2
        self_rows.append(
            jnp.sum(jnp.where(lane_block == iota((blocks, lanes), 0), folded, 0.0), axis=0, keepdims=True)
        )
    split = [parts(row, 3) for row in self_rows]
    rows = [split[d][k] for k in range(3) for d in range(3)]
    place = jnp.where(rank_ref[...] == iota((atoms, atoms), 0).astype(f32), 1.0, 0.0).astype(bf16)
    back = dot(stack_rows(rows, EXTRA).astype(bf16), place)
    spos_ref[...] = back[0:8] + back[3:11] + back[6:14]

    def scatter(t):
        rows = []
        for d in range(3):
            rows.append(parts(dvec[d, pl.ds(t, 1), :], 2))
        rows = [rows[d][k] for k in range(2) for d in range(3)]
        dgbuf[t, chans:, :] = stack_rows(rows, EXTRA).astype(bf16)
        acc[...] += dot(dgbuf[t], selection(nbt_ref[pl.ds(t, 1), :], rank_up[...], (2,)), 1, 1)

    over_tiles(each(scatter), UNROLL_S)

    pack_adjoint(acc, 0, gb_ref, chans, atoms)


def pack_adjoint(acc, low, out, chans, atoms):
    ghosts = out.shape[0] - EXTRA
    out[:ghosts, :] = jnp.transpose(acc[:chans, low : low + ghosts]).astype(bf16)
    tail = acc[chans:, low : low + atoms]
    pieces = parts(tail[0:8] + tail[3:11], 2)
    rows = [q[d : d + 1] for q in pieces for d in range(3)]
    out[ghosts:, :] = stack_rows(rows, EXTRA).astype(bf16)


def late_kernel(
    list_ref, odd_ref, dg_ref, nbt_ref, spos_ref, small_ref, mix_ref, ga_ref, dpos_ref, grad_ref, pick_ref, acc, rank_up
):
    _, high, atoms = dg_ref.shape
    chans = high - EXTRA
    ghosts = pick_ref.shape[2]
    rank_up[...] = iota(rank_up.shape, 0).astype(f32).astype(bf16)
    acc[...] = jnp.zeros(acc.shape, f32)

    def scatter(t):
        chosen = selection(nbt_ref[pl.ds(t, 1), :], rank_up[...], (0, 1))
        acc[...] += dot(dg_ref[t], chosen, 1, 1)

    over_tiles = tile_loop(list_ref)
    over_tiles(each(scatter), UNROLL_S)
    pack_adjoint(acc, atoms, ga_ref, chans, atoms)
    tail = acc[chans:, :atoms]
    dpos_ref[...] = tail[0:8] + tail[3:11] - spos_ref[...]
    for k, lst in enumerate(list_rows(small_ref, odd_ref[0] == 1, ghosts)):
        pick_ref[k] = (iota((atoms, ghosts), 0).astype(f32) == lst).astype(f32).astype(bf16)
    weight = gain_weight(small_ref)
    kinds = weight.shape[0]
    chosen = (iota((kinds, atoms), 0).astype(f32) == small_ref[SPECIES : SPECIES + 1, :]).astype(f32)
    grad = None
    for q in parts(weight, 3):
        part = dot(chosen.astype(bf16), q.astype(bf16), 0, 0)
        grad = part if grad is None else grad + part
    grad += dot(acc[:chans, :atoms].astype(bf16), mix_ref[...], 0, 1)
    grad_ref[...] = grad


def final_kernel(own_ref, dpos_ref, a_ref, b_ref, pick_ref, mix_ref, force_ref, grad_ref):
    ghosts = pick_ref.shape[2]
    total, tail = None, None
    for k, rec in enumerate((a_ref, b_ref)):
        pick = pick_ref[k]
        part, last = dot(rec[:ghosts, :], pick, 0, 1), dot(rec[ghosts:, :ghosts], pick, 1, 1)
        total = part if total is None else total + part
        tail = last if tail is None else tail + last
    pos = dpos_ref[...] + tail[0:8] + tail[3:11]
    force_ref[...] = -pos[:3]
    grad = own_ref[...]
    grad += dot(total.astype(bf16), mix_ref[...], 0, 1)
    grad_ref[...] = grad


def vmem(count):
    return [pl.BlockSpec(memory_space=pltpu.VMEM)] * count


def per_device(
    positions,
    features,
    species,
    neighbours,
    near_count,
    send_left,
    send_right,
    radial_in,
    radial_out,
    mix_weight,
    product_weight,
    species_gain,
    readout,
):
    atoms, chans = features.shape
    ghosts = send_left.shape[0]
    slots = neighbours.shape[1]
    nbasis, hid_n = radial_in.shape
    blocks, groups = atoms // BLOCK, slots // DEPTH
    tiles = blocks * groups
    high = chans + EXTRA
    rows = [row.reshape(1, atoms) for row in (near_count, species, readout)]
    lists = [row.reshape(1, ghosts) for row in (send_left, send_right)]
    inputs = [positions] + rows + lists + [species_gain, features, mix_weight]
    shape = jax.ShapeDtypeStruct
    params = pltpu.CompilerParams(vmem_limit_bytes=44 * 1024 * 1024)
    small = pltpu.CompilerParams(vmem_limit_bytes=16 * 1024 * 1024)

    odd = (lax.axis_index("dom") % 2).astype(jnp.int32).reshape(1)
    smem = [pl.BlockSpec(memory_space=pltpu.SMEM)]
    to_a, to_b, table = pl.pallas_call(
        pack_kernel,
        out_shape=[shape((ghosts + EXTRA, chans), bf16)] * 2
        + [shape((GAIN + species_gain.shape[0], atoms), f32)],
        in_specs=smem + [pl.BlockSpec(memory_space=pltpu.HBM)] * 9,
        out_specs=vmem(3),
        scratch_shapes=[pltpu.VMEM(x.shape, x.dtype) for x in inputs] + [pltpu.SemaphoreType.DMA((9,))],
        compiler_params=pltpu.CompilerParams(vmem_limit_bytes=PACK_LIMIT),
        cost_estimate=pl.CostEstimate(flops=2_000_000_000, bytes_accessed=6_000_000, transcendentals=0),
        name="pack",
    )(odd, *inputs)
    from_a = swapped(to_a, "dom", 0)
    from_b = swapped(to_b, "dom", 1)

    depth = jnp.sum(
        (near_count[None, :] > DEPTH * jnp.arange(groups)[:, None]).astype(jnp.int32), axis=1
    ).astype(jnp.int32)
    nbt, self_pos, rank, own, edir, order = pl.pallas_call(
        functools.partial(sort_kernel, ghosts),
        out_shape=[
            shape((tiles, atoms), f32),
            shape((blocks, 8, atoms), f32),
            shape((1, atoms), f32),
            shape((high, atoms), bf16),
            shape((1, atoms), f32),
            shape((tiles + 1,), jnp.int32),
        ],
        in_specs=smem + smem + vmem(8),
        out_specs=vmem(5) + smem,
        compiler_params=small,
        cost_estimate=pl.CostEstimate(flops=200_000_000, bytes_accessed=2_000_000, transcendentals=0),
        name="sort",
    )(odd, depth, positions, rows[0], rows[1], rows[2], species_gain, neighbours.T, features, mix_weight)
    scratch = [
        pltpu.VMEM((high, atoms), bf16),
        pltpu.VMEM((tiles, 3 * chans, atoms), bf16),
        pltpu.VMEM((tiles, chans, atoms), bf16),
        pltpu.VMEM((tiles, 3 * chans, atoms), bf16),
        pltpu.VMEM((tiles, 8 * BLOCK, atoms), bf16),
        pltpu.VMEM((blocks, 8 * BLOCK, chans), f32),
        pltpu.VMEM((blocks, 8 * BLOCK, chans), bf16),
        pltpu.VMEM((blocks, BLOCK, chans), f32),
        pltpu.VMEM((blocks, chans, atoms // 2), bf16),
        pltpu.VMEM((high, atoms), f32),
        pltpu.VMEM((3, tiles, atoms), f32),
        pltpu.VMEM((8, tiles, atoms), f32),
        pltpu.VMEM((2, tiles, atoms), f32),
        pltpu.VMEM((tiles, nbasis, atoms), f32),
        pltpu.VMEM((tiles, nbasis, atoms), f32),
        pltpu.VMEM((tiles, hid_n, atoms), f32),
        pltpu.VMEM((tiles, hid_n, atoms), bf16),
        pltpu.VMEM((8, tiles, atoms), f32),
        pltpu.VMEM((2, tiles, atoms), f32),
        pltpu.VMEM((3 * chans, hid_n), bf16),
        pltpu.VMEM((atoms, atoms), bf16),
    ]
    picked, near = pl.pallas_call(
        early_kernel,
        out_shape=[shape((tiles, chans, atoms), bf16), shape((3, tiles, atoms), f32)],
        in_specs=smem + vmem(3),
        out_specs=vmem(2),
        scratch_shapes=[
            pltpu.VMEM((high, 2 * atoms), bf16),
            pltpu.VMEM((atoms, atoms), bf16),
        ],
        compiler_params=small,
        cost_estimate=pl.CostEstimate(flops=2_000_000_000, bytes_accessed=6_000_000, transcendentals=0),
        name="early",
    )(order, own, from_a, nbt)
    energies, dg, self_grad, ghost_b = pl.pallas_call(
        main_kernel,
        out_shape=[
            shape((1, atoms), f32),
            shape((tiles, high, atoms), bf16),
            shape((8, atoms), f32),
            shape((ghosts + EXTRA, chans), bf16),
        ],
        in_specs=smem + vmem(11),
        out_specs=vmem(4),
        scratch_shapes=scratch,
        compiler_params=params,
        name="interact",
    )(
        order,
        picked,
        near,
        from_b,
        nbt,
        self_pos,
        rank,
        edir,
        radial_in,
        radial_out,
        product_weight,
        table,
    )
    back_b = swapped(ghost_b, "dom", 1)
    ghost_a, dpos, grad_own, picks = pl.pallas_call(
        late_kernel,
        out_shape=[
            shape((ghosts + EXTRA, chans), bf16),
            shape((8, atoms), f32),
            shape((atoms, chans), f32),
            shape((2, atoms, ghosts), bf16),
        ],
        in_specs=smem + smem + vmem(5),
        out_specs=vmem(4),
        scratch_shapes=[pltpu.VMEM((high, 2 * atoms), f32), pltpu.VMEM((atoms, atoms), bf16)],
        compiler_params=small,
        cost_estimate=pl.CostEstimate(flops=2_000_000_000, bytes_accessed=6_000_000, transcendentals=0),
        name="late",
    )(order, odd, dg, nbt, self_grad, table, mix_weight)
    back_a = swapped(ghost_a, "dom", 0)
    forces, feature_grad = pl.pallas_call(
        final_kernel,
        out_shape=[shape((3, atoms), f32), shape((atoms, chans), f32)],
        in_specs=vmem(6),
        out_specs=vmem(2),
        compiler_params=small,
        name="finish",
    )(grad_own, dpos, back_a, back_b, picks, mix_weight)
    return (energies.reshape(atoms), forces, feature_grad)


def solution(mesh):
    placed = (
        P(None, ("groups", "dom")),
        P(("groups", "dom"), None),
        P(("groups", "dom")),
        P(("groups", "dom"), None),
        P(("groups", "dom")),
        P(("groups", "dom")),
        P(("groups", "dom")),
        P(),
        P(),
        P(),
        P(),
        P(),
        P(),
    )
    return jax.shard_map(
        per_device,
        mesh=mesh,
        in_specs=placed,
        out_specs=(P(("groups", "dom")), P(None, ("groups", "dom")), P(("groups", "dom"), None)),
        check_vma=False,
    )
```
